32 devices in a mesh: dp: 16 (over z, x, core), narrow: 2 (over y).
Axes of the slice: x: 2, y: 2, z: 4, core: 2. Of those that a mesh axis runs over, the one named last changes fastest.
Arguments:
- tokens: bfloat16 [36864, 1024], P(('dp', 'narrow')), may hold values from -6 to 6
- cotangent: bfloat16 [36864, 1024], P(('dp', 'narrow')), may hold values from -6 to 6
- bucket: int32 [32], P(('dp', 'narrow')), may hold values from 0 to 1
- text_lengths: int32 [32, 3], P(('dp', 'narrow')), may hold values from 1 to 128, as said below
- attn_qkv: float32 [3, 1024, 1024], P(None, 'dp', 'narrow'), may hold values from -0.1875 to 0.1875
- attn_out: float32 [1024, 1024], P('dp', 'narrow'), may hold values from -2 to 2
- ffn_in: float32 [2, 1024, 2816], P(None, 'dp', 'narrow'), may hold values from -0.1875 to 0.1875
- ffn_out: float32 [2816, 1024], P('dp', 'narrow'), may hold values from -0.109375 to 0.109375
- norm_gains: float32 [2, 1024], P(None, ('dp', 'narrow')), may hold values from 0.5 to 1.5
- first_qkv: float32 [3, 1024, 1024], P(None, 'dp', 'narrow'), may hold values from -96 to 96
- first_out: float32 [1024, 1024], P('dp', 'narrow'), may hold values from -8 to 8
- first_ffin: float32 [2, 1024, 2816], P(None, 'dp', 'narrow'), may hold values from -48 to 48
- first_ffout: float32 [2816, 1024], P('dp', 'narrow'), may hold values from -80 to 80
- first_gains: float32 [2, 1024], P(None, ('dp', 'narrow')), may hold values from -128 to 128
- second_qkv: float32 [3, 1024, 1024], P(None, 'dp', 'narrow'), may hold values from 18.432 to 73.728
- second_out: float32 [1024, 1024], P('dp', 'narrow'), may hold values from 0.1856 to 0.736
- second_ffin: float32 [2, 1024, 2816], P(None, 'dp', 'narrow'), may hold values from 4.42368 to 18.432
- second_ffout: float32 [2816, 1024], P('dp', 'narrow'), may hold values from 13.27104 to 51.6096
- second_gains: float32 [2, 1024], P(None, ('dp', 'narrow')), may hold values from 36.864 to 147.456
Outputs:
- mixed: bfloat16 [36864, 1024], P(('dp', 'narrow'))
- input_grad: float32 [36864, 1024], P(('dp', 'narrow'))
- grad_qkv: float32 [3, 1024, 1024], P(None, 'dp', 'narrow')
- new_first_qkv: float32 [3, 1024, 1024], P(None, 'dp', 'narrow')
- new_second_qkv: float32 [3, 1024, 1024], P(None, 'dp', 'narrow')
- new_qkv: float32 [3, 1024, 1024], P(None, 'dp', 'narrow')
- grad_out: float32 [1024, 1024], P('dp', 'narrow')
- new_first_out: float32 [1024, 1024], P('dp', 'narrow')
- new_second_out: float32 [1024, 1024], P('dp', 'narrow')
- new_out: float32 [1024, 1024], P('dp', 'narrow')
- grad_ffin: float32 [2, 1024, 2816], P(None, 'dp', 'narrow')
- new_first_ffin: float32 [2, 1024, 2816], P(None, 'dp', 'narrow')
- new_second_ffin: float32 [2, 1024, 2816], P(None, 'dp', 'narrow')
- new_ffin: float32 [2, 1024, 2816], P(None, 'dp', 'narrow')
- grad_ffout: float32 [2816, 1024], P('dp', 'narrow')
- new_first_ffout: float32 [2816, 1024], P('dp', 'narrow')
- new_second_ffout: float32 [2816, 1024], P('dp', 'narrow')
- new_ffout: float32 [2816, 1024], P('dp', 'narrow')
- grad_gains: float32 [2, 1024], P(None, ('dp', 'narrow'))
- new_first_gains: float32 [2, 1024], P(None, ('dp', 'narrow'))
- new_second_gains: float32 [2, 1024], P(None, ('dp', 'narrow'))
- new_gains: float32 [2, 1024], P(None, ('dp', 'narrow'))
The draws below stay inside these ranges and needn't reach their ends.
Inputs may be any that keep to these rules, and one draw needn't show every extreme that they name: `text_lengths`: text tokens of each example of a pack; the value 128 occurs in every draw.
All inputs are finite; a program needn't handle non-finite values.
Results may differ from the reference program's by a relative error of at most 0.025.
Values may be sent and summed in bfloat16 or wider, within the bound.
No kernel may reach another device: no remote copies, remote signals or barrier semaphores. Data moves between devices by JAX's collectives and lax.ppermute only.
A program may use at most 256 MiB of HBM per device.

```python
import math
import jax
import jax.numpy as jnp
from jax import lax

D = 1024
HEADS = 16
DK = 64
FF = 2816
SHORT_PATCH = 256
TEXT = 128
STEP = 10
HD = 1024
SLOT = 384
LONG = 1152
LONG_PATCH = 1024
PACKS = 32
TOKENS = 36864


def draw_text_lengths(key, part):
    key = jax.random.fold_in(key, 7)
    key_lengths, key_pick = jax.random.split(key)
    lengths = jax.random.randint(key_lengths, (PACKS * 3,), 1, TEXT + 1, dtype=jnp.int32)
    chosen = jax.random.randint(key_pick, (), 0, PACKS * 3, dtype=jnp.int32)
    flat_rows = jnp.where(jnp.arange(PACKS * 3, dtype=jnp.int32) == chosen, TEXT, lengths)
    return flat_rows.astype(jnp.int32).reshape(PACKS, 3)


def set_ends(drawn, own_key, least, largest):
    shape = drawn.shape
    index_at = [jax.random.randint(jax.random.fold_in(own_key, axis), (), 0, shape[axis]) for axis in range(len(shape))]
    drawn = drawn.at[tuple(index_at)].set(least)
    longest = shape.index(max(shape))
    index_at[longest] = (index_at[longest] + 1) % shape[longest]
    return drawn.at[tuple(index_at)].set(largest)


def levels(rng, shape, cuts, smallest, largest):
    level, own = 1.0, jax.random.fold_in(rng, 6)
    for dim, shards_of in cuts:
        draws = jnp.exp(jax.random.uniform(jax.random.fold_in(own, dim), (shards_of,), jnp.float32, smallest / len(cuts), largest / len(cuts)))
        level = level * jnp.repeat(draws, shape[dim] // shards_of).reshape([-1 if axis == dim else 1 for axis in range(len(shape))])
    return level


def bell_draw(key, extent, width, reach, cuts=(), held_as=jnp.bfloat16):
    array = width * jax.random.normal(key, extent, jnp.float32)
    if cuts:
        array = array * levels(key, extent, cuts, -0.22, 0.18)
    return jnp.clip(array, -reach, reach).astype(held_as)


def setup_inputs(seed: int = 0) -> dict:
    key_of = jax.random.split(jax.random.key(seed), 20)
    tokens = bell_draw(key_of[0], (TOKENS, D), 1.0, 6.0, ((0, 32),))
    cotangent = bell_draw(key_of[1], (TOKENS, D), 1.0, 6.0, ((0, 32),))
    bucket = set_ends(jax.random.randint(key_of[2], (PACKS,), 0, 2), jax.random.fold_in(key_of[2], 1), 0, 1).astype(jnp.int32)
    text_lengths = draw_text_lengths(jax.random.fold_in(key_of[19], 71), 0)
    attn_qkv = bell_draw(key_of[4], (3, D, HD), D ** -0.5, 0.1875, ((1, 16), (2, 2)), jnp.float32)
    attn_out = bell_draw(key_of[5], (HD, D), (max(1, D * 8 // LONG)) ** -0.5, 2.0, ((0, 16), (1, 2)), jnp.float32)
    ffn_in = bell_draw(key_of[6], (2, D, FF), D ** -0.5, 0.1875, ((1, 16), (2, 2)), jnp.float32)
    ffn_out = bell_draw(key_of[7], (FF, D), FF ** -0.5, 0.109375, ((0, 16), (1, 2)), jnp.float32)
    norm_gains = jnp.clip(1.0 + 0.1 * jax.random.normal(key_of[8], (2, D), jnp.float32), 0.5, 1.5)
    first_qkv = bell_draw(key_of[9], (3, D, HD), (0.078 * TOKENS ** 0.5), 96.0, ((1, 16), (2, 2)), jnp.float32)
    first_out = bell_draw(key_of[10], (HD, D), (0.27 * PACKS ** 0.5), 8.0, ((0, 16), (1, 2)), jnp.float32)
    first_ffin = bell_draw(key_of[11], (2, D, FF), (0.039 * TOKENS ** 0.5), 48.0, ((1, 16), (2, 2)), jnp.float32)
    first_ffout = bell_draw(key_of[12], (FF, D), (0.067 * TOKENS ** 0.5), 80.0, ((0, 16), (1, 2)), jnp.float32)
    first_gains = bell_draw(key_of[13], (2, D), (0.11 * TOKENS ** 0.5), 128.0, ((1, 32),), jnp.float32)
    second_qkv = jnp.clip(jnp.exp(math.log(73.728) - 1.3862944 * jax.random.uniform(key_of[14], (3, D, HD), jnp.float32) ** levels(key_of[14], (3, D, HD), ((1, 16), (2, 2)), -0.2, 0.2)), 18.432, 73.728)
    second_out = jnp.clip(jnp.exp(math.log(0.736) - 1.3776363 * jax.random.uniform(key_of[15], (HD, D), jnp.float32) ** levels(key_of[15], (HD, D), ((0, 16), (1, 2)), -0.2, 0.2)), 0.1856, 0.736)
    second_ffin = jnp.clip(jnp.exp(math.log(18.432) - 1.4271164 * jax.random.uniform(key_of[16], (2, D, FF), jnp.float32) ** levels(key_of[16], (2, D, FF), ((1, 16), (2, 2)), -0.2, 0.2)), 4.42368, 18.432)
    second_ffout = jnp.clip(jnp.exp(math.log(51.6096) - 1.3581235 * jax.random.uniform(key_of[17], (FF, D), jnp.float32) ** levels(key_of[17], (FF, D), ((0, 16), (1, 2)), -0.2, 0.2)), 13.27104, 51.6096)
    second_gains = jnp.clip(jnp.exp(math.log(147.456) - 1.3862944 * jax.random.uniform(key_of[18], (2, D), jnp.float32) ** levels(key_of[18], (2, D), ((1, 32),), -0.2, 0.2)), 36.864, 147.456)
    return dict(tokens=tokens, cotangent=cotangent, bucket=bucket, text_lengths=text_lengths, attn_qkv=attn_qkv, attn_out=attn_out, ffn_in=ffn_in, ffn_out=ffn_out, norm_gains=norm_gains, first_qkv=first_qkv, first_out=first_out, first_ffin=first_ffin, first_ffout=first_ffout, first_gains=first_gains, second_qkv=second_qkv, second_out=second_out, second_ffin=second_ffin, second_ffout=second_ffout, second_gains=second_gains)


@jax.custom_vjp
def low(v):
    return lax.optimization_barrier(v.astype(jnp.bfloat16)).astype(jnp.float32)

@jax.custom_vjp
def low_back(v):
    return v

def low_keep(v):
    return (low(v), None)

def low_pass(kept, grad):
    return (grad,)

def back_keep(v):
    return (v, None)

def back_low(kept, grad):
    return (low(grad),)
low.defvjp(low_keep, low_pass)
low_back.defvjp(back_keep, back_low)
norm_eps = 1e-06
score_scale = 0.125
masked_score = -1e+30
beta_one = 0.9
beta_two = 0.999
adam_eps = 1e-08
decay_rate = 0.01
rates = (0.08, 0.8, 0.08, 0.05, 0.6)

def gelu_tanh(values):
    return 0.5 * values * (1.0 + jnp.tanh(0.7978845608028654 * (values + 0.044715 * values * values * values)))

def norm_scaled(values, gain_row):
    return values * lax.rsqrt(lax.optimization_barrier(jnp.mean(values * values, axis=-1, keepdims=True)) + norm_eps) * gain_row

def segment_ids(bucket_one, text_one):
    position = jnp.arange(LONG, dtype=jnp.int32)
    slot_index = position // SLOT
    inside = position - slot_index * SLOT
    slot_length = SHORT_PATCH + jnp.where(slot_index == 0, text_one[0], jnp.where(slot_index == 1, text_one[1], text_one[2]))
    long_valid = position < LONG_PATCH + text_one[0]
    short_valid = inside < slot_length
    minus_one = jnp.full((LONG,), -1, dtype=jnp.int32)
    return jnp.where(bucket_one == 1, jnp.where(long_valid, jnp.zeros((LONG,), jnp.int32), minus_one), jnp.where(short_valid, slot_index, minus_one)).astype(jnp.int32)

def matmul(left_side, right_side):
    return jnp.dot(left_side, right_side, precision=lax.Precision.HIGHEST, preferred_element_type=jnp.float32)

def layer(inputs, attn_qkv, attn_out, ffn_in, ffn_out, norm_gains, seg_pack):
    qkv_low = low(attn_qkv)
    out_low = low(attn_out)
    ffin_low = low(ffn_in)
    ffout_low = low(ffn_out)
    gains_low = low(norm_gains)
    normed = low(norm_scaled(inputs, gains_low[0]))
    queries = low(low_back(matmul(normed, qkv_low[0]))).reshape(LONG, HEADS, DK)
    keys_all = low(low_back(matmul(normed, qkv_low[1]))).reshape(LONG, HEADS, DK)
    values_all = low(low_back(matmul(normed, qkv_low[2]))).reshape(LONG, HEADS, DK)
    scores = low_back(jnp.einsum('qhd,khd->hqk', queries, keys_all, precision=lax.Precision.HIGHEST) * score_scale)
    same_doc = seg_pack[:, None] == seg_pack[None, :]
    scores = jnp.where(same_doc[None], scores, masked_score)
    row_top = lax.optimization_barrier(jnp.max(scores, axis=-1, keepdims=True))
    expo = jnp.exp(scores - row_top)
    probs = expo / lax.optimization_barrier(jnp.sum(expo, axis=-1, keepdims=True))
    attended = low(low_back(jnp.einsum('hqk,khd->qhd', low(probs), values_all, precision=lax.Precision.HIGHEST))).reshape(LONG, HD)
    hidden_state = inputs + low_back(matmul(attended, out_low))
    normed_two = low(norm_scaled(hidden_state, gains_low[1]))
    gate = low_back(matmul(normed_two, ffin_low[0]))
    upward = low_back(matmul(normed_two, ffin_low[1]))
    inner = low(gelu_tanh(gate) * upward)
    return hidden_state + low_back(matmul(inner, ffout_low))

def adamw(weight, grad_total, first, second, rate):
    first_new = beta_one * first + (1.0 - beta_one) * grad_total
    second_new = beta_two * second + (1.0 - beta_two) * grad_total * grad_total
    first_hat = first_new / (1.0 - beta_one ** STEP)
    second_hat = second_new / (1.0 - beta_two ** STEP)
    weight_new = weight - rate * (first_hat / (jnp.sqrt(second_hat) + adam_eps) + decay_rate * weight)
    return (grad_total, first_new, second_new, weight_new)

def reference(tokens, cotangent, bucket, text_lengths, attn_qkv, attn_out, ffn_in, ffn_out, norm_gains, first_qkv, first_out, first_ffin, first_ffout, first_gains, second_qkv, second_out, second_ffin, second_ffout, second_gains):
    weights = (attn_qkv, attn_out, ffn_in, ffn_out, norm_gains)
    token_packs = tokens.astype(jnp.float32).reshape(PACKS, LONG, D)
    grad_packs = cotangent.astype(jnp.float32).reshape(PACKS, LONG, D)

    def one_pack(totals, items):
        inputs, grad_rows, bucket_one, text_one = items
        seg_pack = segment_ids(bucket_one, text_one)
        valid = (seg_pack >= 0).astype(jnp.float32)[:, None]

        def forward(inputs_in, qkv_in, out_in, ffin_in, ffout_in, gains_in):
            return layer(inputs_in, qkv_in, out_in, ffin_in, ffout_in, gains_in, seg_pack)
        mixed_pack, pull_back = jax.vjp(forward, inputs, attn_qkv, attn_out, ffn_in, ffn_out, norm_gains)
        grads = pull_back(grad_rows * valid)
        new_totals = tuple((running + piece for running, piece in zip(totals, grads[1:])))
        return (new_totals, (mixed_pack.astype(jnp.bfloat16), grads[0]))
    initial = tuple((jnp.zeros_like(weight) for weight in weights))
    totals, (mixed_packs, input_packs) = lax.scan(one_pack, initial, (token_packs, grad_packs, bucket, text_lengths))
    firsts = (first_qkv, first_out, first_ffin, first_ffout, first_gains)
    seconds = (second_qkv, second_out, second_ffin, second_ffout, second_gains)
    results = [mixed_packs.reshape(TOKENS, D), input_packs.reshape(TOKENS, D)]
    for index_weight in range(5):
        results.extend(adamw(weights[index_weight], totals[index_weight], firsts[index_weight], seconds[index_weight], rates[index_weight]))
    return tuple(results)
```

```python
import functools

import jax
import jax.numpy as jnp
from jax import lax
from jax.experimental import pallas as pl
from jax.experimental.pallas import tpu as pltpu
from jax.sharding import PartitionSpec as P

HEADS = 16
DK = 64
SHORT_PATCH = 256
STEP = 10
HD = 1024
SLOT = 384
LONG = 1152
LONG_PATCH = 1024

norm_eps = 1e-06
score_scale = 0.125
beta_one = 0.9
beta_two = 0.999
adam_eps = 1e-08
decay_rate = 0.01
rates = (0.08, 0.8, 0.08, 0.05, 0.6)

BF = jnp.bfloat16
F32 = jnp.float32
PAIRS = HD // 128
NN = (((1,), (0,)), ((), ()))
NT = (((1,), (1,)), ((), ()))
TN = (((0,), (0,)), ((), ()))
AXES = ("dp", "narrow")
VMEM_BYTES = 60 * 2**20
ROWS_GAIN = 16
FF_BLOCK = 256
QUERY_BLOCK = 384


def dot(left, right, dims=NN):
    return lax.dot_general(left, right, dims, preferred_element_type=F32)


def params():
    return pltpu.CompilerParams(vmem_limit_bytes=VMEM_BYTES)


def shape(dims, dtype):
    return jax.ShapeDtypeStruct(dims, dtype)


IN_VMEM = pl.BlockSpec(memory_space=pltpu.VMEM)
IN_HBM = pl.BlockSpec(memory_space=pl.ANY)
IN_SMEM = pl.BlockSpec(memory_space=pltpu.SMEM)


def exchange_perms():
    steps = []
    for kinds in (("z2", "z1"), ("z1", "z2"), ("x", "y"), ("y", "x"), ("core", "core")):
        perm = []
        for z in range(4):
            for x in range(2):
                for core in range(2):
                    for y in range(2):
                        kind = kinds[core]
                        to = [z, x, core, y]
                        if kind == "z2":
                            to[0] ^= 2
                        elif kind == "z1":
                            to[0] ^= 1
                        elif kind == "x":
                            to[1] ^= 1
                        elif kind == "y":
                            to[3] ^= 1
                        else:
                            to[2] ^= 1
                        perm.append(
                            (
                                ((z * 2 + x) * 2 + core) * 2 + y,
                                ((to[0] * 2 + to[1]) * 2 + to[2]) * 2 + to[3],
                            )
                        )
        steps.append(perm)
    return steps


def place_table(fast):
    if not fast:
        return jnp.zeros((1, 2), jnp.int32)
    dp = lax.axis_index("dp")
    narrow = lax.axis_index("narrow")
    z, x, core = dp // 4, (dp // 2) % 2, dp % 2
    rows = []
    for place in range(32):
        one, two, three, four, five = [(place >> bit) & 1 for bit in range(5)]
        core_of = core ^ five
        first = core_of == 0
        z_of = z ^ jnp.where(first, 2 * one + two, one + 2 * two)
        x_of = x ^ jnp.where(first, three, four)
        y_of = narrow ^ jnp.where(first, four, three)
        rows.append(jnp.stack(((z_of * 2 + x_of) * 2 + core_of, y_of)))
    return jnp.stack(rows).astype(jnp.int32)


def gather(piece, perms):
    held = piece[None]
    for perm in perms[:3]:
        held = jnp.concatenate((held, lax.ppermute(held, AXES, perm)), axis=0)
    more = lax.ppermute(held, AXES, perms[3])
    return (held, more, lax.ppermute(held, AXES, perms[4]), lax.ppermute(more, AXES, perms[4]))


def reduce_to_owner(blocks, perms):
    keep, pass_on, away, away_on = blocks
    other_on = lax.ppermute(away_on, AXES, perms[4])
    other = lax.ppermute(away, AXES, perms[4])
    sent = (pass_on.astype(F32) + other_on.astype(F32)).astype(BF)
    parts = [keep, other, lax.ppermute(sent, AXES, perms[3])]
    for perm, low, high in ((perms[2], 4, 8), (perms[1], 2, 4), (perms[0], 1, 2)):
        sent = sum(part[low:high].astype(F32) for part in parts).astype(BF)
        parts.append(lax.ppermute(sent, AXES, perm))
    return sum(part[0].astype(F32) for part in parts)


def place_of(index):
    return index // 8, index % 8


def each_place(table, sources, fast, body):
    if not fast:
        body(sources[0].at[0], 0, 0)
        return
    for index in range(32):
        array, slot = place_of(index)
        body(sources[array].at[slot], table[index, 0], table[index, 1])


def rows_of(start, size, unit):
    if isinstance(start, int):
        return pl.ds(start * size, size)
    return pl.ds(pl.multiple_of(start * size, unit), size)


def project_kernel(fast, row_piece, col_piece, table, x_ref, *refs):
    n_arrays = 4 if fast else 1
    arrays = refs[:n_arrays]
    out_ref, normed_t_ref, gains_ref, weight, gain_parts, normed, sem, gain_sem = refs[n_arrays:]
    step = pl.program_id(0)

    @pl.when(step == 0)
    def _():
        slots = 8 if fast else 1
        for index in range(n_arrays):
            pltpu.make_async_copy(
                arrays[index].at[:, pl.ds(row_piece, ROWS_GAIN), pl.ds(0, HD)],
                gain_parts.at[pl.ds(index * slots, slots)],
                gain_sem,
            ).start()

        def start(source, dp, narrow):
            pltpu.make_async_copy(
                source.at[pl.ds(0, row_piece)],
                weight.at[rows_of(dp, row_piece, 16), rows_of(narrow, col_piece, 128)],
                sem,
            ).start()

        each_place(table, arrays, fast, start)
        x = x_ref[...].astype(F32)
        scaled = x * lax.rsqrt(jnp.mean(x * x, axis=-1, keepdims=True) + norm_eps)
        pltpu.make_async_copy(gain_parts, gain_parts, gain_sem).wait()
        gains = jnp.sum(gain_parts[...].astype(F32), axis=0)
        gains_ref[...] = gains
        low = (scaled * gains[0:1]).astype(BF)
        normed[...] = low
        normed_t_ref[...] = low.T
        pltpu.make_async_copy(weight, weight, sem).wait()

    column = pl.multiple_of(step * 512, 512)
    out_ref[...] = dot(normed[...], weight[:, pl.ds(column, 512)]).astype(BF)


def project(tokens, arrays, table, fast, row_piece, col_piece):
    rows = tokens.shape[0]
    full = lambda dims: pl.BlockSpec(dims, lambda step: (0,) * len(dims))
    n_places = 32 if fast else 1
    return pl.pallas_call(
        functools.partial(project_kernel, fast, row_piece, col_piece),
        grid=(6,),
        in_specs=[IN_SMEM, full((rows, HD))] + [IN_HBM] * len(arrays),
        out_specs=[
            pl.BlockSpec((rows, 512), lambda step: (0, step)),
            full((HD, rows)),
            full((ROWS_GAIN, HD)),
        ],
        out_shape=[shape((rows, 3 * HD), BF), shape((HD, rows), BF), shape((ROWS_GAIN, HD), F32)],
        scratch_shapes=[
            pltpu.VMEM((HD, 3 * HD), BF),
            pltpu.VMEM((n_places, ROWS_GAIN, HD), BF),
            pltpu.VMEM((rows, HD), BF),
            pltpu.SemaphoreType.DMA(()),
            pltpu.SemaphoreType.DMA(()),
        ],
        compiler_params=params(),
        name="project",
    )(table, tokens, *arrays)


def three_parts(values):
    first = values.astype(BF)
    rest = values - first.astype(F32)
    second = rest.astype(BF)
    return first, second, (rest - second.astype(F32)).astype(BF)


def mask_operands(segments):
    kind = jnp.arange(64, dtype=jnp.int32)
    mine = segments[None, :] + 1 == kind[:, None]
    query_side = jnp.where(mine, -1e30, 0.0).astype(BF)
    key_side = jnp.where((kind[None, :] < 4) & ~mine.T, 1.0, 0.0).astype(BF)
    return (
        jnp.concatenate((query_side, query_side), axis=0),
        jnp.concatenate((key_side, key_side), axis=1),
    )


def attend_forward_kernel(q_ref, k_ref, v_ref, mask_q_ref, mask_k_ref, out_ref, extra_ref):
    queries_t = (q_ref[...].astype(F32) * score_scale).astype(BF).T
    keys = k_ref[...]
    values_t = v_ref[...].T
    mask_q = mask_q_ref[...]
    mask_k = mask_k_ref[...]
    lane = lax.broadcasted_iota(jnp.int32, (1, 128), 1)
    row = lax.broadcasted_iota(jnp.int32, (64, 1), 0)
    ones = jnp.ones((16, LONG), BF)
    outs = []
    extras = []
    for head in range(2):
        half = slice(64 * head, 64 * head + 64)
        if head == 0:
            key_side = jnp.where(lane < 64, keys, mask_k)
            query_side = jnp.concatenate((queries_t[half], mask_q[64:128]), axis=0)
        else:
            key_side = jnp.where(lane >= 64, keys, mask_k)
            query_side = jnp.concatenate((mask_q[0:64], queries_t[half]), axis=0)
        value_side = jnp.concatenate((values_t[half], ones), axis=0)
        out_blocks = []
        log_blocks = []
        for start in range(0, LONG, QUERY_BLOCK):
            scores = dot(key_side, query_side[:, start : start + QUERY_BLOCK])
            top = jnp.max(scores, axis=0, keepdims=True)
            expo = jnp.exp(scores - top).astype(BF)
            both = dot(value_side, expo)
            total = both[64:65]
            out_blocks.append((both[0:64] * (1.0 / total)).astype(BF))
            log_blocks.append(-(top + jnp.log(total)))
        outs.append(jnp.concatenate(out_blocks, axis=1))
        extra = mask_q[0:64].astype(F32)
        for index, part in enumerate(three_parts(jnp.concatenate(log_blocks, axis=1))):
            extra = jnp.where(row == 4 + index, part.astype(F32), extra)
        extras.append(extra.astype(BF))
    out_ref[...] = jnp.concatenate(outs, axis=0).T
    extra_ref[...] = jnp.concatenate((extras[1], extras[0]), axis=0).T


def tile_spec(rows, tiles_of, offset):
    return pl.BlockSpec(
        (rows, 128), lambda i: (0, (i // tiles_of) * 3 * tiles_of + offset * tiles_of + i % tiles_of)
    )


def attend_forward(projected, mask_q, mask_k, tiles_of):
    rows = projected.shape[0]
    tile = pl.BlockSpec((rows, 128), lambda i: (0, i))
    return pl.pallas_call(
        attend_forward_kernel,
        grid=(PAIRS,),
        in_specs=[
            tile_spec(rows, tiles_of, 0),
            tile_spec(rows, tiles_of, 1),
            tile_spec(rows, tiles_of, 2),
            pl.BlockSpec((128, rows), lambda i: (0, 0)),
            pl.BlockSpec((rows, 128), lambda i: (0, 0)),
        ],
        out_specs=[tile, tile],
        out_shape=[shape((rows, HD), BF), shape((rows, HD), BF)],
        compiler_params=params(),
        name="attend_forward",
    )(projected, projected, projected, mask_q, mask_k)


def attend_backward_kernel(
    q_ref, k_ref, v_ref, out_ref, grad_ref, extra_ref, mask_k_ref, grad_q_ref, grad_k_ref, grad_v_ref
):
    queries = (q_ref[...].astype(F32) * score_scale).astype(BF)
    queries_t = queries.T
    keys = k_ref[...]
    keys_t = keys.T
    values_t = v_ref[...].T
    grad = grad_ref[...]
    grad_t = grad.T
    extra = extra_ref[...]
    mask_k_t = mask_k_ref[...].T
    lane = lax.broadcasted_iota(jnp.int32, (1, 128), 1)
    row = lax.broadcasted_iota(jnp.int32, (64, 1), 0)
    product_t = (grad.astype(F32) * out_ref[...].astype(F32)).T
    inner = []
    for head in (1, 0):
        total = -jnp.sum(product_t[64 * head : 64 * head + 64], axis=0, keepdims=True)
        rows = jnp.zeros((64, LONG), F32)
        for index, part in enumerate(three_parts(total)):
            rows = jnp.where(row == index, part.astype(F32), rows)
        inner.append(rows.astype(BF))
    inner_cols = jnp.concatenate(inner, axis=0).T
    key_extra = jnp.where((row >= 4) & (row < 7), 1.0, mask_k_t[0:64].astype(F32)).astype(BF)
    value_extra = jnp.broadcast_to(jnp.where(row < 3, 1.0, 0.0).astype(BF), (64, LONG))
    grad_q = []
    grad_k = []
    grad_v = []
    for head in range(2):
        half = slice(64 * head, 64 * head + 64)
        own = (lane < 64) if head == 0 else (lane >= 64)
        query_side = jnp.where(own, queries, extra)
        grad_side = jnp.where(own, grad, inner_cols)
        if head == 0:
            key_side = jnp.concatenate((keys_t[half], key_extra), axis=0)
            value_side = jnp.concatenate((values_t[half], value_extra), axis=0)
        else:
            key_side = jnp.concatenate((key_extra, keys_t[half]), axis=0)
            value_side = jnp.concatenate((value_extra, values_t[half]), axis=0)
        q_blocks = []
        k_total = None
        v_total = None
        for start in range(0, LONG, QUERY_BLOCK):
            block = slice(start, start + QUERY_BLOCK)
            probs = jnp.exp(dot(query_side[block], key_side))
            grad_scores = (probs * dot(grad_side[block], value_side)).astype(BF)
            v_part = dot(grad_t[half, block], probs.astype(BF))
            k_part = dot(queries_t[half, block], grad_scores)
            v_total = v_part if v_total is None else v_total + v_part
            k_total = k_part if k_total is None else k_total + k_part
            q_blocks.append(dot(grad_scores, keys) * score_scale)
        grad_q.append(jnp.concatenate(q_blocks, axis=0))
        grad_k.append(k_total)
        grad_v.append(v_total)
    grad_q_ref[...] = jnp.where(lane < 64, grad_q[0], grad_q[1]).astype(BF)
    grad_k_ref[...] = jnp.concatenate(grad_k, axis=0).astype(BF).T
    grad_v_ref[...] = jnp.concatenate(grad_v, axis=0).astype(BF).T


def attend_backward(projected, attended, grad_attended, extra, mask_k, tiles_of):
    rows = projected.shape[0]
    tile = pl.BlockSpec((rows, 128), lambda i: (0, i))
    return pl.pallas_call(
        attend_backward_kernel,
        grid=(PAIRS,),
        in_specs=[
            tile_spec(rows, tiles_of, 0),
            tile_spec(rows, tiles_of, 1),
            tile_spec(rows, tiles_of, 2),
            tile,
            tile,
            tile,
            pl.BlockSpec((rows, 128), lambda i: (0, 0)),
        ],
        out_specs=[tile, tile, tile],
        out_shape=[shape((rows, HD), BF)] * 3,
        compiler_params=params(),
        name="attend_backward",
    )(projected, projected, projected, attended, grad_attended, extra, mask_k)


def middle_kernel(fast, sizes, table, x_ref, attended_ref, cotangent_ref, valid_ref, gains_ref, *refs):
    n_arrays = 4 if fast else 1
    row_d, row_f, col_d, col_f = sizes
    square, gates, ups = (refs[i * n_arrays : (i + 1) * n_arrays] for i in range(3))
    refs = refs[3 * n_arrays :]
    mixed_ref, grad_hidden_ref, grad_attended_ref = refs[:3]
    refs = refs[3:]
    grad_square, grad_gates, grad_ups = (refs[i * n_arrays : (i + 1) * n_arrays] for i in range(3))
    refs = refs[3 * n_arrays :]
    gain_grad_ref, w_out, w_gate, w_up, w_down, hidden, normed, normed_t, grad_mixed, grad_normed, sems, out_sem = refs

    def start(source, dp, narrow):
        pltpu.make_async_copy(
            source.at[pl.ds(0, row_d)], w_out.at[rows_of(dp, row_d, 16), rows_of(narrow, col_d, 128)], sems.at[0]
        ).start()

    each_place(table, square, fast, start)

    def start_gate(source, dp, narrow):
        pltpu.make_async_copy(
            source, w_gate.at[rows_of(dp, row_d, 16), rows_of(narrow, col_f, 128)], sems.at[1]
        ).start()

    each_place(table, gates, fast, start_gate)

    def start_up(source, dp, narrow):
        pltpu.make_async_copy(
            source, w_up.at[rows_of(dp, row_d, 16), rows_of(narrow, col_f, 128)], sems.at[2]
        ).start()

    each_place(table, ups, fast, start_up)

    def start_down(source, dp, narrow):
        pltpu.make_async_copy(
            source.at[pl.ds(row_d, row_f)],
            w_down.at[rows_of(dp, row_f, 16), rows_of(narrow, col_d, 128)],
            sems.at[3],
        ).start()

    each_place(table, square, fast, start_down)
    gain = gains_ref[1:2]
    pltpu.make_async_copy(w_out, w_out, sems.at[0]).wait()
    mixed_sum = grad_hidden_ref

    def before(index, carry):
        part = pl.ds(pl.multiple_of(index * QUERY_BLOCK, QUERY_BLOCK), QUERY_BLOCK)
        state = x_ref[part, :].astype(F32) + dot(attended_ref[part, :], w_out[...])
        hidden[part, :] = state
        mixed_sum[part, :] = state
        low = (state * lax.rsqrt(jnp.mean(state * state, axis=-1, keepdims=True) + norm_eps) * gain).astype(BF)
        normed[part, :] = low
        normed_t[:, part] = low.T
        grad_mixed[part, :] = (cotangent_ref[part, :].astype(F32) * valid_ref[part, :]).astype(BF)
        return carry

    lax.fori_loop(0, x_ref.shape[0] // QUERY_BLOCK, before, 0)
    grad_normed[...] = jnp.zeros_like(grad_normed)
    pltpu.make_async_copy(w_gate, w_gate, sems.at[1]).wait()
    pltpu.make_async_copy(w_up, w_up, sems.at[2]).wait()
    pltpu.make_async_copy(w_down, w_down, sems.at[3]).wait()

    def block(index, carry):
        cols = pl.ds(pl.multiple_of(index * FF_BLOCK, FF_BLOCK), FF_BLOCK)
        gate_w = w_gate[:, cols]
        up_w = w_up[:, cols]
        down_w = w_down[cols, :]
        gate = dot(normed[...], gate_w)
        upward = dot(normed[...], up_w)
        grad_inner = dot(grad_mixed[...], down_w, NT)
        square_gate = gate * gate
        curve = jnp.tanh(0.7978845608028654 * gate * (1.0 + 0.044715 * square_gate))
        half = 0.5 * (1.0 + curve)
        active = gate * half
        slope = half + (0.5 * gate) * (1.0 - curve * curve) * (
            0.7978845608028654 + (0.7978845608028654 * 3.0 * 0.044715) * square_gate
        )
        inner = (active * upward).astype(BF)
        grad_gate = (grad_inner * upward * slope).astype(BF)
        grad_up = (grad_inner * active).astype(BF)
        mixed_sum[...] += dot(inner, down_w)
        grad_normed[...] += dot(grad_gate, gate_w, NT) + dot(grad_up, up_w, NT)
        w_down[cols, :] = dot(inner.T, grad_mixed[...]).astype(BF)
        w_gate[:, cols] = dot(normed_t[...], grad_gate).astype(BF)
        w_up[:, cols] = dot(normed_t[...], grad_up).astype(BF)
        return carry

    lax.fori_loop(0, w_gate.shape[1] // FF_BLOCK, block, 0)

    def finish_gate(target, dp, narrow):
        pltpu.make_async_copy(
            w_gate.at[rows_of(dp, row_d, 16), rows_of(narrow, col_f, 128)], target, out_sem.at[0]
        ).start()

    def finish_up(target, dp, narrow):
        pltpu.make_async_copy(
            w_up.at[rows_of(dp, row_d, 16), rows_of(narrow, col_f, 128)], target, out_sem.at[1]
        ).start()

    def finish_down(target, dp, narrow):
        pltpu.make_async_copy(
            w_down.at[rows_of(dp, row_f, 16), rows_of(narrow, col_d, 128)],
            target.at[pl.ds(row_d, row_f)],
            out_sem.at[2],
        ).start()

    def finish_out(target, dp, narrow):
        pltpu.make_async_copy(
            w_out.at[rows_of(dp, row_d, 16), rows_of(narrow, col_d, 128)],
            target.at[pl.ds(0, row_d)],
            out_sem.at[3],
        ).start()

    each_place(table, grad_gates, fast, finish_gate)
    each_place(table, grad_ups, fast, finish_up)
    each_place(table, grad_square, fast, finish_down)
    gain_grad_ref[...] = jnp.zeros_like(gain_grad_ref)

    def after(index, carry):
        part = pl.ds(pl.multiple_of(index * QUERY_BLOCK, QUERY_BLOCK), QUERY_BLOCK)
        mixed_ref[part, :] = mixed_sum[part, :].astype(BF)
        state = hidden[part, :]
        scale = lax.rsqrt(jnp.mean(state * state, axis=-1, keepdims=True) + norm_eps)
        unit = state * scale
        through = grad_normed[part, :]
        gain_grad_ref[...] += jnp.sum(through * unit, axis=0, keepdims=True)
        through = through * gain
        result = grad_mixed[part, :].astype(F32) + scale * (
            through - unit * jnp.mean(through * unit, axis=-1, keepdims=True)
        )
        grad_hidden_ref[part, :] = result
        branch = result.astype(BF)
        normed[part, :] = branch
        grad_attended_ref[part, :] = dot(branch, w_out[...], NT).astype(BF)
        return carry

    lax.fori_loop(0, x_ref.shape[0] // QUERY_BLOCK, after, 0)
    branch = normed[...]
    w_out[...] = dot(attended_ref[...].T, branch).astype(BF)
    each_place(table, grad_square, fast, finish_out)
    pltpu.make_async_copy(w_gate, w_gate, out_sem.at[0]).wait()
    pltpu.make_async_copy(w_up, w_up, out_sem.at[1]).wait()
    pltpu.make_async_copy(w_down, w_down, out_sem.at[2]).wait()
    pltpu.make_async_copy(w_out, w_out, out_sem.at[3]).wait()


def middle(tokens, attended, cotangent, valid, gains, square, gates, ups, table, fast, sizes):
    rows = tokens.shape[0]
    ff = sizes[1] * (16 if fast else 1)
    n_arrays = len(square)
    outs = pl.pallas_call(
        functools.partial(middle_kernel, fast, sizes),
        in_specs=[IN_SMEM] + [IN_VMEM] * 5 + [IN_HBM] * (3 * n_arrays),
        out_specs=[IN_VMEM] * 3 + [IN_HBM] * (3 * n_arrays) + [IN_VMEM],
        out_shape=[shape((rows, HD), BF), shape((rows, HD), F32), shape((rows, HD), BF)]
        + [shape(array.shape, BF) for array in (*square, *gates, *ups)]
        + [shape((1, HD), F32)],
        scratch_shapes=[
            pltpu.VMEM((HD, HD), BF),
            pltpu.VMEM((HD, ff), BF),
            pltpu.VMEM((HD, ff), BF),
            pltpu.VMEM((ff, HD), BF),
            pltpu.VMEM((rows, HD), F32),
            pltpu.VMEM((rows, HD), BF),
            pltpu.VMEM((HD, rows), BF),
            pltpu.VMEM((rows, HD), BF),
            pltpu.VMEM((rows, HD), F32),
            pltpu.SemaphoreType.DMA((4,)),
            pltpu.SemaphoreType.DMA((4,)),
        ],
        compiler_params=params(),
        name="middle",
    )(table, tokens, attended, cotangent, valid, gains, *square, *gates, *ups)
    mixed, grad_hidden, grad_attended = outs[:3]
    grads = [outs[3 + i * n_arrays : 3 + (i + 1) * n_arrays] for i in range(3)]
    return mixed, grad_hidden, grad_attended, *grads, outs[-1]


def weight_grad_kernel(fast, row_piece, col_piece, table, normed_t_ref, q_ref, k_ref, v_ref, *refs):
    n_arrays = 4 if fast else 1
    targets = refs[:n_arrays]
    weight, sem = refs[n_arrays:]
    ny = HD * 3 // col_piece if fast else HD // 128
    width = HD // ny
    left = normed_t_ref[...]
    for narrow in range(ny):
        for index, ref in enumerate((q_ref, k_ref, v_ref)):
            start = narrow * 3 * width + index * width
            weight[:, start : start + width] = dot(left, ref[:, narrow * width : (narrow + 1) * width]).astype(BF)

    def finish(target, dp, narrow):
        pltpu.make_async_copy(
            weight.at[rows_of(dp, row_piece, 16), rows_of(narrow, col_piece, 128)], target, sem
        ).start()

    each_place(table, targets, fast, finish)
    pltpu.make_async_copy(weight, weight, sem).wait()


def weight_grad(normed_t, grads, table, fast, row_piece, col_piece):
    if fast:
        outs = [shape((8, row_piece, col_piece), BF)] * 4
    else:
        outs = [shape((1, row_piece, col_piece), BF)]
    return pl.pallas_call(
        functools.partial(weight_grad_kernel, fast, row_piece, col_piece),
        in_specs=[IN_SMEM] + [IN_VMEM] * 4,
        out_specs=[IN_HBM] * len(outs),
        out_shape=outs,
        scratch_shapes=[pltpu.VMEM((HD, 3 * HD), BF), pltpu.SemaphoreType.DMA(())],
        compiler_params=params(),
        name="weight_grad",
    )(table, normed_t, *grads)


def input_grad_kernel(
    fast, row_piece, col_piece, ny, table, x_ref, gains_ref, grad_hidden_ref, q_ref, k_ref, v_ref, *refs
):
    n_arrays = 4 if fast else 1
    arrays = refs[:n_arrays]
    out_ref, gain_grad_ref, weight, sem = refs[n_arrays:]

    def start(source, dp, narrow):
        pltpu.make_async_copy(
            source.at[pl.ds(0, row_piece)],
            weight.at[rows_of(dp, row_piece, 16), rows_of(narrow, col_piece, 128)],
            sem,
        ).start()

    each_place(table, arrays, fast, start)
    x = x_ref[...].astype(F32)
    scale = lax.rsqrt(jnp.mean(x * x, axis=-1, keepdims=True) + norm_eps)
    pltpu.make_async_copy(weight, weight, sem).wait()
    width = HD // ny
    through = None
    for narrow in range(ny):
        for index, ref in enumerate((q_ref, k_ref, v_ref)):
            begin = narrow * 3 * width + index * width
            part = dot(ref[:, narrow * width : (narrow + 1) * width], weight[:, begin : begin + width], NT)
            through = part if through is None else through + part
    unit = x * scale
    gain_grad_ref[...] = jnp.sum(through * unit, axis=0, keepdims=True)
    through = through * gains_ref[0:1]
    out_ref[...] = grad_hidden_ref[...] + scale * (
        through - unit * jnp.mean(through * unit, axis=-1, keepdims=True)
    )


def input_gradient(tokens, gains, grad_hidden, grads, arrays, table, fast, row_piece, col_piece, ny):
    rows = tokens.shape[0]
    return pl.pallas_call(
        functools.partial(input_grad_kernel, fast, row_piece, col_piece, ny),
        in_specs=[IN_SMEM] + [IN_VMEM] * 6 + [IN_HBM] * len(arrays),
        out_specs=[IN_VMEM] * 2,
        out_shape=[shape((rows, HD), F32), shape((1, HD), F32)],
        scratch_shapes=[pltpu.VMEM((HD, 3 * HD), BF), pltpu.SemaphoreType.DMA(())],
        compiler_params=params(),
        name="input_gradient",
    )(table, tokens, gains, grad_hidden, *grads, *arrays)


def segment_ids(bucket_one, text_one):
    position = jnp.arange(LONG, dtype=jnp.int32)
    slot_index = position // SLOT
    inside = position - slot_index * SLOT
    slot_length = SHORT_PATCH + jnp.where(
        slot_index == 0, text_one[0], jnp.where(slot_index == 1, text_one[1], text_one[2])
    )
    long_valid = position < LONG_PATCH + text_one[0]
    short_valid = inside < slot_length
    return jnp.where(
        bucket_one == 1, jnp.where(long_valid, 0, -1), jnp.where(short_valid, slot_index, -1)
    ).astype(jnp.int32)


def adamw(weight, grad_total, first, second, rate):
    first_new = beta_one * first + (1.0 - beta_one) * grad_total
    second_new = beta_two * second + (1.0 - beta_two) * grad_total * grad_total
    first_hat = first_new / (1.0 - beta_one**STEP)
    second_hat = second_new / (1.0 - beta_two**STEP)
    weight_new = weight - rate * (first_hat / (jnp.sqrt(second_hat) + adam_eps) + decay_rate * weight)
    return (grad_total, first_new, second_new, weight_new)


def rows_of_shards(array, n_narrow):
    count, rows, columns = array.shape
    width = columns // n_narrow
    return array.reshape(count, rows, n_narrow, width).transpose(1, 2, 0, 3).reshape(rows, -1)


def local(
    n_dp,
    n_narrow,
    tokens,
    cotangent,
    bucket,
    text_lengths,
    attn_qkv,
    attn_out,
    ffn_in,
    ffn_out,
    norm_gains,
    first_qkv,
    first_out,
    first_ffin,
    first_ffout,
    first_gains,
    second_qkv,
    second_out,
    second_ffin,
    second_ffout,
    second_gains,
):
    fast = (n_dp, n_narrow) == (16, 2)
    perms = exchange_perms() if fast else None
    table = place_table(fast)
    me = lax.axis_index("dp") * n_narrow + lax.axis_index("narrow")
    row_d, width = attn_out.shape
    row_f = ffn_out.shape[0]
    col_f = ffn_in.shape[2]
    own_gains = norm_gains.shape[1]
    low_gains = lax.dynamic_update_slice(
        jnp.zeros((ROWS_GAIN, HD), BF), norm_gains.astype(BF), (0, me * own_gains)
    )
    if fast:
        low_qkv = attn_qkv.astype(BF).transpose(1, 0, 2).reshape(row_d, 3 * width)
        piece = jnp.concatenate((low_qkv, jnp.pad(low_gains, ((0, 0), (0, 3 * width - HD)))), axis=0)
        qkv_arrays = gather(piece, perms)
        square = gather(jnp.concatenate((attn_out.astype(BF), ffn_out.astype(BF)), axis=0), perms)
        gates = gather(ffn_in[0].astype(BF), perms)
        ups = gather(ffn_in[1].astype(BF), perms)
        sizes = (row_d, row_f, width, col_f)
        qkv_size = (row_d, 3 * width)
    else:
        whole = lambda low, axis: lax.all_gather(
            lax.all_gather(low.astype(BF), "narrow", axis=axis + 1, tiled=True), "dp", axis=axis, tiled=True
        )
        full_qkv = rows_of_shards(whole(attn_qkv, 1), n_narrow)
        gains_rows = jnp.pad(lax.psum(low_gains, AXES), ((0, 0), (0, 2 * HD)))
        qkv_arrays = (jnp.concatenate((full_qkv, gains_rows), axis=0)[None],)
        square = (jnp.concatenate((whole(attn_out, 0), whole(ffn_out, 0)), axis=0)[None],)
        full_ffin = whole(ffn_in, 1)
        gates = (full_ffin[0][None],)
        ups = (full_ffin[1][None],)
        sizes = (HD, full_ffin.shape[2], HD, full_ffin.shape[2])
        qkv_size = (HD, 3 * HD)
    tiles_of = width // 128
    segments = segment_ids(bucket[0], text_lengths[0])
    valid = (segments >= 0).astype(F32)[:, None]
    mask_q, mask_k = mask_operands(segments)
    projected, normed_t, gains = project(tokens, qkv_arrays, table, fast, *qkv_size)
    attended, extra = attend_forward(projected, mask_q, mask_k, tiles_of)
    mixed, grad_hidden, grad_attended, grad_square, grad_gates, grad_ups, gain_two = middle(
        tokens, attended, cotangent, valid, gains, square, gates, ups, table, fast, sizes
    )
    grads = attend_backward(projected, attended, grad_attended, extra, mask_k, tiles_of)
    grad_qkv = weight_grad(normed_t, grads, table, fast, *qkv_size)
    input_grad, gain_one = input_gradient(
        tokens, gains, grad_hidden, grads, qkv_arrays, table, fast, *qkv_size, n_narrow
    )
    gain_sums = lax.psum(jnp.concatenate((gain_one, gain_two), axis=0), AXES)
    share_gains = lax.dynamic_slice(gain_sums, (0, me * own_gains), (2, own_gains))
    if fast:
        share_square = reduce_to_owner(grad_square, perms)
        share_gate = reduce_to_owner(grad_gates, perms)
        share_up = reduce_to_owner(grad_ups, perms)
        share_qkv = reduce_to_owner(grad_qkv, perms).reshape(row_d, 3, width).transpose(1, 0, 2)
        share_out, share_down = share_square[:row_d], share_square[row_d:]
        share_ffin = jnp.stack((share_gate, share_up))
    else:
        own = lambda grad, axis: lax.psum_scatter(
            lax.psum_scatter(grad, "dp", scatter_dimension=axis, tiled=True),
            "narrow",
            scatter_dimension=axis + 1,
            tiled=True,
        ).astype(F32)
        ordered = grad_qkv[0][0].reshape(HD, n_narrow, 3, width).transpose(2, 0, 1, 3).reshape(3, HD, HD)
        share_qkv = own(ordered, 1)
        share_out = own(grad_square[0][0, :HD], 0)
        share_down = own(grad_square[0][0, HD:], 0)
        share_ffin = own(jnp.stack((grad_gates[0][0], grad_ups[0][0])), 1)
    shares = (share_qkv, share_out, share_ffin, share_down, share_gains)
    masters = (attn_qkv, attn_out, ffn_in, ffn_out, norm_gains)
    firsts = (first_qkv, first_out, first_ffin, first_ffout, first_gains)
    seconds = (second_qkv, second_out, second_ffin, second_ffout, second_gains)
    results = [mixed, input_grad]
    for index in range(5):
        results.extend(adamw(masters[index], shares[index], firsts[index], seconds[index], rates[index]))
    return tuple(results)


def solution(mesh):
    rows = P(("dp", "narrow"), None)
    cube = P(None, "dp", "narrow")
    flat = P("dp", "narrow")
    gain = P(None, ("dp", "narrow"))
    weights = (cube, flat, cube, flat, gain)
    in_specs = (rows, rows, P(("dp", "narrow")), rows, *weights, *weights, *weights)
    out_specs = (rows, rows, *(spec for spec in weights for _ in range(4)))
    step = functools.partial(local, mesh.shape["dp"], mesh.shape["narrow"])
    return jax.shard_map(step, mesh=mesh, in_specs=in_specs, out_specs=out_specs, check_vma=False)
```

```python
import functools

import jax
import jax.numpy as jnp
from jax import lax
from jax.experimental import pallas as pl
from jax.experimental.pallas import tpu as pltpu
from jax.sharding import PartitionSpec as P

HEADS = 16
DK = 64
SHORT_PATCH = 256
STEP = 10
HD = 1024
SLOT = 384
LONG = 1152
LONG_PATCH = 1024

norm_eps = 1e-06
score_scale = 0.125
beta_one = 0.9
beta_two = 0.999
adam_eps = 1e-08
decay_rate = 0.01
rates = (0.08, 0.8, 0.08, 0.05, 0.6)

BF = jnp.bfloat16
F32 = jnp.float32
NN = (((1,), (0,)), ((), ()))
NT = (((1,), (1,)), ((), ()))
TN = (((0,), (0,)), ((), ()))
AXES = ("dp", "narrow")
VMEM_BYTES = 60 * 2**20
ROWS_GAIN = 16
GAIN_COLS = 512
PART = 6 * 128
HALF = 2 * PART
FF_BLOCK = 256
QUERY_BLOCK = 384
ROW_PARTS = (slice(0, 512), slice(512, LONG))


def dot(left, right, dims=NN):
    return lax.dot_general(left, right, dims, preferred_element_type=F32)


def params():
    return pltpu.CompilerParams(vmem_limit_bytes=VMEM_BYTES)


def shape(dims, dtype):
    return jax.ShapeDtypeStruct(dims, dtype)


IN_VMEM = pl.BlockSpec(memory_space=pltpu.VMEM)
IN_HBM = pl.BlockSpec(memory_space=pl.ANY)
IN_SMEM = pl.BlockSpec(memory_space=pltpu.SMEM)


BY_Z = (("z2", "z1"), ("z1", "z2"), ("x", "y"), ("y", "x"), ("core", "core"))
BY_PLANE = (("x", "y"), ("y", "x"), ("z2", "z1"), ("z1", "z2"), ("core", "core"))
BIT = {"y": 1, "core": 2, "x": 4, "z1": 8, "z2": 16}


def partners(kinds):
    return [(me, me ^ BIT[kinds[(me >> 1) & 1]]) for me in range(32)]


def swap(array, kinds):
    return lax.ppermute(array, AXES, partners(kinds))


def owner_of(me, index, order):
    flips = [0, 0]
    for step in range(4):
        if (index >> step) & 1:
            for core in range(2):
                flips[core] ^= BIT[order[step][core]]
    own = me ^ 2 if index >> 4 else me
    device = own ^ jnp.where((own >> 1) & 1 == 1, flips[1], flips[0])
    return device >> 1, device & 1


def tie(*values):
    return lax.optimization_barrier(values)


def total(*parts):
    return sum(part.astype(F32) for part in parts)


def joined(held, arrived):
    return jnp.concatenate((held, arrived), axis=0)


def add_low(parts, low, high):
    return total(*(part[low:high] for part in parts)).astype(BF)


def each_place(me_ref, arrays, order, body):
    if order is None:
        body(arrays[0].at[0], 0, 0)
        return
    me = me_ref[0]
    for index in range(32):
        dp, narrow = owner_of(me, index, order)
        body(arrays[index // 8].at[index % 8], dp, narrow)


def span(start, size, unit):
    if isinstance(start, int):
        return pl.ds(start * size, size)
    return pl.ds(pl.multiple_of(start * size, unit), size)


def head_rows(dp, fast):
    return (dp & 4) * 2 + (dp >> 3) * 4 + (dp & 3) if fast else 0


def load_half(me_ref, arrays, order, rows_piece, weight, sem):
    cols = PART if order else HALF

    def start(source, dp, narrow):
        pltpu.make_async_copy(
            source.at[pl.ds(0, rows_piece), pl.ds(0, cols)],
            weight.at[span(dp, rows_piece, 16), span(narrow, cols, 128)],
            sem,
        ).start()

    each_place(me_ref, arrays, order, start)


def first_project_kernel(order, rows_piece, me_ref, x_ref, *refs):
    n_arrays = 4 if order else 1
    arrays = refs[:n_arrays]
    out_ref, normed_ref, normed_t_ref, gains_ref, weight, gain_parts, sem, gain_sem = refs[n_arrays:]
    step = pl.program_id(0)

    @pl.when(step == 0)
    def _():
        slots = 8 if order else 1
        for index in range(n_arrays):
            pltpu.make_async_copy(
                arrays[index].at[:, pl.ds(rows_piece, ROWS_GAIN), pl.ds(0, GAIN_COLS)],
                gain_parts.at[pl.ds(index * slots, slots)],
                gain_sem,
            ).start()
        load_half(me_ref, arrays, order, rows_piece, weight, sem)
        x = x_ref[...].astype(F32)
        scaled = x * lax.rsqrt(jnp.mean(x * x, axis=-1, keepdims=True) + norm_eps)
        pltpu.make_async_copy(gain_parts, gain_parts, gain_sem).wait()
        parts = jnp.sum(gain_parts[...].astype(F32), axis=0)
        one = jnp.concatenate((parts[0:1], parts[1:2]), axis=1)
        gains_ref[...] = jnp.concatenate((one, jnp.concatenate((parts[2:3], parts[3:4]), axis=1)), axis=0)
        low = (scaled * one).astype(BF)
        normed_ref[...] = low
        normed_t_ref[...] = low.T
        pltpu.make_async_copy(weight, weight, sem).wait()

    column = pl.multiple_of(step * PART, PART)
    out_ref[...] = dot(normed_ref[...], weight[:, pl.ds(column, PART)]).astype(BF)


def first_project(me, tokens, arrays, order, rows_piece):
    rows = tokens.shape[0]
    full = lambda dims: pl.BlockSpec(dims, lambda step: (0,) * len(dims))
    return pl.pallas_call(
        functools.partial(first_project_kernel, order, rows_piece),
        grid=(2,),
        in_specs=[IN_SMEM, full((rows, HD))] + [IN_HBM] * len(arrays),
        out_specs=[
            pl.BlockSpec((rows, PART), lambda step: (0, step)),
            full((rows, HD)),
            full((HD, rows)),
            full((2, HD)),
        ],
        out_shape=[shape((rows, HALF), BF), shape((rows, HD), BF), shape((HD, rows), BF), shape((2, HD), F32)],
        scratch_shapes=[
            pltpu.VMEM((HD, HALF), BF),
            pltpu.VMEM((32 if order else 1, ROWS_GAIN, GAIN_COLS), BF),
            pltpu.SemaphoreType.DMA(()),
            pltpu.SemaphoreType.DMA(()),
        ],
        compiler_params=params(),
        name="first_project",
    )(me, tokens, *arrays)


def second_project_kernel(order, rows_piece, me_ref, normed_ref, *refs):
    n_arrays = 4 if order else 1
    arrays = refs[:n_arrays]
    out_ref, weight, sem = refs[n_arrays:]
    step = pl.program_id(0)

    @pl.when(step == 0)
    def _():
        load_half(me_ref, arrays, order, rows_piece, weight, sem)
        pltpu.make_async_copy(weight, weight, sem).wait()

    column = pl.multiple_of(step * PART, PART)
    out_ref[...] = dot(normed_ref[...], weight[:, pl.ds(column, PART)]).astype(BF)


def second_project(me, normed, arrays, order, rows_piece):
    rows = normed.shape[0]
    return pl.pallas_call(
        functools.partial(second_project_kernel, order, rows_piece),
        grid=(2,),
        in_specs=[IN_SMEM, pl.BlockSpec((rows, HD), lambda step: (0, 0))] + [IN_HBM] * len(arrays),
        out_specs=pl.BlockSpec((rows, PART), lambda step: (0, step)),
        out_shape=shape((rows, HALF), BF),
        scratch_shapes=[pltpu.VMEM((HD, HALF), BF), pltpu.SemaphoreType.DMA(())],
        compiler_params=params(),
        name="second_project",
    )(me, normed, *arrays)


def three_parts(values):
    first = values.astype(BF)
    rest = values - first.astype(F32)
    second = rest.astype(BF)
    return first, second, (rest - second.astype(F32)).astype(BF)


def mask_operands(segments):
    kind = jnp.arange(64, dtype=jnp.int32)
    mine = segments[None, :] + 1 == kind[:, None]
    query_side = jnp.where(mine, -1e30, 0.0).astype(BF)
    key_side = jnp.where((kind[None, :] < 4) & ~mine.T, 1.0, 0.0).astype(BF)
    return (
        jnp.concatenate((query_side, query_side), axis=0),
        jnp.concatenate((key_side, key_side), axis=1),
    )


def attend_forward_kernel(q_ref, k_ref, v_ref, mask_q_ref, mask_k_ref, out_ref, extra_ref):
    queries_t = (q_ref[...].astype(F32) * score_scale).astype(BF).T
    keys = k_ref[...]
    values_t = v_ref[...].T
    mask_q = mask_q_ref[...]
    mask_k = mask_k_ref[...]
    lane = lax.broadcasted_iota(jnp.int32, (1, 128), 1)
    row = lax.broadcasted_iota(jnp.int32, (64, 1), 0)
    ones = jnp.ones((16, LONG), BF)
    key_sides = (jnp.where(lane < 64, keys, mask_k), jnp.where(lane >= 64, keys, mask_k))
    query_sides = (
        jnp.concatenate((queries_t[0:64], mask_q[64:128]), axis=0),
        jnp.concatenate((mask_q[0:64], queries_t[64:128]), axis=0),
    )
    value_sides = [jnp.concatenate((values_t[64 * head : 64 * head + 64], ones), axis=0) for head in range(2)]
    out_blocks = ([], [])
    log_blocks = ([], [])

    def score(head, start):
        return dot(key_sides[head], query_sides[head][:, start : start + QUERY_BLOCK])

    def finish(head, top, expo):
        both = dot(value_sides[head], expo)
        sums = both[64:65]
        out_blocks[head].append((both[0:64] * (1.0 / sums)).astype(BF))
        log_blocks[head].append(-(top + jnp.log(sums)))

    jobs = [(head, start) for head in range(2) for start in range(0, LONG, QUERY_BLOCK)]
    scores = score(*jobs[0])
    waiting = None
    for index, job in enumerate(jobs):
        later = score(*jobs[index + 1]) if index + 1 < len(jobs) else None
        top = jnp.max(scores, axis=0, keepdims=True)
        expo = jnp.exp(scores - top).astype(BF)
        if waiting is not None:
            finish(*waiting)
        waiting = (job[0], top, expo)
        scores = later
    finish(*waiting)
    outs = [jnp.concatenate(blocks, axis=1) for blocks in out_blocks]
    extras = []
    for head in range(2):
        extra = mask_q[0:64].astype(F32)
        for index, part in enumerate(three_parts(jnp.concatenate(log_blocks[head], axis=1))):
            extra = jnp.where(row == 4 + index, part.astype(F32), extra)
        extras.append(extra.astype(BF))
    out_ref[...] = jnp.concatenate(outs, axis=0).T
    extra_ref[...] = jnp.concatenate((extras[1], extras[0]), axis=0).T


def tile_specs(rows, narrow, first):
    return [pl.BlockSpec((rows, 128), lambda i, c=c: (0, narrow * 6 + (first + i) * 3 + c)) for c in range(3)]


def attend_forward(projected, narrow, mask_q, mask_k):
    rows = projected.shape[0]
    tile = pl.BlockSpec((rows, 128), lambda i: (0, i))
    return pl.pallas_call(
        attend_forward_kernel,
        grid=(2,),
        in_specs=tile_specs(rows, narrow, 0)
        + [pl.BlockSpec((128, rows), lambda i: (0, 0)), pl.BlockSpec((rows, 128), lambda i: (0, 0))],
        out_specs=[tile, tile],
        out_shape=[shape((rows, 256), BF), shape((rows, 256), BF)],
        compiler_params=params(),
        name="attend_forward",
    )(projected, projected, projected, mask_q, mask_k)


def attend_backward_kernel(
    q_ref, k_ref, v_ref, out_ref, grad_ref, extra_ref, mask_k_ref, result_ref
):
    queries = (q_ref[...].astype(F32) * score_scale).astype(BF)
    queries_t = queries.T
    keys = k_ref[...]
    keys_t = keys.T
    values_t = v_ref[...].T
    grad = grad_ref[...]
    grad_t = grad.T
    extra = extra_ref[...]
    mask_k_t = mask_k_ref[...].T
    lane = lax.broadcasted_iota(jnp.int32, (1, 128), 1)
    row = lax.broadcasted_iota(jnp.int32, (64, 1), 0)
    product_t = (grad.astype(F32) * out_ref[...].astype(F32)).T
    inner = []
    for head in (1, 0):
        total = -jnp.sum(product_t[64 * head : 64 * head + 64], axis=0, keepdims=True)
        rows = jnp.zeros((64, LONG), F32)
        for index, part in enumerate(three_parts(total)):
            rows = jnp.where(row == index, part.astype(F32), rows)
        inner.append(rows.astype(BF))
    inner_cols = jnp.concatenate(inner, axis=0).T
    key_extra = jnp.where((row >= 4) & (row < 7), 1.0, mask_k_t[0:64].astype(F32)).astype(BF)
    value_extra = jnp.broadcast_to(jnp.where(row < 3, 1.0, 0.0).astype(BF), (64, LONG))
    grad_q = []
    grad_k = []
    grad_v = []
    for head in range(2):
        half = slice(64 * head, 64 * head + 64)
        own = (lane < 64) if head == 0 else (lane >= 64)
        query_side = jnp.where(own, queries, extra)
        grad_side = jnp.where(own, grad, inner_cols)
        if head == 0:
            key_side = jnp.concatenate((keys_t[half], key_extra), axis=0)
            value_side = jnp.concatenate((values_t[half], value_extra), axis=0)
        else:
            key_side = jnp.concatenate((key_extra, keys_t[half]), axis=0)
            value_side = jnp.concatenate((value_extra, values_t[half]), axis=0)
        q_blocks = []
        k_total = None
        v_total = None
        for start in range(0, LONG, QUERY_BLOCK):
            block = slice(start, start + QUERY_BLOCK)
            probs = jnp.exp(dot(query_side[block], key_side))
            grad_scores = (probs * dot(grad_side[block], value_side)).astype(BF)
            v_part = dot(grad_t[half, block], probs.astype(BF))
            k_part = dot(queries_t[half, block], grad_scores)
            v_total = v_part if v_total is None else v_total + v_part
            k_total = k_part if k_total is None else k_total + k_part
            q_blocks.append(dot(grad_scores, keys) * score_scale)
        grad_q.append(jnp.concatenate(q_blocks, axis=0))
        grad_k.append(k_total)
        grad_v.append(v_total)
    result_ref[:, 0:128] = jnp.where(lane < 64, grad_q[0], grad_q[1]).astype(BF)
    result_ref[:, 128:256] = jnp.concatenate(grad_k, axis=0).astype(BF).T
    result_ref[:, 256:384] = jnp.concatenate(grad_v, axis=0).astype(BF).T


def attend_backward(projected, attended, grad_attended, extra, mask_k, half, narrow, first, count):
    rows = projected.shape[0]
    own = pl.BlockSpec((rows, 128), lambda i: (0, first + i))
    return pl.pallas_call(
        attend_backward_kernel,
        grid=(count,),
        in_specs=tile_specs(rows, narrow, first)
        + [
            own,
            pl.BlockSpec((rows, 128), lambda i: (0, half * 4 + narrow * 2 + first + i)),
            own,
            pl.BlockSpec((rows, 128), lambda i: (0, 0)),
        ],
        out_specs=pl.BlockSpec((rows, 384), lambda i: (0, i)),
        out_shape=shape((rows, 384 * count), BF),
        compiler_params=params(),
        name="attend_backward",
    )(projected, projected, projected, attended, grad_attended, extra, mask_k)


def one_buffer(dims):
    return pl.BlockSpec(dims, lambda step: (0,) * len(dims), pipeline_mode=pl.Buffered(buffer_count=1))


def load_out(me_ref, arrays, order, rows_piece, w_out, sem):
    cols, at = (GAIN_COLS, PART) if order else (HD, HALF)

    def start(source, dp, narrow):
        pltpu.make_async_copy(
            source.at[pl.ds(0, rows_piece), pl.ds(at, cols)],
            w_out.at[span(head_rows(dp, order is not None), rows_piece, 16), span(narrow, cols, 128)],
            sem,
        ).start()

    each_place(me_ref, arrays, order, start)


def load_wide(me_ref, arrays, order, rows_piece, targets, sems):
    cols = targets[0].shape[1] // (2 if order else 1)

    def start(source, dp, narrow):
        for index, target in enumerate(targets):
            pltpu.make_async_copy(
                source.at[pl.ds(index * rows_piece, rows_piece)],
                target.at[span(dp, rows_piece, 16), span(narrow, cols, 128)],
                sems[index],
            ).start()

    each_place(me_ref, arrays, order, start)


def load_wide_by_half(me_ref, arrays, order, rows_piece, targets, sems):
    whole = targets[0].shape[1]
    if order is None:
        for index, target in enumerate(targets):
            for half in range(2):
                cols = pl.ds(half * (whole // 2), whole // 2)
                pltpu.make_async_copy(
                    arrays[0].at[0, pl.ds(index * rows_piece, rows_piece), cols], target.at[:, cols], sems.at[index, half]
                ).start()
        return
    for half in range(2):

        def start(source, dp, narrow, half=half):
            @pl.when(narrow == half)
            def _():
                for index, target in enumerate(targets):
                    pltpu.make_async_copy(
                        source.at[pl.ds(index * rows_piece, rows_piece)],
                        target.at[span(dp, rows_piece, 16), pl.ds(half * (whole // 2), whole // 2)],
                        sems.at[index, half],
                    ).start()

        each_place(me_ref, arrays, order, start)


def wait_half(targets, sems, half):
    whole = targets[0].shape[1]
    for index, target in enumerate(targets):
        part = target.at[:, pl.ds(half * (whole // 2), whole // 2)]
        pltpu.make_async_copy(part, part, sems.at[index, half]).wait()


def load_down(me_ref, arrays, order, w_down, sem):
    rows, cols = arrays[0].shape[1:]

    def start(source, dp, narrow):
        pltpu.make_async_copy(source, w_down.at[span(dp, rows, 16), span(narrow, cols, 128)], sem).start()

    each_place(me_ref, arrays, order, start)


N_GROUPS = 4


def load_down_by_group(me_ref, arrays, order, w_down, sems):
    rows, cols = arrays[0].shape[1:]
    if order is None:
        rows = rows // N_GROUPS
        for group in range(N_GROUPS):
            part = pl.ds(group * rows, rows)
            pltpu.make_async_copy(arrays[0].at[0, part], w_down.at[part], sems.at[group]).start()
        return

    def start(source, dp, narrow):
        pltpu.make_async_copy(
            source, w_down.at[span(dp, rows, 16), span(narrow, cols, 128)], sems.at[dp >> 2]
        ).start()

    each_place(me_ref, arrays, order, start)


def wait_group(w_down, sems, group):
    rows = w_down.shape[0] // N_GROUPS
    part = w_down.at[pl.ds(group * rows, rows)]
    pltpu.make_async_copy(part, part, sems.at[group]).wait()


def at_step(step, wanted, body):
    pl.when(step == wanted)(body)


def last_step_of(rows):
    return -(-rows // FF_BLOCK) - 1


def all_of(ref, sem):
    pltpu.make_async_copy(ref, ref, sem).wait()


def gelu_parts(gate):
    square = gate * gate
    curve = jnp.tanh(0.7978845608028654 * gate * (1.0 + 0.044715 * square))
    half = 0.5 * (1.0 + curve)
    slope = half + (0.5 * gate) * (1.0 - curve * curve) * (
        0.7978845608028654 + (0.7978845608028654 * 3.0 * 0.044715) * square
    )
    return gate * half, slope


def feed_in_kernel(orders, rows_piece, me_ref, x_ref, att_a, att_b, att_c, att_d, cotangent_ref, valid_ref, gains_ref, *refs):
    square_order, wide_order, down_order = orders
    n_arrays = 4 if wide_order else 1
    square, wide = (refs[i * n_arrays : (i + 1) * n_arrays] for i in range(2))
    refs = refs[2 * n_arrays :]
    active_ref, sloped_ref, inner_ref, hidden_out, normed_t_out, grad_mixed_out = refs[:6]
    grad_down = refs[6 : 6 + n_arrays]
    w_out, w_gate, w_up, w_down, hidden, normed, normed_t, grad_mixed, sem, wide_sems, out_sems, down_sems = refs[6 + n_arrays :]
    step = pl.program_id(0)

    @pl.when(step == 0)
    def _():
        load_out(me_ref, square, square_order, rows_piece, w_out, sem)
        load_wide_by_half(me_ref, wide, wide_order, rows_piece, (w_gate, w_up), wide_sems)
        gain = gains_ref[1:2]
        all_of(w_out, sem)

        def before(index, carry):
            part = pl.ds(pl.multiple_of(index * QUERY_BLOCK, QUERY_BLOCK), QUERY_BLOCK)
            left = jnp.concatenate([ref[part, :] for ref in (att_a, att_b, att_c, att_d)], axis=1)
            state = x_ref[part, :].astype(F32) + dot(left, w_out[...])
            hidden[part, :] = state
            low = (state * lax.rsqrt(jnp.mean(state * state, axis=-1, keepdims=True) + norm_eps) * gain).astype(BF)
            normed[part, :] = low
            normed_t[:, part] = low.T
            grad_mixed[part, :] = (cotangent_ref[part, :].astype(F32) * valid_ref[part, :]).astype(BF)
            return carry

        lax.fori_loop(0, x_ref.shape[0] // QUERY_BLOCK, before, 0)
        pltpu.make_async_copy(hidden, hidden_out, out_sems.at[0]).start()
        pltpu.make_async_copy(normed_t, normed_t_out, out_sems.at[1]).start()
        pltpu.make_async_copy(grad_mixed, grad_mixed_out, out_sems.at[2]).start()
        wait_half((w_gate, w_up), wide_sems, 0)

    at_step(step, w_gate.shape[1] // 2 // FF_BLOCK, lambda: wait_half((w_gate, w_up), wide_sems, 1))
    cols = pl.ds(pl.multiple_of(step * FF_BLOCK, FF_BLOCK), FF_BLOCK)
    gate_w = w_gate[:, cols]
    up_w = w_up[:, cols]
    found = [(dot(normed[part, :], gate_w), dot(normed[part, :], up_w)) for part in ROW_PARTS]
    down_sum = None
    for part, (gate, upward) in zip(ROW_PARTS, found):
        active, slope = gelu_parts(gate)
        active_ref[part, :] = active.astype(BF)
        sloped_ref[part, :] = (upward * slope).astype(BF)
        inner = (active * upward).astype(BF)
        inner_ref[part, :] = inner
        down_part = dot(inner.T, grad_mixed[part, :])
        down_sum = down_part if down_sum is None else down_sum + down_part
    w_down[cols, :] = down_sum.astype(BF)

    ff = w_down.shape[0]
    for group in range(N_GROUPS):

        def store_group(group=group):
            if down_order is None:
                part = pl.ds(group * (ff // N_GROUPS), ff // N_GROUPS)
                pltpu.make_async_copy(w_down.at[part], grad_down[0].at[0, part], down_sems.at[group]).start()
                return

            def finish(target, dp, narrow):
                rows, width = target.shape

                @pl.when(dp >> 2 == group)
                def _():
                    pltpu.make_async_copy(
                        w_down.at[span(dp, rows, 16), span(narrow, width, 128)], target, down_sems.at[group]
                    ).start()

            each_place(me_ref, grad_down, down_order, finish)

        at_step(step, last_step_of((group + 1) * (ff // N_GROUPS)), store_group)

    @pl.when(step == pl.num_programs(0) - 1)
    def _():
        pltpu.make_async_copy(hidden, hidden_out, out_sems.at[0]).wait()
        pltpu.make_async_copy(normed_t, normed_t_out, out_sems.at[1]).wait()
        pltpu.make_async_copy(grad_mixed, grad_mixed_out, out_sems.at[2]).wait()
        for group in range(N_GROUPS):
            wait_group(w_down, down_sems, group)


def feed_in(me, tokens, attended, cotangent, valid, gains, square, wide, orders, rows_piece, ff, down_shape):
    rows = tokens.shape[0]
    n_arrays = len(square)
    tile = pl.BlockSpec((rows, FF_BLOCK), lambda step: (0, step))
    outs = pl.pallas_call(
        functools.partial(feed_in_kernel, orders, rows_piece),
        grid=(ff // FF_BLOCK,),
        in_specs=[IN_SMEM]
        + [one_buffer(array.shape) for array in (tokens, *attended, cotangent, valid, gains)]
        + [IN_HBM] * (2 * n_arrays),
        out_specs=[tile] * 3 + [IN_HBM] * (3 + n_arrays),
        out_shape=[
            shape((rows, ff), BF),
            shape((rows, ff), BF),
            shape((rows, ff), BF),
            shape((rows, HD), F32),
            shape((HD, rows), BF),
            shape((rows, HD), BF),
        ]
        + [shape(down_shape, BF)] * n_arrays,
        scratch_shapes=[
            pltpu.VMEM((HD, HD), BF),
            pltpu.VMEM((HD, ff), BF),
            pltpu.VMEM((HD, ff), BF),
            pltpu.VMEM((ff, HD), BF),
            pltpu.VMEM((rows, HD), F32),
            pltpu.VMEM((rows, HD), BF),
            pltpu.VMEM((HD, rows), BF),
            pltpu.VMEM((rows, HD), BF),
            pltpu.SemaphoreType.DMA(()),
            pltpu.SemaphoreType.DMA((2, 2)),
            pltpu.SemaphoreType.DMA((3,)),
            pltpu.SemaphoreType.DMA((N_GROUPS,)),
        ],
        compiler_params=params(),
        name="feed_in",
    )(me, tokens, *attended, cotangent, valid, gains, *square, *wide)
    return (*outs[:6], outs[6:])


def feed_grad_kernel(orders, rows_piece, me_ref, active_ref, sloped_ref, grad_mixed_ref, normed_t_ref, *refs):
    wide_order, down_order = orders
    n_arrays = 4 if wide_order else 1
    down = refs[:n_arrays]
    grad_gate_ref, grad_up_ref = refs[n_arrays : n_arrays + 2]
    grad_wide = refs[n_arrays + 2 : 2 * n_arrays + 2]
    w_down, w_gate, w_up, down_sems, out_sems = refs[2 * n_arrays + 2 :]
    step = pl.program_id(0)

    @pl.when(step == 0)
    def _():
        load_down_by_group(me_ref, down, down_order, w_down, down_sems)

    ff = w_down.shape[0]
    for group in range(N_GROUPS):
        at_step(step, group * (ff // N_GROUPS) // FF_BLOCK, lambda group=group: wait_group(w_down, down_sems, group))

    cols = pl.ds(pl.multiple_of(step * FF_BLOCK, FF_BLOCK), FF_BLOCK)
    grad_inner = dot(grad_mixed_ref[...], w_down[cols, :], NT)
    grad_gate = (grad_inner * sloped_ref[...].astype(F32)).astype(BF)
    grad_up = (grad_inner * active_ref[...].astype(F32)).astype(BF)
    grad_gate_ref[...] = grad_gate
    grad_up_ref[...] = grad_up
    w_gate[:, cols] = dot(normed_t_ref[...], grad_gate).astype(BF)
    w_up[:, cols] = dot(normed_t_ref[...], grad_up).astype(BF)

    ends = (ff // 2, ff // 2 + 3 * FF_BLOCK + FF_BLOCK // 2, ff)
    width = ff // 2 if wide_order else ff
    for place, (begin, end) in enumerate(zip((0, *ends), ends)):

        def store(place=place, begin=begin, end=end):
            count = end - begin

            def finish(target, dp, narrow):
                def copies():
                    for index, source in enumerate((w_gate, w_up)):
                        pltpu.make_async_copy(
                            source.at[span(dp, rows_piece, 16), pl.ds(begin, count)],
                            target.at[pl.ds(index * rows_piece, rows_piece), pl.ds(begin % width, count)],
                            out_sems.at[index, place],
                        ).start()

                if wide_order is None:
                    copies()
                else:
                    pl.when(narrow == begin // width)(copies)

            each_place(me_ref, grad_wide, wide_order, finish)

        at_step(step, last_step_of(end), store)

    @pl.when(step == pl.num_programs(0) - 1)
    def _():
        for index, source in enumerate((w_gate, w_up)):
            for place, (begin, end) in enumerate(zip((0, *ends), ends)):
                part = source.at[:, pl.ds(begin, end - begin)]
                pltpu.make_async_copy(part, part, out_sems.at[index, place]).wait()


def feed_grad(me, active, sloped, grad_mixed, normed_t, down, orders, rows_piece, wide_shape):
    rows, ff = active.shape
    n_arrays = len(down)
    tile = pl.BlockSpec((rows, FF_BLOCK), lambda step: (0, step))
    outs = pl.pallas_call(
        functools.partial(feed_grad_kernel, orders, rows_piece),
        grid=(ff // FF_BLOCK,),
        in_specs=[IN_SMEM, tile, tile, one_buffer((rows, HD)), one_buffer((HD, rows))] + [IN_HBM] * n_arrays,
        out_specs=[tile, tile] + [IN_HBM] * n_arrays,
        out_shape=[shape((rows, ff), BF)] * 2 + [shape(wide_shape, BF)] * n_arrays,
        scratch_shapes=[
            pltpu.VMEM((ff, HD), BF),
            pltpu.VMEM((HD, ff), BF),
            pltpu.VMEM((HD, ff), BF),
            pltpu.SemaphoreType.DMA((N_GROUPS,)),
            pltpu.SemaphoreType.DMA((2, 3)),
        ],
        compiler_params=params(),
        name="feed_grad",
    )(me, active, sloped, grad_mixed, normed_t, *down)
    return outs[0], outs[1], outs[2:]


def feed_out_kernel(orders, rows_piece, me_ref, inner_ref, grad_gate_ref, grad_up_ref, hidden_ref, grad_mixed_ref, gains_ref, *refs):
    square_order, wide_order, down_order = orders
    n_arrays = 4 if wide_order else 1
    square, wide, down = (refs[i * n_arrays : (i + 1) * n_arrays] for i in range(3))
    mixed_ref, grad_hidden_ref, grad_attended_ref, gain_grad_ref = refs[3 * n_arrays : 3 * n_arrays + 4]
    w_out, w_gate, w_up, w_down, sems = refs[3 * n_arrays + 4 :]
    step = pl.program_id(0)

    @pl.when(step == 0)
    def _():
        load_down(me_ref, down, down_order, w_down, sems.at[3])
        load_wide(me_ref, wide, wide_order, rows_piece, (w_gate, w_up), (sems.at[1], sems.at[2]))
        load_out(me_ref, square, square_order, rows_piece, w_out, sems.at[0])
        gain_grad_ref[...] = jnp.zeros_like(gain_grad_ref)
        all_of(w_down, sems.at[3])

    @pl.when(step < pl.num_programs(0) // 2)
    def _():
        mixed_ref[...] = (hidden_ref[...] + dot(inner_ref[...], w_down[...])).astype(BF)

    @pl.when(step == pl.num_programs(0) // 2)
    def _():
        all_of(w_gate, sems.at[1])
        all_of(w_up, sems.at[2])
        all_of(w_out, sems.at[0])

    @pl.when(step >= pl.num_programs(0) // 2)
    def _():
        state = hidden_ref[...]
        through = dot(grad_gate_ref[...], w_gate[...], NT) + dot(grad_up_ref[...], w_up[...], NT)
        scale = lax.rsqrt(jnp.mean(state * state, axis=-1, keepdims=True) + norm_eps)
        unit = state * scale
        gain_grad_ref[...] += jnp.sum(through * unit, axis=0, keepdims=True)
        through = through * gains_ref[1:2]
        result = grad_mixed_ref[...].astype(F32) + scale * (
            through - unit * jnp.mean(through * unit, axis=-1, keepdims=True)
        )
        grad_hidden_ref[...] = result
        grad_attended_ref[...] = dot(result.astype(BF), w_out[...], NT).astype(BF)


def feed_out(me, inner, grad_gate, grad_up, hidden, grad_mixed, gains, square, wide, down, orders, rows_piece):
    rows, ff = inner.shape
    n_arrays = len(down)
    count = rows // QUERY_BLOCK
    early = lambda cols: pl.BlockSpec((QUERY_BLOCK, cols), lambda step: (jnp.minimum(step, count - 1), 0))
    late = lambda cols: pl.BlockSpec((QUERY_BLOCK, cols), lambda step: (jnp.maximum(step - count, 0), 0))
    both = pl.BlockSpec((QUERY_BLOCK, HD), lambda step: (step % count, 0))
    return pl.pallas_call(
        functools.partial(feed_out_kernel, orders, rows_piece),
        grid=(2 * count,),
        in_specs=[IN_SMEM, early(ff), late(ff), late(ff), both, late(HD), one_buffer((2, HD))]
        + [IN_HBM] * (3 * n_arrays),
        out_specs=[early(HD), late(HD), late(HD), pl.BlockSpec((1, HD), lambda step: (0, 0))],
        out_shape=[shape((rows, HD), BF), shape((rows, HD), F32), shape((rows, HD), BF), shape((1, HD), F32)],
        scratch_shapes=[
            pltpu.VMEM((HD, HD), BF),
            pltpu.VMEM((HD, ff), BF),
            pltpu.VMEM((HD, ff), BF),
            pltpu.VMEM((ff, HD), BF),
            pltpu.SemaphoreType.DMA((4,)),
        ],
        compiler_params=params(),
        name="feed_out",
    )(me, inner, grad_gate, grad_up, hidden, grad_mixed, gains, *square, *wide, *down)


def half_of_grads(refs):
    wide = []
    held = []
    for ref in refs:
        held.append(ref)
        if sum(part.shape[1] for part in held) == PART:
            wide.append(held)
            held = []
    return wide


def fetch(sources, targets, sems):
    copies = [pltpu.make_async_copy(*triple) for triple in zip(sources, targets, sems)]
    for copy in copies:
        copy.start()

    def get(index):
        copies[index].wait()
        return targets[index][...]

    return get


def fetched(arrays):
    return [pltpu.VMEM(array.shape, array.dtype) for array in arrays] + [pltpu.SemaphoreType.DMA((len(arrays),))]


def weight_grad_kernel(order, rows_piece, n_grads, with_out, me_ref, *refs):
    n_arrays = 4 if order else 1
    fast = order is not None
    n_in = 1 + n_grads + (5 if with_out else 0)
    sources, targets, own = refs[:n_in], refs[n_in : n_in + n_arrays], refs[n_in + n_arrays :]
    held, in_sems = own[:n_in], own[n_in]
    weight, sems = own[n_in + 1 : n_in + 3]
    get = fetch(sources, held, [in_sems.at[index] for index in range(n_in)])
    cols = PART if fast else HALF
    left = get(0)
    begin = 1
    for index, group in enumerate(half_of_grads(sources[1 : 1 + n_grads])):
        right = [get(begin + place) for place in range(len(group))]
        begin += len(group)
        right = right[0] if len(right) == 1 else jnp.concatenate(right, axis=1)
        part = pl.ds(index * PART, PART)
        weight[:, part] = dot(left, right).astype(BF)

        def finish(target, dp, narrow, index=index, part=part):
            copy = pltpu.make_async_copy(
                weight.at[span(dp, rows_piece, 16), part],
                target.at[pl.ds(0, rows_piece), pl.ds(0 if fast else index * PART, PART)],
                sems.at[index],
            )
            if fast:
                pl.when(narrow == index)(copy.start)
            else:
                copy.start()

        each_place(me_ref, targets, order, finish)
    if with_out:
        w_out, out_sem = own[n_in + 3 :]
        col_d = GAIN_COLS if fast else HD
        attended = [get(1 + n_grads + index) for index in range(4)]
        branch = get(n_in - 1).astype(BF)
        for index in range(4):
            w_out[index * 256 : (index + 1) * 256, :] = dot(attended[index].T, branch).astype(BF)

        def finish_out(target, dp, narrow):
            pltpu.make_async_copy(
                w_out.at[span(head_rows(dp, fast), rows_piece, 16), span(narrow, col_d, 128)],
                target.at[pl.ds(0, rows_piece), pl.ds(cols, col_d)],
                out_sem,
            ).start()

        each_place(me_ref, targets, order, finish_out)
        all_of(w_out, out_sem)
    for index in range(2):
        part = weight.at[:, pl.ds(index * PART, PART)]
        pltpu.make_async_copy(part, part, sems.at[index]).wait()


def weight_grad(me, normed_t, grads, order, rows_piece, attended=(), grad_hidden=None):
    with_out = grad_hidden is not None
    cols = (PART if order else HALF) + ((GAIN_COLS if order else HD) if with_out else 0)
    outs = [shape((8 if order else 1, rows_piece, cols), BF)] * (4 if order else 1)
    more = [*attended, grad_hidden] if with_out else []
    given = [normed_t, *grads, *more]
    scratch = fetched(given) + [pltpu.VMEM((HD, HALF), BF), pltpu.SemaphoreType.DMA((2,))]
    if with_out:
        scratch += [pltpu.VMEM((HD, HD), BF), pltpu.SemaphoreType.DMA(())]
    return pl.pallas_call(
        functools.partial(weight_grad_kernel, order, rows_piece, len(grads), with_out),
        in_specs=[IN_SMEM] + [IN_HBM] * len(given),
        out_specs=[IN_HBM] * len(outs),
        out_shape=outs,
        scratch_shapes=scratch,
        compiler_params=params(),
        name="weight_grad",
    )(me, *given)


def input_grad_kernel(order, rows_piece, n_grads, last, me_ref, *refs):
    n_arrays = 4 if order else 1
    n_in = n_grads + (3 if last else 0)
    arrays, sources = refs[:n_arrays], refs[n_arrays : n_arrays + n_in]
    refs = refs[n_arrays + n_in :]
    if last:
        gains_ref, out_ref, gain_grad_ref = refs[:3]
        refs = refs[3:]
    else:
        out_ref = refs[0]
        refs = refs[1:]
    held, in_sems, weight, sem = refs[:n_in], refs[n_in], refs[n_in + 1], refs[n_in + 2]
    load_half(me_ref, arrays, order, rows_piece, weight, sem)
    get = fetch(sources, held, [in_sems.at[index] for index in range(n_in)])
    left = jnp.concatenate([get(index) for index in range(n_grads)], axis=1)
    all_of(weight, sem)
    if not last:
        out_ref[...] = dot(left, weight[...], NT)
        return
    out_ref[...] = dot(left, weight[...], NT)
    through = get(n_grads) + out_ref[...]
    x = get(n_grads + 1).astype(F32)
    scale = lax.rsqrt(jnp.mean(x * x, axis=-1, keepdims=True) + norm_eps)
    unit = x * scale
    gain_grad_ref[...] = jnp.sum(through * unit, axis=0, keepdims=True)
    through = through * gains_ref[0:1]
    out_ref[...] = get(n_grads + 2) + scale * (through - unit * jnp.mean(through * unit, axis=-1, keepdims=True))


def input_gradient(me, grads, arrays, order, rows_piece, more=(), gains=None):
    rows = grads[0].shape[0]
    last = gains is not None
    given = [*grads, *more]
    outs = [shape((rows, HD), F32)] + ([shape((1, HD), F32)] if last else [])
    return pl.pallas_call(
        functools.partial(input_grad_kernel, order, rows_piece, len(grads), last),
        in_specs=[IN_SMEM] + [IN_HBM] * (len(arrays) + len(given)) + ([IN_VMEM] if last else []),
        out_specs=[IN_VMEM] * len(outs),
        out_shape=outs,
        scratch_shapes=fetched(given) + [pltpu.VMEM((HD, HALF), BF), pltpu.SemaphoreType.DMA(())],
        compiler_params=params(),
        name="input_gradient",
    )(me, *arrays, *given, *([gains] if last else []))


def segment_ids(bucket_one, text_one):
    position = jnp.arange(LONG, dtype=jnp.int32)
    slot_index = position // SLOT
    inside = position - slot_index * SLOT
    slot_length = SHORT_PATCH + jnp.where(
        slot_index == 0, text_one[0], jnp.where(slot_index == 1, text_one[1], text_one[2])
    )
    long_valid = position < LONG_PATCH + text_one[0]
    short_valid = inside < slot_length
    return jnp.where(
        bucket_one == 1, jnp.where(long_valid, 0, -1), jnp.where(short_valid, slot_index, -1)
    ).astype(jnp.int32)


def adamw(weight, grad_total, first, second, rate):
    first_new = beta_one * first + (1.0 - beta_one) * grad_total
    second_new = beta_two * second + (1.0 - beta_two) * grad_total * grad_total
    first_hat = first_new / (1.0 - beta_one**STEP)
    second_hat = second_new / (1.0 - beta_two**STEP)
    weight_new = weight - rate * (first_hat / (jnp.sqrt(second_hat) + adam_eps) + decay_rate * weight)
    return (grad_total, first_new, second_new, weight_new)


def heads_first(array):
    rows = array.shape[1]
    return array.reshape(3, rows, 2, 2, 2, 128).transpose(3, 1, 2, 4, 0, 5).reshape(2, rows, HALF)


def heads_back(first, second):
    rows = first.shape[0]
    stacked = jnp.stack((first, second)).reshape(2, rows, 2, 2, 3, 128)
    return stacked.transpose(4, 1, 2, 0, 3, 5).reshape(3, rows, HD)


def gain_block(low_gains, cols):
    return jnp.pad(low_gains.reshape(4, GAIN_COLS), ((0, ROWS_GAIN - 4), (0, cols - GAIN_COLS)))


def local(n_dp, n_narrow, tokens, cotangent, bucket, text_lengths, *weights):
    attn_qkv, attn_out, ffn_in, ffn_out, norm_gains = weights[:5]
    masters, firsts, seconds = weights[:5], weights[5:10], weights[10:]
    run = local_fast if (n_dp, n_narrow) == (16, 2) else local_any
    linear = lax.axis_index("dp") * n_narrow + lax.axis_index("narrow")
    me = linear.astype(jnp.int32)[None]
    own = norm_gains.shape[1]
    low_gains = lax.dynamic_update_slice(jnp.zeros((2, HD), BF), norm_gains.astype(BF), (0, linear * own))
    segments = segment_ids(bucket[0], text_lengths[0])
    valid = (segments >= 0).astype(F32)[:, None]
    masks = mask_operands(segments)
    mixed, input_grad, shares, gain_sums = run(
        me, tokens, cotangent, valid, masks, attn_qkv, attn_out, ffn_in, ffn_out, low_gains
    )
    shares = (*shares, lax.dynamic_slice(gain_sums, (0, linear * own), (2, own)))
    results = [mixed, input_grad]
    for index in range(5):
        results.extend(adamw(masters[index], shares[index], firsts[index], seconds[index], rates[index]))
    return tuple(results)


def local_fast(me, tokens, cotangent, valid, masks, attn_qkv, attn_out, ffn_in, ffn_out, low_gains):
    mask_q, mask_k = masks
    row_d, width = attn_out.shape
    row_f, col_f = ffn_out.shape[0], ffn_in.shape[2]
    low_qkv = attn_qkv.astype(BF).reshape(3, row_d, 2, 2, 128).transpose(2, 1, 3, 0, 4).reshape(2, row_d, PART)
    one = joined(low_qkv[0], gain_block(low_gains, PART))[None]
    two = jnp.concatenate((low_qkv[1], attn_out.astype(BF)), axis=1)[None]
    wide = ffn_in.astype(BF).reshape(1, 2 * row_d, col_f)
    down = ffn_out.astype(BF)[None]
    z_a, z_b, z_c, z_d, core = BY_Z
    p_a, p_b, p_c, p_d, _ = BY_PLANE

    one_in, down_in, two, wide = tie(swap(one, z_a), swap(down, p_a), two, wide)
    one, down = joined(one, one_in), joined(down, down_in)
    one_in, down_in, two, wide = tie(swap(one, z_b), swap(down, p_b), two, wide)
    one, down = joined(one, one_in), joined(down, down_in)
    one_in, two_in, down, wide, valid = tie(swap(one, z_c), swap(two, z_a), down, wide, valid)
    one, two = joined(one, one_in), joined(two, two_in)
    one_more, one_away, two_in, wide, down, mask_q, mask_k = tie(
        swap(one, z_d), swap(one, core), swap(two, z_b), wide, down, mask_q, mask_k
    )
    one_last = swap(one_more, core)
    two = joined(two, two_in)
    one_last, two, cotangent = tie(one_last, two, cotangent)
    two_in = swap(two, z_c)
    wide_in = swap(wide, z_a)
    ones = (one, one_more, one_away, one_last)
    first, normed, normed_t, gains = first_project(me, tokens, ones, BY_Z, row_d)
    first, two_in, wide_in, down = tie(first, two_in, wide_in, down)
    two = joined(two, two_in)
    wide = joined(wide, wide_in)
    two_more = swap(two, z_d)
    wide_in = swap(wide, z_b)
    two_away = swap(two, core)
    att_a, extra_a = attend_forward(first, 0, mask_q, mask_k)
    first, att_a, two_more, two_away, wide_in, down = tie(first, att_a, two_more, two_away, wide_in, down)
    wide = joined(wide, wide_in)
    two_last = swap(two_more, core)
    wide_in = swap(wide, z_c)
    down_in = swap(down, p_c)
    att_b, extra_b = attend_forward(first, 1, mask_q, mask_k)
    normed, att_b, two_last, wide_in, down_in = tie(normed, att_b, two_last, wide_in, down_in)
    wide = joined(wide, wide_in)
    down = joined(down, down_in)
    twos = (two, two_more, two_away, two_last)
    wide_more = swap(wide, z_d)
    wide_away = swap(wide, core)
    down_more = swap(down, p_d)
    second = second_project(me, normed, twos, BY_Z, row_d)
    second, wide_away, down_next = tie(second, wide_away, down)
    att_c, extra_c = attend_forward(second, 0, mask_q, mask_k)
    second, att_c, down_next = tie(second, att_c, down_next)
    down_away = swap(down_next, core)
    att_d, extra_d = attend_forward(second, 1, mask_q, mask_k)
    att_d, down_away, wide_more, down_more = tie(att_d, down_away, wide_more, down_more)
    wide_last = swap(wide_more, core)
    wide_last, down_more = tie(wide_last, down_more)
    wides = (wide, wide_more, wide_away, wide_last)
    attended = (att_a, att_b, att_c, att_d)
    extras = (extra_a, extra_b, extra_c, extra_d)
    down_last = swap(down_more, core)
    active, sloped, inner, hidden, normed_two_t, grad_mixed, g_down = feed_in(
        me, tokens, attended, cotangent, valid, gains, twos, wides, (BY_Z, BY_Z, BY_PLANE), row_d, 2 * col_f,
        (8, row_f, width),
    )
    grad_mixed, g_down, down_last = tie(grad_mixed, g_down, down_last)
    downs = (down, down_more, down_away, down_last)

    def back(half, narrow, start, count, grad_now):
        place = half * 2 + narrow
        return attend_backward(
            (first, second)[half], attended[place], grad_now, extras[place], mask_k, half, narrow, start, count
        )

    d_on = swap(g_down[3], core)
    d_other = swap(g_down[2], core)
    grad_gate, grad_up, g_wide = feed_grad(
        me, active, sloped, grad_mixed, normed_two_t, downs, (BY_Z, BY_PLANE), row_d, (8, 2 * row_d, col_f)
    )
    grad_gate, g_wide, d_on, d_other = tie(grad_gate, g_wide, d_on, d_other)
    d_in = swap(add_low((g_down[1], d_on), 0, 8), p_d)
    w_on = swap(g_wide[3], core)
    w_other = swap(g_wide[2], core)
    mixed, grad_hidden, grad_att, gain_two = feed_out(
        me, inner, grad_gate, grad_up, hidden, grad_mixed, gains, twos, wides, downs, (BY_Z, BY_Z, BY_PLANE), row_d
    )
    grad_att, d_in, w_on, w_other = tie(grad_att, d_in, w_on, w_other)
    w_in = swap(add_low((g_wide[1], w_on), 0, 8), z_d)
    d_parts = [g_down[0], d_other, d_in]
    d_next = swap(add_low(d_parts, 4, 8), p_c)
    back_a = back(0, 0, 0, 2, grad_att)
    grad_att, back_a, d_next = tie(grad_att, back_a, d_next)
    d_parts.append(d_next)
    d_next = swap(add_low(d_parts, 2, 4), p_b)
    back_c = back(0, 1, 0, 2, grad_att)
    normed_t, back_c, w_in, d_next = tie(normed_t, back_c, w_in, d_next)
    d_parts.append(d_next)
    d_next = swap(add_low(d_parts, 1, 2), p_a)
    w_parts = [g_wide[0], w_other, w_in]
    w_next = swap(add_low(w_parts, 4, 8), z_c)
    g_one = weight_grad(me, normed_t, (back_a, back_c), BY_Z, row_d, attended, grad_hidden)
    grad_att, g_one, w_next, d_next = tie(grad_att, g_one, w_next, d_next)
    d_parts.append(d_next)
    w_parts.append(w_next)
    o_on = swap(g_one[3], core)
    o_other = swap(g_one[2], core)
    w_next = swap(add_low(w_parts, 2, 4), z_b)
    back_d = back(1, 0, 0, 1, grad_att)
    grad_att, back_d, o_on, o_other = tie(grad_att, back_d, o_on, o_other)
    o_in = swap(add_low((g_one[1], o_on), 0, 8), z_d)
    back_e = back(1, 0, 1, 1, grad_att)
    grad_att, back_e, w_next, o_in = tie(grad_att, back_e, w_next, o_in)
    w_parts.append(w_next)
    o_parts = [g_one[0], o_other, o_in]
    w_next = swap(add_low(w_parts, 1, 2), z_a)
    o_next = swap(add_low(o_parts, 4, 8), z_c)
    back_f = back(1, 1, 0, 2, grad_att)
    back_f, normed_t, w_next, o_next = tie(back_f, normed_t, w_next, o_next)
    w_parts.append(w_next)
    o_parts.append(o_next)
    o_next = swap(add_low(o_parts, 2, 4), z_b)
    g_two = weight_grad(me, normed_t, (back_d, back_e, back_f), BY_Z, row_d)
    g_two, o_next = tie(g_two, o_next)
    o_parts.append(o_next)
    t_on = swap(g_two[3], core)
    t_other = swap(g_two[2], core)
    tokens, t_on, t_other = tie(tokens, t_on, t_other)
    t_in = swap(add_low((g_two[1], t_on), 0, 8), z_d)
    o_next = swap(add_low(o_parts, 1, 2), z_a)
    (through,) = input_gradient(me, (back_a, back_c), ones, BY_Z, row_d)
    through, t_in, o_next = tie(through, t_in, o_next)
    o_parts.append(o_next)
    t_parts = [g_two[0], t_other, t_in]
    t_next = swap(add_low(t_parts, 4, 8), z_c)
    input_grad, gain_one = input_gradient(
        me, (back_d, back_e, back_f), twos, BY_Z, row_d, (through, tokens, grad_hidden), gains
    )
    gain_one, t_next = tie(gain_one, t_next)
    gain_sums = jnp.concatenate((gain_one, gain_two), axis=0)
    t_parts.append(t_next)
    t_next = swap(add_low(t_parts, 2, 4), z_b)
    gain_in = swap(gain_sums, z_c)
    share_ffin = total(*(part[0] for part in w_parts)).reshape(2, row_d, col_f)
    share_down = total(*(part[0] for part in d_parts))
    t_next, gain_in = tie(t_next, gain_in)
    t_parts.append(t_next)
    gain_sums = gain_sums + gain_in
    t_next = swap(add_low(t_parts, 1, 2), z_a)
    gain_sums = gain_sums + swap(gain_sums, z_b)
    gain_sums = gain_sums + swap(gain_sums, z_a)
    gain_sums = gain_sums + swap(gain_sums, z_d)
    gain_sums = gain_sums + swap(gain_sums, core)
    t_parts.append(t_next)
    share_one = total(*(part[0] for part in o_parts))
    share_two = total(*(part[0] for part in t_parts))
    share_qkv = jnp.stack((share_one[:, :PART], share_two)).reshape(2, row_d, 2, 3, 128)
    share_qkv = share_qkv.transpose(3, 1, 0, 2, 4).reshape(3, row_d, width)
    return mixed, input_grad, (share_qkv, share_one[:, PART:], share_ffin, share_down), gain_sums


def local_any(me, tokens, cotangent, valid, masks, attn_qkv, attn_out, ffn_in, ffn_out, low_gains):
    mask_q, mask_k = masks

    def whole(array, axis):
        wide = lax.all_gather(array.astype(BF), "narrow", axis=axis + 1, tiled=True)
        return lax.all_gather(wide, "dp", axis=axis, tiled=True)

    def own(grad, axis):
        rows = lax.psum_scatter(grad, "dp", scatter_dimension=axis, tiled=True)
        return lax.psum_scatter(rows, "narrow", scatter_dimension=axis + 1, tiled=True).astype(F32)

    halves = heads_first(whole(attn_qkv, 1))
    full_gains = lax.psum(low_gains, AXES)
    full_out = whole(attn_out, 0).reshape(2, 2, 256, HD).transpose(1, 0, 2, 3).reshape(HD, HD)
    full_ffin = whole(ffn_in, 1)
    ff = full_ffin.shape[2]
    ones = (joined(halves[0], gain_block(full_gains, HALF))[None],)
    twos = (jnp.concatenate((halves[1], full_out), axis=1)[None],)
    wides = (full_ffin.reshape(1, 2 * HD, ff),)
    downs = (whole(ffn_out, 0)[None],)
    first, normed, normed_t, gains = first_project(me, tokens, ones, None, HD)
    second = second_project(me, normed, twos, None, HD)
    projected = (first, first, second, second)
    found = [attend_forward(projected[i], i % 2, mask_q, mask_k) for i in range(4)]
    attended = tuple(pair[0] for pair in found)
    active, sloped, inner, hidden, normed_two_t, grad_mixed, g_down = feed_in(
        me, tokens, attended, cotangent, valid, gains, twos, wides, (None,) * 3, HD, ff, (1, ff, HD)
    )
    grad_gate, grad_up, g_wide = feed_grad(
        me, active, sloped, grad_mixed, normed_two_t, downs, (None,) * 2, HD, (1, 2 * HD, ff)
    )
    mixed, grad_hidden, grad_att, gain_two = feed_out(
        me, inner, grad_gate, grad_up, hidden, grad_mixed, gains, twos, wides, downs, (None,) * 3, HD
    )
    grads = [
        attend_backward(projected[i], attended[i], grad_att, found[i][1], mask_k, i // 2, i % 2, 0, 2)
        for i in range(4)
    ]
    g_one = weight_grad(me, normed_t, grads[:2], None, HD, attended, grad_hidden)[0][0]
    g_two = weight_grad(me, normed_t, grads[2:], None, HD)[0][0]
    (through,) = input_gradient(me, grads[:2], ones, None, HD)
    input_grad, gain_one = input_gradient(me, grads[2:], twos, None, HD, (through, tokens, grad_hidden), gains)
    gain_sums = lax.psum(jnp.concatenate((gain_one, gain_two), axis=0), AXES)
    grad_out = g_one[:, HALF:].reshape(2, 2, 256, HD).transpose(1, 0, 2, 3).reshape(HD, HD)
    shares = (
        own(heads_back(g_one[:, :HALF], g_two), 1),
        own(grad_out, 0),
        own(g_wide[0].reshape(2, HD, ff), 1),
        own(g_down[0][0], 0),
    )
    return mixed, input_grad, shares, gain_sums


def solution(mesh):
    rows = P(("dp", "narrow"), None)
    cube = P(None, "dp", "narrow")
    flat = P("dp", "narrow")
    gain = P(None, ("dp", "narrow"))
    weights = (cube, flat, cube, flat, gain)
    in_specs = (rows, rows, P(("dp", "narrow")), rows, *weights, *weights, *weights)
    out_specs = (rows, rows, *(spec for spec in weights for _ in range(4)))
    step = functools.partial(local, mesh.shape["dp"], mesh.shape["narrow"])
    return jax.shard_map(step, mesh=mesh, in_specs=in_specs, out_specs=out_specs, check_vma=False)
```

```python
import functools

import jax
import jax.numpy as jnp
from jax import lax
from jax.experimental import pallas as pl
from jax.experimental.pallas import tpu as pltpu
from jax.sharding import PartitionSpec as P

HEADS = 16
DK = 64
SHORT_PATCH = 256
STEP = 10
HD = 1024
SLOT = 384
LONG = 1152
LONG_PATCH = 1024

norm_eps = 1e-06
score_scale = 0.125
beta_one = 0.9
beta_two = 0.999
adam_eps = 1e-08
decay_rate = 0.01
rates = (0.08, 0.8, 0.08, 0.05, 0.6)

BF = jnp.bfloat16
F32 = jnp.float32
NN = (((1,), (0,)), ((), ()))
NT = (((1,), (1,)), ((), ()))
TN = (((0,), (0,)), ((), ()))
AXES = ("dp", "narrow")
VMEM_BYTES = 60 * 2**20
ROWS_GAIN = 16
GAIN_COLS = 512
PART = 6 * 128
HALF = 2 * PART
FF_BLOCK = 256
QUERY_BLOCK = 384
N_GROUPS = 4
GATHERED = 8
SCATTERED = 4
ROW_PARTS = (slice(0, 512), slice(512, LONG))


def dot(left, right, dims=NN):
    return lax.dot_general(left, right, dims, preferred_element_type=F32)


def params():
    return pltpu.CompilerParams(vmem_limit_bytes=VMEM_BYTES)


def shape(dims, dtype):
    return jax.ShapeDtypeStruct(dims, dtype)


IN_VMEM = pl.BlockSpec(memory_space=pltpu.VMEM)
IN_HBM = pl.BlockSpec(memory_space=pl.ANY)
IN_SMEM = pl.BlockSpec(memory_space=pltpu.SMEM)


BY_Z = (("z2", "z1"), ("z1", "z2"), ("x", "y"), ("y", "x"), ("core", "core"))
BY_PLANE = (("x", "y"), ("y", "x"), ("z2", "z1"), ("z1", "z2"), ("core", "core"))
BIT = {"y": 1, "core": 2, "x": 4, "xy": 5, "z1": 8, "z2": 16}


def partners(kinds):
    return [(me, me ^ BIT[kinds[(me >> 1) & 1]]) for me in range(32)]


def swap(array, kinds):
    return lax.ppermute(array, AXES, partners(kinds))


def owner_of(me, index, order):
    flips = [0, 0]
    for step in range(4):
        if (index >> step) & 1:
            for core in range(2):
                flips[core] ^= BIT[order[step][core]]
    own = me ^ 2 if index >> 4 else me
    device = own ^ jnp.where((own >> 1) & 1 == 1, flips[1], flips[0])
    return device >> 1, device & 1


def tie(*values):
    return lax.optimization_barrier(values)


def total(*parts):
    return sum(part.astype(F32) for part in parts)


def joined(held, arrived):
    return jnp.concatenate((held, arrived), axis=0)


def add_low(parts, low, high):
    return total(*(part[low:high] for part in parts)).astype(BF)


def each_place(me_ref, arrays, order, body):
    if order is None:
        body(arrays[0].at[0], 0, 0)
        return
    me = me_ref[0]
    slots = 32 // len(arrays)
    for index in range(32):
        dp, narrow = owner_of(me, index, order)
        body(arrays[index // slots].at[index % slots], dp, narrow)


def span(start, size, unit):
    if isinstance(start, int):
        return pl.ds(start * size, size)
    return pl.ds(pl.multiple_of(start * size, unit), size)


def head_rows(dp, fast):
    return (dp & 4) * 2 + (dp >> 3) * 4 + (dp & 3) if fast else 0


def load_half(me_ref, arrays, order, rows_piece, weight, sem):
    cols = PART if order else HALF

    def start(source, dp, narrow):
        pltpu.make_async_copy(
            source.at[pl.ds(0, rows_piece), pl.ds(0, cols)],
            weight.at[span(dp, rows_piece, 16), span(narrow, cols, 128)],
            sem,
        ).start()

    each_place(me_ref, arrays, order, start)


def first_project_kernel(order, rows_piece, me_ref, x_ref, *refs):
    n_arrays = GATHERED if order else 1
    arrays = refs[:n_arrays]
    out_ref, normed_ref, normed_t_ref, gains_ref, weight, gain_parts, sem, gain_sem = refs[n_arrays:]
    step = pl.program_id(0)

    @pl.when(step == 0)
    def _():
        slots = 32 // GATHERED if order else 1
        for index in range(n_arrays):
            pltpu.make_async_copy(
                arrays[index].at[:, pl.ds(rows_piece, ROWS_GAIN), pl.ds(0, GAIN_COLS)],
                gain_parts.at[pl.ds(index * slots, slots)],
                gain_sem,
            ).start()
        load_half(me_ref, arrays, order, rows_piece, weight, sem)
        x = x_ref[...].astype(F32)
        scaled = x * lax.rsqrt(jnp.mean(x * x, axis=-1, keepdims=True) + norm_eps)
        pltpu.make_async_copy(gain_parts, gain_parts, gain_sem).wait()
        parts = jnp.sum(gain_parts[...].astype(F32), axis=0)
        one = jnp.concatenate((parts[0:1], parts[1:2]), axis=1)
        gains_ref[...] = jnp.concatenate((one, jnp.concatenate((parts[2:3], parts[3:4]), axis=1)), axis=0)
        low = (scaled * one).astype(BF)
        normed_ref[...] = low
        normed_t_ref[...] = low.T
        pltpu.make_async_copy(weight, weight, sem).wait()

    column = pl.multiple_of(step * PART, PART)
    out_ref[...] = dot(normed_ref[...], weight[:, pl.ds(column, PART)]).astype(BF)


def first_project(me, tokens, arrays, order, rows_piece):
    rows = tokens.shape[0]
    full = lambda dims: pl.BlockSpec(dims, lambda step: (0,) * len(dims))
    return pl.pallas_call(
        functools.partial(first_project_kernel, order, rows_piece),
        grid=(2,),
        in_specs=[IN_SMEM, full((rows, HD))] + [IN_HBM] * len(arrays),
        out_specs=[
            pl.BlockSpec((rows, PART), lambda step: (0, step)),
            full((rows, HD)),
            full((HD, rows)),
            full((2, HD)),
        ],
        out_shape=[shape((rows, HALF), BF), shape((rows, HD), BF), shape((HD, rows), BF), shape((2, HD), F32)],
        scratch_shapes=[
            pltpu.VMEM((HD, HALF), BF),
            pltpu.VMEM((32 if order else 1, ROWS_GAIN, GAIN_COLS), BF),
            pltpu.SemaphoreType.DMA(()),
            pltpu.SemaphoreType.DMA(()),
        ],
        compiler_params=params(),
        name="first_project",
    )(me, tokens, *arrays)


def second_project_kernel(order, rows_piece, me_ref, normed_ref, *refs):
    n_arrays = GATHERED if order else 1
    arrays = refs[:n_arrays]
    out_ref, weight, sem = refs[n_arrays:]
    step = pl.program_id(0)

    @pl.when(step == 0)
    def _():
        load_half(me_ref, arrays, order, rows_piece, weight, sem)
        pltpu.make_async_copy(weight, weight, sem).wait()

    column = pl.multiple_of(step * PART, PART)
    out_ref[...] = dot(normed_ref[...], weight[:, pl.ds(column, PART)]).astype(BF)


def second_project(me, normed, arrays, order, rows_piece):
    rows = normed.shape[0]
    return pl.pallas_call(
        functools.partial(second_project_kernel, order, rows_piece),
        grid=(2,),
        in_specs=[IN_SMEM, pl.BlockSpec((rows, HD), lambda step: (0, 0))] + [IN_HBM] * len(arrays),
        out_specs=pl.BlockSpec((rows, PART), lambda step: (0, step)),
        out_shape=shape((rows, HALF), BF),
        scratch_shapes=[pltpu.VMEM((HD, HALF), BF), pltpu.SemaphoreType.DMA(())],
        compiler_params=params(),
        name="second_project",
    )(me, normed, *arrays)


def three_parts(values):
    first = values.astype(BF)
    rest = values - first.astype(F32)
    second = rest.astype(BF)
    return first, second, (rest - second.astype(F32)).astype(BF)


def mask_operands(segments):
    kind = jnp.arange(64, dtype=jnp.int32)
    mine = segments[None, :] + 1 == kind[:, None]
    query_side = jnp.where(mine, -1e30, 0.0).astype(BF)
    key_side = jnp.where((kind[None, :] < 4) & ~mine.T, 1.0, 0.0).astype(BF)
    return (
        jnp.concatenate((query_side, query_side), axis=0),
        jnp.concatenate((key_side, key_side), axis=1),
    )


def attend_forward_kernel(q_ref, k_ref, v_ref, mask_q_ref, mask_k_ref, out_ref, extra_ref):
    queries_t = (q_ref[...].astype(F32) * score_scale).astype(BF).T
    keys = k_ref[...]
    values_t = v_ref[...].T
    mask_q = mask_q_ref[...]
    mask_k = mask_k_ref[...]
    lane = lax.broadcasted_iota(jnp.int32, (1, 128), 1)
    row = lax.broadcasted_iota(jnp.int32, (64, 1), 0)
    ones = jnp.ones((16, LONG), BF)
    key_sides = (jnp.where(lane < 64, keys, mask_k), jnp.where(lane >= 64, keys, mask_k))
    query_sides = (
        jnp.concatenate((queries_t[0:64], mask_q[64:128]), axis=0),
        jnp.concatenate((mask_q[0:64], queries_t[64:128]), axis=0),
    )
    value_sides = [jnp.concatenate((values_t[64 * head : 64 * head + 64], ones), axis=0) for head in range(2)]
    out_blocks = ([], [])
    log_blocks = ([], [])

    def score(head, start):
        return dot(key_sides[head], query_sides[head][:, start : start + QUERY_BLOCK])

    def finish(head, top, expo):
        both = dot(value_sides[head], expo)
        sums = both[64:65]
        out_blocks[head].append((both[0:64] * (1.0 / sums)).astype(BF))
        log_blocks[head].append(-(top + jnp.log(sums)))

    jobs = [(head, start) for head in range(2) for start in range(0, LONG, QUERY_BLOCK)]
    scores = score(*jobs[0])
    waiting = None
    for index, job in enumerate(jobs):
        later = score(*jobs[index + 1]) if index + 1 < len(jobs) else None
        top = jnp.max(scores, axis=0, keepdims=True)
        expo = jnp.exp(scores - top).astype(BF)
        if waiting is not None:
            finish(*waiting)
        waiting = (job[0], top, expo)
        scores = later
    finish(*waiting)
    outs = [jnp.concatenate(blocks, axis=1) for blocks in out_blocks]
    extras = []
    for head in range(2):
        extra = mask_q[0:64].astype(F32)
        for index, part in enumerate(three_parts(jnp.concatenate(log_blocks[head], axis=1))):
            extra = jnp.where(row == 4 + index, part.astype(F32), extra)
        extras.append(extra.astype(BF))
    out_ref[...] = jnp.concatenate(outs, axis=0).T
    extra_ref[...] = jnp.concatenate((extras[1], extras[0]), axis=0).T


def tile_specs(rows, narrow, first):
    return [pl.BlockSpec((rows, 128), lambda i, c=c: (0, narrow * 6 + (first + i) * 3 + c)) for c in range(3)]


def attend_forward(projected, narrow, mask_q, mask_k):
    rows = projected.shape[0]
    tile = pl.BlockSpec((rows, 128), lambda i: (0, i))
    return pl.pallas_call(
        attend_forward_kernel,
        grid=(2,),
        in_specs=tile_specs(rows, narrow, 0)
        + [pl.BlockSpec((128, rows), lambda i: (0, 0)), pl.BlockSpec((rows, 128), lambda i: (0, 0))],
        out_specs=[tile, tile],
        out_shape=[shape((rows, 256), BF), shape((rows, 256), BF)],
        compiler_params=params(),
        name="attend_forward",
    )(projected, projected, projected, mask_q, mask_k)


def attend_backward_kernel(
    q_ref, k_ref, v_ref, out_ref, grad_ref, extra_ref, mask_k_ref, result_ref
):
    queries = (q_ref[...].astype(F32) * score_scale).astype(BF)
    queries_t = queries.T
    keys = k_ref[...]
    keys_t = keys.T
    values_t = v_ref[...].T
    grad = grad_ref[...]
    grad_t = grad.T
    extra = extra_ref[...]
    mask_k_t = mask_k_ref[...].T
    lane = lax.broadcasted_iota(jnp.int32, (1, 128), 1)
    row = lax.broadcasted_iota(jnp.int32, (64, 1), 0)
    product_t = (grad.astype(F32) * out_ref[...].astype(F32)).T
    inner = []
    for head in (1, 0):
        total = -jnp.sum(product_t[64 * head : 64 * head + 64], axis=0, keepdims=True)
        rows = jnp.zeros((64, LONG), F32)
        for index, part in enumerate(three_parts(total)):
            rows = jnp.where(row == index, part.astype(F32), rows)
        inner.append(rows.astype(BF))
    inner_cols = jnp.concatenate(inner, axis=0).T
    key_extra = jnp.where((row >= 4) & (row < 7), 1.0, mask_k_t[0:64].astype(F32)).astype(BF)
    value_extra = jnp.broadcast_to(jnp.where(row < 3, 1.0, 0.0).astype(BF), (64, LONG))
    grad_q = []
    grad_k = []
    grad_v = []
    for head in range(2):
        half = slice(64 * head, 64 * head + 64)
        own = (lane < 64) if head == 0 else (lane >= 64)
        query_side = jnp.where(own, queries, extra)
        grad_side = jnp.where(own, grad, inner_cols)
        if head == 0:
            key_side = jnp.concatenate((keys_t[half], key_extra), axis=0)
            value_side = jnp.concatenate((values_t[half], value_extra), axis=0)
        else:
            key_side = jnp.concatenate((key_extra, keys_t[half]), axis=0)
            value_side = jnp.concatenate((value_extra, values_t[half]), axis=0)
        q_blocks = []
        k_total = None
        v_total = None
        for start in range(0, LONG, QUERY_BLOCK):
            block = slice(start, start + QUERY_BLOCK)
            probs = jnp.exp(dot(query_side[block], key_side))
            grad_scores = (probs * dot(grad_side[block], value_side)).astype(BF)
            v_part = dot(grad_t[half, block], probs.astype(BF))
            k_part = dot(queries_t[half, block], grad_scores)
            v_total = v_part if v_total is None else v_total + v_part
            k_total = k_part if k_total is None else k_total + k_part
            q_blocks.append(dot(grad_scores, keys) * score_scale)
        grad_q.append(jnp.concatenate(q_blocks, axis=0))
        grad_k.append(k_total)
        grad_v.append(v_total)
    result_ref[:, 0:128] = jnp.where(lane < 64, grad_q[0], grad_q[1]).astype(BF)
    result_ref[:, 128:256] = jnp.concatenate(grad_k, axis=0).astype(BF).T
    result_ref[:, 256:384] = jnp.concatenate(grad_v, axis=0).astype(BF).T


def attend_backward(projected, attended, grad_attended, extra, mask_k, half, narrow, first, count):
    rows = projected.shape[0]
    own = pl.BlockSpec((rows, 128), lambda i: (0, first + i))
    return pl.pallas_call(
        attend_backward_kernel,
        grid=(count,),
        in_specs=tile_specs(rows, narrow, first)
        + [
            own,
            pl.BlockSpec((rows, 128), lambda i: (0, half * 4 + narrow * 2 + first + i)),
            own,
            pl.BlockSpec((rows, 128), lambda i: (0, 0)),
        ],
        out_specs=pl.BlockSpec((rows, 384), lambda i: (0, i)),
        out_shape=shape((rows, 384 * count), BF),
        compiler_params=params(),
        name="attend_backward",
    )(projected, projected, projected, attended, grad_attended, extra, mask_k)


def one_buffer(dims):
    return pl.BlockSpec(dims, lambda step: (0,) * len(dims), pipeline_mode=pl.Buffered(buffer_count=1))


def load_out(me_ref, arrays, order, rows_piece, w_out, sem):
    cols, at = (GAIN_COLS, PART) if order else (HD, HALF)

    def start(source, dp, narrow):
        pltpu.make_async_copy(
            source.at[pl.ds(0, rows_piece), pl.ds(at, cols)],
            w_out.at[span(head_rows(dp, order is not None), rows_piece, 16), span(narrow, cols, 128)],
            sem,
        ).start()

    each_place(me_ref, arrays, order, start)


def load_wide(me_ref, arrays, orders, targets, sems):
    count = len(arrays) // 2
    for index, target in enumerate(targets):
        order = orders and orders[index]
        cols = target.shape[1] // (2 if order else 1)

        def start(source, dp, narrow, index=index, target=target, cols=cols):
            rows = source.shape[0]
            pltpu.make_async_copy(
                source, target.at[span(dp, rows, 16), span(narrow, cols, 128)], sems[index]
            ).start()

        each_place(me_ref, arrays[index * count : (index + 1) * count], order, start)


def load_wide_by_half(me_ref, arrays, orders, targets, sems):
    whole = targets[0].shape[1]
    count = len(arrays) // 2
    for half in range(2):
        cols = pl.ds(half * (whole // 2), whole // 2)
        for index, target in enumerate(targets):
            if orders is None:
                pltpu.make_async_copy(arrays[index].at[0, :, cols], target.at[:, cols], sems.at[index, half]).start()
                continue

            def start(source, dp, narrow, half=half, index=index, target=target, cols=cols):
                copy = pltpu.make_async_copy(
                    source, target.at[span(dp, source.shape[0], 16), cols], sems.at[index, half]
                )
                pl.when(narrow == half)(copy.start)

            each_place(me_ref, arrays[index * count : (index + 1) * count], orders[index], start)


def wait_half(targets, sems, half):
    whole = targets[0].shape[1]
    for index, target in enumerate(targets):
        part = target.at[:, pl.ds(half * (whole // 2), whole // 2)]
        pltpu.make_async_copy(part, part, sems.at[index, half]).wait()


def load_down(me_ref, arrays, order, w_down, sem):
    rows, cols = arrays[0].shape[1:]

    def start(source, dp, narrow):
        pltpu.make_async_copy(source, w_down.at[span(dp, rows, 16), span(narrow, cols, 128)], sem).start()

    each_place(me_ref, arrays, order, start)


def load_down_by_group(me_ref, arrays, order, w_down, sems):
    rows, cols = arrays[0].shape[1:]
    if order is None:
        rows = rows // N_GROUPS
        for group in range(N_GROUPS):
            part = pl.ds(group * rows, rows)
            pltpu.make_async_copy(arrays[0].at[0, part], w_down.at[part], sems.at[group]).start()
        return

    def start(source, dp, narrow):
        pltpu.make_async_copy(
            source, w_down.at[span(dp, rows, 16), span(narrow, cols, 128)], sems.at[dp >> 2]
        ).start()

    each_place(me_ref, arrays, order, start)


def wait_group(w_down, sems, group):
    rows = w_down.shape[0] // N_GROUPS
    part = w_down.at[pl.ds(group * rows, rows)]
    pltpu.make_async_copy(part, part, sems.at[group]).wait()


def at_step(step, wanted, body):
    pl.when(step == wanted)(body)


def last_step_of(rows):
    return -(-rows // FF_BLOCK) - 1


def all_of(ref, sem):
    pltpu.make_async_copy(ref, ref, sem).wait()


def gelu_parts(gate):
    square = gate * gate
    curve = jnp.tanh(0.7978845608028654 * gate * (1.0 + 0.044715 * square))
    half = 0.5 * (1.0 + curve)
    slope = half + (0.5 * gate) * (1.0 - curve * curve) * (
        0.7978845608028654 + (0.7978845608028654 * 3.0 * 0.044715) * square
    )
    return gate * half, slope


def feed_in_kernel(orders, rows_piece, me_ref, x_ref, att_a, att_b, att_c, att_d, cotangent_ref, valid_ref, gains_ref, *refs):
    square_order, wide_orders, _, _, down_order = orders
    n_arrays = GATHERED if down_order else 1
    square, wide = refs[:n_arrays], refs[n_arrays : 3 * n_arrays]
    refs = refs[3 * n_arrays :]
    n_arrays = SCATTERED if down_order else 1
    active_ref, sloped_ref, inner_ref, hidden_out, normed_t_out, grad_mixed_out = refs[:6]
    grad_down = refs[6 : 6 + n_arrays]
    w_out, w_gate, w_up, w_down, hidden, normed, normed_t, grad_mixed, sem, wide_sems, out_sems, down_sems = refs[6 + n_arrays :]
    step = pl.program_id(0)

    @pl.when(step == 0)
    def _():
        load_out(me_ref, square, square_order, rows_piece, w_out, sem)
        load_wide_by_half(me_ref, wide, wide_orders, (w_gate, w_up), wide_sems)
        gain = gains_ref[1:2]
        all_of(w_out, sem)

        def before(index, carry):
            part = pl.ds(pl.multiple_of(index * QUERY_BLOCK, QUERY_BLOCK), QUERY_BLOCK)
            left = jnp.concatenate([ref[part, :] for ref in (att_a, att_b, att_c, att_d)], axis=1)
            state = x_ref[part, :].astype(F32) + dot(left, w_out[...])
            hidden[part, :] = state
            low = (state * lax.rsqrt(jnp.mean(state * state, axis=-1, keepdims=True) + norm_eps) * gain).astype(BF)
            normed[part, :] = low
            normed_t[:, part] = low.T
            grad_mixed[part, :] = (cotangent_ref[part, :].astype(F32) * valid_ref[part, :]).astype(BF)
            return carry

        lax.fori_loop(0, x_ref.shape[0] // QUERY_BLOCK, before, 0)
        pltpu.make_async_copy(hidden, hidden_out, out_sems.at[0]).start()
        pltpu.make_async_copy(normed_t, normed_t_out, out_sems.at[1]).start()
        pltpu.make_async_copy(grad_mixed, grad_mixed_out, out_sems.at[2]).start()
        wait_half((w_gate, w_up), wide_sems, 0)

    at_step(step, w_gate.shape[1] // 2 // FF_BLOCK, lambda: wait_half((w_gate, w_up), wide_sems, 1))
    cols = pl.ds(pl.multiple_of(step * FF_BLOCK, FF_BLOCK), FF_BLOCK)
    gate_w = w_gate[:, cols]
    up_w = w_up[:, cols]
    found = [(dot(normed[part, :], gate_w), dot(normed[part, :], up_w)) for part in ROW_PARTS]
    down_sum = None
    for part, (gate, upward) in zip(ROW_PARTS, found):
        active, slope = gelu_parts(gate)
        active_ref[part, :] = active.astype(BF)
        sloped_ref[part, :] = (upward * slope).astype(BF)
        inner = (active * upward).astype(BF)
        inner_ref[part, :] = inner
        down_part = dot(inner.T, grad_mixed[part, :])
        down_sum = down_part if down_sum is None else down_sum + down_part
    w_down[cols, :] = down_sum.astype(BF)

    ff = w_down.shape[0]
    for group in range(N_GROUPS):

        def store_group(group=group):
            if down_order is None:
                part = pl.ds(group * (ff // N_GROUPS), ff // N_GROUPS)
                pltpu.make_async_copy(w_down.at[part], grad_down[0].at[0, part], down_sems.at[group]).start()
                return

            def finish(target, dp, narrow):
                rows, width = target.shape

                @pl.when(dp >> 2 == group)
                def _():
                    pltpu.make_async_copy(
                        w_down.at[span(dp, rows, 16), span(narrow, width, 128)], target, down_sems.at[group]
                    ).start()

            each_place(me_ref, grad_down, down_order, finish)

        at_step(step, last_step_of((group + 1) * (ff // N_GROUPS)), store_group)

    @pl.when(step == pl.num_programs(0) - 1)
    def _():
        pltpu.make_async_copy(hidden, hidden_out, out_sems.at[0]).wait()
        pltpu.make_async_copy(normed_t, normed_t_out, out_sems.at[1]).wait()
        pltpu.make_async_copy(grad_mixed, grad_mixed_out, out_sems.at[2]).wait()
        for group in range(N_GROUPS):
            wait_group(w_down, down_sems, group)


def feed_in(me, tokens, attended, cotangent, valid, gains, square, wide, orders, rows_piece, ff, down_shape):
    rows = tokens.shape[0]
    n_arrays = len(square)
    n_grads = SCATTERED if orders[2] else 1
    tile = pl.BlockSpec((rows, FF_BLOCK), lambda step: (0, step))
    outs = pl.pallas_call(
        functools.partial(feed_in_kernel, orders, rows_piece),
        grid=(ff // FF_BLOCK,),
        in_specs=[IN_SMEM]
        + [one_buffer(array.shape) for array in (tokens, *attended, cotangent, valid, gains)]
        + [IN_HBM] * (3 * n_arrays),
        out_specs=[tile] * 3 + [IN_HBM] * (3 + n_grads),
        out_shape=[
            shape((rows, ff), BF),
            shape((rows, ff), BF),
            shape((rows, ff), BF),
            shape((rows, HD), F32),
            shape((HD, rows), BF),
            shape((rows, HD), BF),
        ]
        + [shape(down_shape, BF)] * n_grads,
        scratch_shapes=[
            pltpu.VMEM((HD, HD), BF),
            pltpu.VMEM((HD, ff), BF),
            pltpu.VMEM((HD, ff), BF),
            pltpu.VMEM((ff, HD), BF),
            pltpu.VMEM((rows, HD), F32),
            pltpu.VMEM((rows, HD), BF),
            pltpu.VMEM((HD, rows), BF),
            pltpu.VMEM((rows, HD), BF),
            pltpu.SemaphoreType.DMA(()),
            pltpu.SemaphoreType.DMA((2, 2)),
            pltpu.SemaphoreType.DMA((3,)),
            pltpu.SemaphoreType.DMA((N_GROUPS,)),
        ],
        compiler_params=params(),
        name="feed_in",
    )(me, tokens, *attended, cotangent, valid, gains, *square, *wide)
    return (*outs[:6], outs[6:])


def feed_grad_kernel(orders, rows_piece, me_ref, active_ref, sloped_ref, grad_mixed_ref, normed_t_ref, *refs):
    _, _, down_order, wide_order, _ = orders
    n_arrays = GATHERED if wide_order else 1
    down = refs[:n_arrays]
    grad_gate_ref, grad_up_ref = refs[n_arrays : n_arrays + 2]
    grad_wide = refs[n_arrays + 2 : -5]
    w_down, w_gate, w_up, down_sems, out_sems = refs[-5:]
    step = pl.program_id(0)

    @pl.when(step == 0)
    def _():
        load_down_by_group(me_ref, down, down_order, w_down, down_sems)

    ff = w_down.shape[0]
    for group in range(N_GROUPS):
        at_step(step, group * (ff // N_GROUPS) // FF_BLOCK, lambda group=group: wait_group(w_down, down_sems, group))

    cols = pl.ds(pl.multiple_of(step * FF_BLOCK, FF_BLOCK), FF_BLOCK)
    grad_inner = dot(grad_mixed_ref[...], w_down[cols, :], NT)
    grad_gate = (grad_inner * sloped_ref[...].astype(F32)).astype(BF)
    grad_up = (grad_inner * active_ref[...].astype(F32)).astype(BF)
    grad_gate_ref[...] = grad_gate
    grad_up_ref[...] = grad_up
    w_gate[:, cols] = dot(normed_t_ref[...], grad_gate).astype(BF)
    w_up[:, cols] = dot(normed_t_ref[...], grad_up).astype(BF)

    ends = (ff // 2, ff // 2 + 3 * FF_BLOCK + FF_BLOCK // 2, ff)
    width = ff // 2 if wide_order else ff
    for place, (begin, end) in enumerate(zip((0, *ends), ends)):

        def store(place=place, begin=begin, end=end):
            count = end - begin

            def finish(target, dp, narrow):
                def copies():
                    for index, source in enumerate((w_gate, w_up)):
                        pltpu.make_async_copy(
                            source.at[span(dp, rows_piece, 16), pl.ds(begin, count)],
                            target.at[pl.ds(index * rows_piece, rows_piece), pl.ds(begin % width, count)],
                            out_sems.at[index, place],
                        ).start()

                if wide_order is None:
                    copies()
                else:
                    pl.when(narrow == begin // width)(copies)

            each_place(me_ref, grad_wide, wide_order, finish)

        at_step(step, last_step_of(end), store)

    @pl.when(step == pl.num_programs(0) - 1)
    def _():
        for index, source in enumerate((w_gate, w_up)):
            for place, (begin, end) in enumerate(zip((0, *ends), ends)):
                part = source.at[:, pl.ds(begin, end - begin)]
                pltpu.make_async_copy(part, part, out_sems.at[index, place]).wait()


def feed_grad(me, active, sloped, grad_mixed, normed_t, down, orders, rows_piece, wide_shape):
    rows, ff = active.shape
    n_arrays = len(down)
    n_grads = SCATTERED if orders[2] else 1
    tile = pl.BlockSpec((rows, FF_BLOCK), lambda step: (0, step))
    outs = pl.pallas_call(
        functools.partial(feed_grad_kernel, orders, rows_piece),
        grid=(ff // FF_BLOCK,),
        in_specs=[IN_SMEM, tile, tile, one_buffer((rows, HD)), one_buffer((HD, rows))] + [IN_HBM] * n_arrays,
        out_specs=[tile, tile] + [IN_HBM] * n_grads,
        out_shape=[shape((rows, ff), BF)] * 2 + [shape(wide_shape, BF)] * n_grads,
        scratch_shapes=[
            pltpu.VMEM((ff, HD), BF),
            pltpu.VMEM((HD, ff), BF),
            pltpu.VMEM((HD, ff), BF),
            pltpu.SemaphoreType.DMA((N_GROUPS,)),
            pltpu.SemaphoreType.DMA((2, 3)),
        ],
        compiler_params=params(),
        name="feed_grad",
    )(me, active, sloped, grad_mixed, normed_t, *down)
    return outs[0], outs[1], outs[2:]


def feed_out_kernel(orders, rows_piece, me_ref, inner_ref, grad_gate_ref, grad_up_ref, hidden_ref, grad_mixed_ref, gains_ref, *refs):
    square_order, wide_orders, down_order, _, _ = orders
    n_arrays = GATHERED if down_order else 1
    square, wide, down = refs[:n_arrays], refs[n_arrays : 3 * n_arrays], refs[3 * n_arrays : 4 * n_arrays]
    mixed_ref, grad_hidden_ref, grad_attended_ref, gain_grad_ref = refs[4 * n_arrays : 4 * n_arrays + 4]
    w_out, w_gate, w_up, w_down, sems = refs[4 * n_arrays + 4 :]
    step = pl.program_id(0)

    @pl.when(step == 0)
    def _():
        load_down(me_ref, down, down_order, w_down, sems.at[3])
        load_wide(me_ref, wide, wide_orders, (w_gate, w_up), (sems.at[1], sems.at[2]))
        load_out(me_ref, square, square_order, rows_piece, w_out, sems.at[0])
        gain_grad_ref[...] = jnp.zeros_like(gain_grad_ref)
        all_of(w_down, sems.at[3])

    @pl.when(step < pl.num_programs(0) // 2)
    def _():
        mixed_ref[...] = (hidden_ref[...] + dot(inner_ref[...], w_down[...])).astype(BF)

    @pl.when(step == pl.num_programs(0) // 2)
    def _():
        all_of(w_gate, sems.at[1])
        all_of(w_up, sems.at[2])
        all_of(w_out, sems.at[0])

    @pl.when(step >= pl.num_programs(0) // 2)
    def _():
        state = hidden_ref[...]
        through = dot(grad_gate_ref[...], w_gate[...], NT) + dot(grad_up_ref[...], w_up[...], NT)
        scale = lax.rsqrt(jnp.mean(state * state, axis=-1, keepdims=True) + norm_eps)
        unit = state * scale
        gain_grad_ref[...] += jnp.sum(through * unit, axis=0, keepdims=True)
        through = through * gains_ref[1:2]
        result = grad_mixed_ref[...].astype(F32) + scale * (
            through - unit * jnp.mean(through * unit, axis=-1, keepdims=True)
        )
        grad_hidden_ref[...] = result
        grad_attended_ref[...] = dot(result.astype(BF), w_out[...], NT).astype(BF)


def feed_out(me, inner, grad_gate, grad_up, hidden, grad_mixed, gains, square, wide, down, orders, rows_piece):
    rows, ff = inner.shape
    n_arrays = len(down)
    count = rows // QUERY_BLOCK
    early = lambda cols: pl.BlockSpec((QUERY_BLOCK, cols), lambda step: (jnp.minimum(step, count - 1), 0))
    late = lambda cols: pl.BlockSpec((QUERY_BLOCK, cols), lambda step: (jnp.maximum(step - count, 0), 0))
    both = pl.BlockSpec((QUERY_BLOCK, HD), lambda step: (step % count, 0))
    return pl.pallas_call(
        functools.partial(feed_out_kernel, orders, rows_piece),
        grid=(2 * count,),
        in_specs=[IN_SMEM, early(ff), late(ff), late(ff), both, late(HD), one_buffer((2, HD))]
        + [IN_HBM] * (4 * n_arrays),
        out_specs=[early(HD), late(HD), late(HD), pl.BlockSpec((1, HD), lambda step: (0, 0))],
        out_shape=[shape((rows, HD), BF), shape((rows, HD), F32), shape((rows, HD), BF), shape((1, HD), F32)],
        scratch_shapes=[
            pltpu.VMEM((HD, HD), BF),
            pltpu.VMEM((HD, ff), BF),
            pltpu.VMEM((HD, ff), BF),
            pltpu.VMEM((ff, HD), BF),
            pltpu.SemaphoreType.DMA((4,)),
        ],
        compiler_params=params(),
        name="feed_out",
    )(me, inner, grad_gate, grad_up, hidden, grad_mixed, gains, *square, *wide, *down)


def half_of_grads(refs):
    wide = []
    held = []
    for ref in refs:
        held.append(ref)
        if sum(part.shape[1] for part in held) == PART:
            wide.append(held)
            held = []
    return wide


def fetch(sources, targets, sems):
    copies = [pltpu.make_async_copy(*triple) for triple in zip(sources, targets, sems)]
    for copy in copies:
        copy.start()

    def get(index):
        copies[index].wait()
        return targets[index][...]

    return get


def fetched(arrays):
    return [pltpu.VMEM(array.shape, array.dtype) for array in arrays] + [pltpu.SemaphoreType.DMA((len(arrays),))]


def weight_grad_kernel(order, rows_piece, n_grads, with_out, me_ref, *refs):
    n_arrays = 4 if order else 1
    fast = order is not None
    n_in = 1 + n_grads + (5 if with_out else 0)
    sources, targets, own = refs[:n_in], refs[n_in : n_in + n_arrays], refs[n_in + n_arrays :]
    held, in_sems = own[:n_in], own[n_in]
    weight, sems = own[n_in + 1 : n_in + 3]
    get = fetch(sources, held, [in_sems.at[index] for index in range(n_in)])
    cols = PART if fast else HALF
    left = get(0)
    begin = 1
    for index, group in enumerate(half_of_grads(sources[1 : 1 + n_grads])):
        right = [get(begin + place) for place in range(len(group))]
        begin += len(group)
        right = right[0] if len(right) == 1 else jnp.concatenate(right, axis=1)
        part = pl.ds(index * PART, PART)
        weight[:, part] = dot(left, right).astype(BF)

        def finish(target, dp, narrow, index=index, part=part):
            copy = pltpu.make_async_copy(
                weight.at[span(dp, rows_piece, 16), part],
                target.at[pl.ds(0, rows_piece), pl.ds(0 if fast else index * PART, PART)],
                sems.at[index],
            )
            if fast:
                pl.when(narrow == index)(copy.start)
            else:
                copy.start()

        each_place(me_ref, targets, order, finish)
    if with_out:
        w_out, out_sem = own[n_in + 3 :]
        col_d = GAIN_COLS if fast else HD
        attended = [get(1 + n_grads + index) for index in range(4)]
        branch = get(n_in - 1).astype(BF)
        for index in range(4):
            w_out[index * 256 : (index + 1) * 256, :] = dot(attended[index].T, branch).astype(BF)

        def finish_out(target, dp, narrow):
            pltpu.make_async_copy(
                w_out.at[span(head_rows(dp, fast), rows_piece, 16), span(narrow, col_d, 128)],
                target.at[pl.ds(0, rows_piece), pl.ds(cols, col_d)],
                out_sem,
            ).start()

        each_place(me_ref, targets, order, finish_out)
        all_of(w_out, out_sem)
    for index in range(2):
        part = weight.at[:, pl.ds(index * PART, PART)]
        pltpu.make_async_copy(part, part, sems.at[index]).wait()


def weight_grad(me, normed_t, grads, order, rows_piece, attended=(), grad_hidden=None):
    with_out = grad_hidden is not None
    cols = (PART if order else HALF) + ((GAIN_COLS if order else HD) if with_out else 0)
    outs = [shape((8 if order else 1, rows_piece, cols), BF)] * (4 if order else 1)
    more = [*attended, grad_hidden] if with_out else []
    given = [normed_t, *grads, *more]
    scratch = fetched(given) + [pltpu.VMEM((HD, HALF), BF), pltpu.SemaphoreType.DMA((2,))]
    if with_out:
        scratch += [pltpu.VMEM((HD, HD), BF), pltpu.SemaphoreType.DMA(())]
    return pl.pallas_call(
        functools.partial(weight_grad_kernel, order, rows_piece, len(grads), with_out),
        in_specs=[IN_SMEM] + [IN_HBM] * len(given),
        out_specs=[IN_HBM] * len(outs),
        out_shape=outs,
        scratch_shapes=scratch,
        compiler_params=params(),
        name="weight_grad",
    )(me, *given)


def input_grad_kernel(order, rows_piece, n_grads, last, me_ref, *refs):
    n_arrays = GATHERED if order else 1
    n_in = n_grads + (3 if last else 0)
    arrays, sources = refs[:n_arrays], refs[n_arrays : n_arrays + n_in]
    refs = refs[n_arrays + n_in :]
    if last:
        gains_ref, out_ref, gain_grad_ref = refs[:3]
        refs = refs[3:]
    else:
        out_ref = refs[0]
        refs = refs[1:]
    held, in_sems, weight, sem = refs[:n_in], refs[n_in], refs[n_in + 1], refs[n_in + 2]
    load_half(me_ref, arrays, order, rows_piece, weight, sem)
    get = fetch(sources, held, [in_sems.at[index] for index in range(n_in)])
    left = jnp.concatenate([get(index) for index in range(n_grads)], axis=1)
    all_of(weight, sem)
    if not last:
        out_ref[...] = dot(left, weight[...], NT)
        return
    out_ref[...] = dot(left, weight[...], NT)
    through = get(n_grads) + out_ref[...]
    x = get(n_grads + 1).astype(F32)
    scale = lax.rsqrt(jnp.mean(x * x, axis=-1, keepdims=True) + norm_eps)
    unit = x * scale
    gain_grad_ref[...] = jnp.sum(through * unit, axis=0, keepdims=True)
    through = through * gains_ref[0:1]
    out_ref[...] = get(n_grads + 2) + scale * (through - unit * jnp.mean(through * unit, axis=-1, keepdims=True))


def input_gradient(me, grads, arrays, order, rows_piece, more=(), gains=None):
    rows = grads[0].shape[0]
    last = gains is not None
    given = [*grads, *more]
    outs = [shape((rows, HD), F32)] + ([shape((1, HD), F32)] if last else [])
    return pl.pallas_call(
        functools.partial(input_grad_kernel, order, rows_piece, len(grads), last),
        in_specs=[IN_SMEM] + [IN_HBM] * (len(arrays) + len(given)) + ([IN_VMEM] if last else []),
        out_specs=[IN_VMEM] * len(outs),
        out_shape=outs,
        scratch_shapes=fetched(given) + [pltpu.VMEM((HD, HALF), BF), pltpu.SemaphoreType.DMA(())],
        compiler_params=params(),
        name="input_gradient",
    )(me, *arrays, *given, *([gains] if last else []))


def segment_ids(bucket_one, text_one):
    position = jnp.arange(LONG, dtype=jnp.int32)
    slot_index = position // SLOT
    inside = position - slot_index * SLOT
    slot_length = SHORT_PATCH + jnp.where(
        slot_index == 0, text_one[0], jnp.where(slot_index == 1, text_one[1], text_one[2])
    )
    long_valid = position < LONG_PATCH + text_one[0]
    short_valid = inside < slot_length
    return jnp.where(
        bucket_one == 1, jnp.where(long_valid, 0, -1), jnp.where(short_valid, slot_index, -1)
    ).astype(jnp.int32)


def adamw(weight, grad_total, first, second, rate):
    first_new = beta_one * first + (1.0 - beta_one) * grad_total
    second_new = beta_two * second + (1.0 - beta_two) * grad_total * grad_total
    first_hat = first_new / (1.0 - beta_one**STEP)
    second_hat = second_new / (1.0 - beta_two**STEP)
    weight_new = weight - rate * (first_hat / (jnp.sqrt(second_hat) + adam_eps) + decay_rate * weight)
    return (grad_total, first_new, second_new, weight_new)


def heads_first(array):
    rows = array.shape[1]
    return array.reshape(3, rows, 2, 2, 2, 128).transpose(3, 1, 2, 4, 0, 5).reshape(2, rows, HALF)


def heads_back(first, second):
    rows = first.shape[0]
    stacked = jnp.stack((first, second)).reshape(2, rows, 2, 2, 3, 128)
    return stacked.transpose(4, 1, 2, 0, 3, 5).reshape(3, rows, HD)


def gain_block(low_gains, cols):
    return jnp.pad(low_gains.reshape(4, GAIN_COLS), ((0, ROWS_GAIN - 4), (0, cols - GAIN_COLS)))


def local(n_dp, n_narrow, tokens, cotangent, bucket, text_lengths, *weights):
    attn_qkv, attn_out, ffn_in, ffn_out, norm_gains = weights[:5]
    masters, firsts, seconds = weights[:5], weights[5:10], weights[10:]
    run = local_fast if (n_dp, n_narrow) == (16, 2) else local_any
    linear = lax.axis_index("dp") * n_narrow + lax.axis_index("narrow")
    me = linear.astype(jnp.int32)[None]
    own = norm_gains.shape[1]
    low_gains = lax.dynamic_update_slice(jnp.zeros((2, HD), BF), norm_gains.astype(BF), (0, linear * own))
    segments = segment_ids(bucket[0], text_lengths[0])
    valid = (segments >= 0).astype(F32)[:, None]
    masks = mask_operands(segments)
    mixed, input_grad, shares, gain_sums = run(
        me, tokens, cotangent, valid, masks, attn_qkv, attn_out, ffn_in, ffn_out, low_gains
    )
    shares = (*shares, lax.dynamic_slice(gain_sums, (0, linear * own), (2, own)))
    results = [mixed, input_grad]
    for index in range(5):
        results.extend(adamw(masters[index], shares[index], firsts[index], seconds[index], rates[index]))
    return tuple(results)


def local_fast(me, tokens, cotangent, valid, masks, attn_qkv, attn_out, ffn_in, ffn_out, low_gains):
    mask_q, mask_k = masks
    row_d, width = attn_out.shape
    row_f, col_f = ffn_out.shape[0], ffn_in.shape[2]
    low_qkv = attn_qkv.astype(BF).reshape(3, row_d, 2, 2, 128).transpose(2, 1, 3, 0, 4).reshape(2, row_d, PART)
    one = joined(low_qkv[0], gain_block(low_gains, PART))[None]
    two = jnp.concatenate((low_qkv[1], attn_out.astype(BF)), axis=1)[None]
    gate = ffn_in[0].astype(BF)[None]
    up = ffn_in[1].astype(BF)[None]
    down = ffn_out.astype(BF)[None]
    z_a, z_b, z_c, z_d, core = BY_Z
    p_a, p_b, p_c, p_d, _ = BY_PLANE

    one_in, gate_in, two, up = tie(swap(one, z_a), swap(gate, p_a), two, up)
    one, gate = joined(one, one_in), joined(gate, gate_in)
    one_in, gate_in, two, up = tie(swap(one, z_b), swap(gate, p_b), two, up)
    one, gate = joined(one, one_in), joined(gate, gate_in)
    one_c, one_d, one_x, two_in, gate, up, valid = tie(
        swap(one, z_c), swap(one, z_d), swap(one, core), swap(two, z_a), gate, up, valid
    )
    two = joined(two, two_in)
    two_in = swap(two, z_b)
    one_cd, one_cx, one_dx, up, gate, mask_q, mask_k = tie(
        swap(one_c, z_d), swap(one_c, core), swap(one_d, core), up, gate, mask_q, mask_k
    )
    one_cdx, two_in, up, gate, cotangent = tie(swap(one_cd, core), two_in, up, gate, cotangent)
    two = joined(two, two_in)
    ones = (one, one_c, one_d, one_cd, one_x, one_cx, one_dx, one_cdx)
    two_c = swap(two, z_c)
    up_in = swap(up, z_a)
    two_x = swap(two, core)
    gate_x = swap(gate, core)
    first, normed, normed_t, gains = first_project(me, tokens, ones, BY_Z, row_d)
    first, two, two_c, two_x, gate_x, up_in, gate = tie(first, two, two_c, two_x, gate_x, up_in, gate)
    up = joined(up, up_in)
    two_d = swap(two, z_d)
    two_cd = swap(two_c, z_d)
    gate_c = swap(gate, p_c)
    two_cx = swap(two_c, core)
    up_in = swap(up, z_b)
    att_a, extra_a = attend_forward(first, 0, mask_q, mask_k)
    first, att_a, two_d, two_cx, up_in, down = tie(first, att_a, two_d, two_cx, up_in, down)
    up = joined(up, up_in)
    up_c = swap(up, z_c)
    two_dx = swap(two_d, core)
    down_in = swap(down, z_a)
    att_b, extra_b = attend_forward(first, 1, mask_q, mask_k)
    normed, att_b, two_cd, two_dx, up_c, gate_c, down_in, up, gate = tie(
        normed, att_b, two_cd, two_dx, up_c, gate_c, down_in, up, gate
    )
    down = joined(down, down_in)
    up_d = swap(up, z_d)
    gate_d = swap(gate, p_d)
    normed, two_cdx = tie(normed, swap(two_cd, core))
    twos = (two, two_c, two_d, two_cd, two_x, two_cx, two_dx, two_cdx)
    up_x = swap(up, core)
    gate_cx = swap(gate_c, core)
    down_in = swap(down, z_b)
    second = second_project(me, normed, twos, BY_Z, row_d)
    second, up_d, up_x, gate_cx, down_in, up_c, gate_c = tie(second, up_d, up_x, gate_cx, down_in, up_c, gate_c)
    down = joined(down, down_in)
    up_cd = swap(up_c, z_d)
    gate_cd = swap(gate_c, p_d)
    up_cx = swap(up_c, core)
    up_dx = swap(up_d, core)
    att_c, extra_c = attend_forward(second, 0, mask_q, mask_k)
    second, att_c, up_cd, up_cx, up_dx, gate_d, down = tie(second, att_c, up_cd, up_cx, up_dx, gate_d, down)
    up_cdx = swap(up_cd, core)
    gate_dx = swap(gate_d, core)
    down_c = swap(down, z_c)
    down_x = swap(down, core)
    att_d, extra_d = attend_forward(second, 1, mask_q, mask_k)
    att_d, up_cdx, gate_dx, gate_cd, down_c, down_x, down = tie(
        att_d, up_cdx, gate_dx, gate_cd, down_c, down_x, down
    )
    down_d = swap(down, z_d)
    gate_cdx, att_d = tie(swap(gate_cd, core), att_d)
    down_cd = swap(down_c, z_d)
    down_cx = swap(down_c, core)
    gates = (gate, gate_c, gate_d, gate_cd, gate_x, gate_cx, gate_dx, gate_cdx)
    ups = (up, up_c, up_d, up_cd, up_x, up_cx, up_dx, up_cdx)
    wides = (*gates, *ups)
    attended = (att_a, att_b, att_c, att_d)
    extras = (extra_a, extra_b, extra_c, extra_d)
    orders = (BY_Z, (BY_PLANE, BY_Z), BY_Z, BY_Z, BY_PLANE)
    active, sloped, inner, hidden, normed_two_t, grad_mixed, g_down = feed_in(
        me, tokens, attended, cotangent, valid, gains, twos, wides, orders, row_d, 2 * col_f, (8, row_f, width)
    )
    grad_mixed, g_down, down_d, down_cd, down_cx = tie(grad_mixed, g_down, down_d, down_cd, down_cx)
    down_dx = swap(down_d, core)
    down_cdx = swap(down_cd, core)
    d_on = swap(g_down[3], core)
    d_other = swap(g_down[2], core)
    grad_mixed, down_dx, down_cdx = tie(grad_mixed, down_dx, down_cdx)
    downs = (down, down_c, down_d, down_cd, down_x, down_cx, down_dx, down_cdx)

    def back(half, narrow, grad_now):
        place = half * 2 + narrow
        return attend_backward(
            (first, second)[half], attended[place], grad_now, extras[place], mask_k, half, narrow, 0, 2
        )

    grad_gate, grad_up, g_wide = feed_grad(
        me, active, sloped, grad_mixed, normed_two_t, downs, orders, row_d, (8, 2 * row_d, col_f)
    )
    grad_gate, g_wide, d_on, d_other = tie(grad_gate, g_wide, d_on, d_other)
    d_in = swap(add_low((g_down[1], d_on), 0, 8), p_d)
    w_on = swap(g_wide[3], core)
    w_other = swap(g_wide[2], core)
    mixed, grad_hidden, grad_att, gain_two = feed_out(
        me, inner, grad_gate, grad_up, hidden, grad_mixed, gains, twos, wides, downs, orders, row_d
    )
    grad_att, d_in, w_on, w_other = tie(grad_att, d_in, w_on, w_other)
    w_in = swap(add_low((g_wide[1], w_on), 0, 8), z_d)
    d_parts = [g_down[0], d_other, d_in]
    d_next = swap(add_low(d_parts, 4, 8), p_c)
    back_a = back(0, 0, grad_att)
    grad_att, back_a, d_next = tie(grad_att, back_a, d_next)
    d_parts.append(d_next)
    d_next = swap(add_low(d_parts, 2, 4), p_b)
    back_b = back(0, 1, grad_att)
    normed_t, back_b, w_in, d_next = tie(normed_t, back_b, w_in, d_next)
    d_parts.append(d_next)
    d_next = swap(add_low(d_parts, 1, 2), p_a)
    w_parts = [g_wide[0], w_other, w_in]
    w_next = swap(add_low(w_parts, 4, 8), z_c)
    g_one = weight_grad(me, normed_t, (back_a, back_b), BY_Z, row_d, attended, grad_hidden)
    back_a, g_one, d_next = tie(back_a, g_one, d_next)
    d_parts.append(d_next)
    o_on = swap(g_one[3], core)
    o_other = swap(g_one[2], core)
    (through,) = input_gradient(me, (back_a, back_b), ones, BY_Z, row_d)
    grad_att, through, o_on, o_other, w_next = tie(grad_att, through, o_on, o_other, w_next)
    w_parts.append(w_next)
    o_in = swap(add_low((g_one[1], o_on), 0, 8), z_d)
    w_next = swap(add_low(w_parts, 2, 4), z_b)
    back_c = back(1, 0, grad_att)
    grad_att, back_c, w_next, o_in = tie(grad_att, back_c, w_next, o_in)
    w_parts.append(w_next)
    o_parts = [g_one[0], o_other, o_in]
    o_next = swap(add_low(o_parts, 4, 8), z_c)
    w_next = swap(add_low(w_parts, 1, 2), z_a)
    back_d = back(1, 1, grad_att)
    back_d, normed_t, w_next, o_next = tie(back_d, normed_t, w_next, o_next)
    w_parts.append(w_next)
    o_parts.append(o_next)
    o_next = swap(add_low(o_parts, 2, 4), z_b)
    g_two = weight_grad(me, normed_t, (back_c, back_d), BY_Z, row_d)
    g_two, o_next = tie(g_two, o_next)
    o_parts.append(o_next)
    t_on = swap(g_two[3], core)
    t_other = swap(g_two[2], core)
    tokens, t_on, t_other = tie(tokens, t_on, t_other)
    t_in = swap(add_low((g_two[1], t_on), 0, 8), z_d)
    o_next = swap(add_low(o_parts, 1, 2), z_a)
    input_grad, gain_one = input_gradient(
        me, (back_c, back_d), twos, BY_Z, row_d, (through, tokens, grad_hidden), gains
    )
    gain_one, t_in, o_next = tie(gain_one, t_in, o_next)
    o_parts.append(o_next)
    t_parts = [g_two[0], t_other, t_in]
    t_next = swap(add_low(t_parts, 4, 8), z_c)
    gain_sums = jnp.concatenate((gain_one, gain_two), axis=0)
    gain_sums = gain_sums + swap(gain_sums, core)
    gain_in = [swap(gain_sums, (kind, kind)) for kind in ("x", "y", "xy")]
    share_ffin = total(*(part[0] for part in w_parts)).reshape(2, row_d, col_f)
    share_down = total(*(part[0] for part in d_parts))
    t_next, gain_in = tie(t_next, gain_in)
    t_parts.append(t_next)
    t_next = swap(add_low(t_parts, 2, 4), z_b)
    gain_sums = gain_sums + (gain_in[0] + gain_in[1] + gain_in[2])
    gain_in = swap(gain_sums, z_b)
    t_next, gain_in = tie(t_next, gain_in)
    t_parts.append(t_next)
    t_next = swap(add_low(t_parts, 1, 2), z_a)
    gain_sums = gain_sums + gain_in
    gain_sums = gain_sums + swap(gain_sums, z_a)
    t_parts.append(t_next)
    share_one = total(*(part[0] for part in o_parts))
    share_two = total(*(part[0] for part in t_parts))
    share_qkv = jnp.stack((share_one[:, :PART], share_two)).reshape(2, row_d, 2, 3, 128)
    share_qkv = share_qkv.transpose(3, 1, 0, 2, 4).reshape(3, row_d, width)
    return mixed, input_grad, (share_qkv, share_one[:, PART:], share_ffin, share_down), gain_sums


def local_any(me, tokens, cotangent, valid, masks, attn_qkv, attn_out, ffn_in, ffn_out, low_gains):
    mask_q, mask_k = masks

    def whole(array, axis):
        wide = lax.all_gather(array.astype(BF), "narrow", axis=axis + 1, tiled=True)
        return lax.all_gather(wide, "dp", axis=axis, tiled=True)

    def own(grad, axis):
        rows = lax.psum_scatter(grad, "dp", scatter_dimension=axis, tiled=True)
        return lax.psum_scatter(rows, "narrow", scatter_dimension=axis + 1, tiled=True).astype(F32)

    halves = heads_first(whole(attn_qkv, 1))
    full_gains = lax.psum(low_gains, AXES)
    full_out = whole(attn_out, 0).reshape(2, 2, 256, HD).transpose(1, 0, 2, 3).reshape(HD, HD)
    full_ffin = whole(ffn_in, 1)
    ff = full_ffin.shape[2]
    ones = (joined(halves[0], gain_block(full_gains, HALF))[None],)
    twos = (jnp.concatenate((halves[1], full_out), axis=1)[None],)
    wides = (full_ffin[0][None], full_ffin[1][None])
    orders = (None,) * 5
    downs = (whole(ffn_out, 0)[None],)
    first, normed, normed_t, gains = first_project(me, tokens, ones, None, HD)
    second = second_project(me, normed, twos, None, HD)
    projected = (first, first, second, second)
    found = [attend_forward(projected[i], i % 2, mask_q, mask_k) for i in range(4)]
    attended = tuple(pair[0] for pair in found)
    active, sloped, inner, hidden, normed_two_t, grad_mixed, g_down = feed_in(
        me, tokens, attended, cotangent, valid, gains, twos, wides, orders, HD, ff, (1, ff, HD)
    )
    grad_gate, grad_up, g_wide = feed_grad(
        me, active, sloped, grad_mixed, normed_two_t, downs, orders, HD, (1, 2 * HD, ff)
    )
    mixed, grad_hidden, grad_att, gain_two = feed_out(
        me, inner, grad_gate, grad_up, hidden, grad_mixed, gains, twos, wides, downs, orders, HD
    )
    grads = [
        attend_backward(projected[i], attended[i], grad_att, found[i][1], mask_k, i // 2, i % 2, 0, 2)
        for i in range(4)
    ]
    g_one = weight_grad(me, normed_t, grads[:2], None, HD, attended, grad_hidden)[0][0]
    g_two = weight_grad(me, normed_t, grads[2:], None, HD)[0][0]
    (through,) = input_gradient(me, grads[:2], ones, None, HD)
    input_grad, gain_one = input_gradient(me, grads[2:], twos, None, HD, (through, tokens, grad_hidden), gains)
    gain_sums = lax.psum(jnp.concatenate((gain_one, gain_two), axis=0), AXES)
    grad_out = g_one[:, HALF:].reshape(2, 2, 256, HD).transpose(1, 0, 2, 3).reshape(HD, HD)
    shares = (
        own(heads_back(g_one[:, :HALF], g_two), 1),
        own(grad_out, 0),
        own(g_wide[0].reshape(2, HD, ff), 1),
        own(g_down[0][0], 0),
    )
    return mixed, input_grad, shares, gain_sums


def solution(mesh):
    rows = P(("dp", "narrow"), None)
    cube = P(None, "dp", "narrow")
    flat = P("dp", "narrow")
    gain = P(None, ("dp", "narrow"))
    weights = (cube, flat, cube, flat, gain)
    in_specs = (rows, rows, P(("dp", "narrow")), rows, *weights, *weights, *weights)
    out_specs = (rows, rows, *(spec for spec in weights for _ in range(4)))
    step = functools.partial(local, mesh.shape["dp"], mesh.shape["narrow"])
    return jax.shard_map(step, mesh=mesh, in_specs=in_specs, out_specs=out_specs, check_vma=False)
```

```python
import functools

import jax
import jax.numpy as jnp
from jax import lax
from jax.experimental import pallas as pl
from jax.experimental.pallas import tpu as pltpu
from jax.sharding import PartitionSpec as P

HEADS = 16
DK = 64
SHORT_PATCH = 256
STEP = 10
HD = 1024
SLOT = 384
LONG = 1152
LONG_PATCH = 1024

norm_eps = 1e-06
score_scale = 0.125
beta_one = 0.9
beta_two = 0.999
adam_eps = 1e-08
decay_rate = 0.01
rates = (0.08, 0.8, 0.08, 0.05, 0.6)

BF = jnp.bfloat16
F32 = jnp.float32
NN = (((1,), (0,)), ((), ()))
NT = (((1,), (1,)), ((), ()))
TN = (((0,), (0,)), ((), ()))
AXES = ("dp", "narrow")
VMEM_BYTES = 60 * 2**20
ROWS_GAIN = 16
GAIN_COLS = 512
PART = 6 * 128
HALF = 2 * PART
FF_BLOCK = 256
QUERY_BLOCK = 384
N_GROUPS = 4
DOWN_BLOCK = 768
GATHERED = 8
SCATTERED = 4


def dot(left, right, dims=NN):
    return lax.dot_general(left, right, dims, preferred_element_type=F32)


def params():
    return pltpu.CompilerParams(vmem_limit_bytes=VMEM_BYTES)


def shape(dims, dtype):
    return jax.ShapeDtypeStruct(dims, dtype)


IN_VMEM = pl.BlockSpec(memory_space=pltpu.VMEM)
IN_HBM = pl.BlockSpec(memory_space=pl.ANY)
IN_SMEM = pl.BlockSpec(memory_space=pltpu.SMEM)


BY_Z = (("z2", "z1"), ("z1", "z2"), ("x", "y"), ("y", "x"), ("core", "core"))
BY_PLANE = (("x", "y"), ("y", "x"), ("z2", "z1"), ("z1", "z2"), ("core", "core"))
BIT = {"y": 1, "core": 2, "x": 4, "xy": 5, "z1": 8, "z2": 16}


def partners(kinds):
    return [(me, me ^ BIT[kinds[(me >> 1) & 1]]) for me in range(32)]


def swap(array, kinds):
    return lax.ppermute(array, AXES, partners(kinds))


def owner_of(me, index, order):
    flips = [0, 0]
    for step in range(4):
        if (index >> step) & 1:
            for core in range(2):
                flips[core] ^= BIT[order[step][core]]
    own = me ^ 2 if index >> 4 else me
    device = own ^ jnp.where((own >> 1) & 1 == 1, flips[1], flips[0])
    return device >> 1, device & 1


def tie(*values):
    return lax.optimization_barrier(values)


def total(*parts):
    return sum(part.astype(F32) for part in parts)


def joined(held, arrived):
    return jnp.concatenate((held, arrived), axis=0)


def add_low(parts, low, high):
    return total(*(part[low:high] for part in parts)).astype(BF)


def each_place(me_ref, arrays, order, body):
    if order is None:
        body(arrays[0].at[0], 0, 0)
        return
    me = me_ref[0]
    slots = 32 // len(arrays)
    for index in range(32):
        dp, narrow = owner_of(me, index, order)
        body(arrays[index // slots].at[index % slots], dp, narrow)


def span(start, size, unit):
    if isinstance(start, int):
        return pl.ds(start * size, size)
    return pl.ds(pl.multiple_of(start * size, unit), size)


def head_rows(dp, fast):
    return (dp & 4) * 2 + (dp >> 3) * 4 + (dp & 3) if fast else 0


def load_half(me_ref, arrays, order, rows_piece, weight, sem):
    cols = PART if order else HALF

    def start(source, dp, narrow):
        pltpu.make_async_copy(
            source.at[pl.ds(0, rows_piece), pl.ds(0, cols)],
            weight.at[span(dp, rows_piece, 16), span(narrow, cols, 128)],
            sem,
        ).start()

    each_place(me_ref, arrays, order, start)


def first_project_kernel(order, rows_piece, me_ref, x_ref, *refs):
    n_arrays = GATHERED if order else 1
    arrays = refs[:n_arrays]
    out_ref, normed_ref, normed_t_ref, gains_ref, weight, gain_parts, sem, gain_sem = refs[n_arrays:]
    step = pl.program_id(0)

    @pl.when(step == 0)
    def _():
        slots = 32 // GATHERED if order else 1
        for index in range(n_arrays):
            pltpu.make_async_copy(
                arrays[index].at[:, pl.ds(rows_piece, ROWS_GAIN), pl.ds(0, GAIN_COLS)],
                gain_parts.at[pl.ds(index * slots, slots)],
                gain_sem,
            ).start()
        load_half(me_ref, arrays, order, rows_piece, weight, sem)
        x = x_ref[...].astype(F32)
        scaled = x * lax.rsqrt(jnp.mean(x * x, axis=-1, keepdims=True) + norm_eps)
        pltpu.make_async_copy(gain_parts, gain_parts, gain_sem).wait()
        parts = jnp.sum(gain_parts[...].astype(F32), axis=0)
        one = jnp.concatenate((parts[0:1], parts[1:2]), axis=1)
        gains_ref[...] = jnp.concatenate((one, jnp.concatenate((parts[2:3], parts[3:4]), axis=1)), axis=0)
        low = (scaled * one).astype(BF)
        normed_ref[...] = low
        normed_t_ref[...] = low.T
        pltpu.make_async_copy(weight, weight, sem).wait()

    column = pl.multiple_of(step * PART, PART)
    out_ref[...] = dot(normed_ref[...], weight[:, pl.ds(column, PART)]).astype(BF)


def first_project(me, tokens, arrays, order, rows_piece):
    rows = tokens.shape[0]
    full = lambda dims: pl.BlockSpec(dims, lambda step: (0,) * len(dims))
    return pl.pallas_call(
        functools.partial(first_project_kernel, order, rows_piece),
        grid=(2,),
        in_specs=[IN_SMEM, full((rows, HD))] + [IN_HBM] * len(arrays),
        out_specs=[
            pl.BlockSpec((rows, PART), lambda step: (0, step)),
            full((rows, HD)),
            full((HD, rows)),
            full((2, HD)),
        ],
        out_shape=[shape((rows, HALF), BF), shape((rows, HD), BF), shape((HD, rows), BF), shape((2, HD), F32)],
        scratch_shapes=[
            pltpu.VMEM((HD, HALF), BF),
            pltpu.VMEM((32 if order else 1, ROWS_GAIN, GAIN_COLS), BF),
            pltpu.SemaphoreType.DMA(()),
            pltpu.SemaphoreType.DMA(()),
        ],
        compiler_params=params(),
        name="first_project",
    )(me, tokens, *arrays)


def second_project_kernel(order, rows_piece, me_ref, normed_ref, *refs):
    n_arrays = GATHERED if order else 1
    arrays = refs[:n_arrays]
    out_ref, weight, sem = refs[n_arrays:]
    step = pl.program_id(0)

    @pl.when(step == 0)
    def _():
        load_half(me_ref, arrays, order, rows_piece, weight, sem)
        pltpu.make_async_copy(weight, weight, sem).wait()

    column = pl.multiple_of(step * PART, PART)
    out_ref[...] = dot(normed_ref[...], weight[:, pl.ds(column, PART)]).astype(BF)


def second_project(me, normed, arrays, order, rows_piece):
    rows = normed.shape[0]
    return pl.pallas_call(
        functools.partial(second_project_kernel, order, rows_piece),
        grid=(2,),
        in_specs=[IN_SMEM, pl.BlockSpec((rows, HD), lambda step: (0, 0))] + [IN_HBM] * len(arrays),
        out_specs=pl.BlockSpec((rows, PART), lambda step: (0, step)),
        out_shape=shape((rows, HALF), BF),
        scratch_shapes=[pltpu.VMEM((HD, HALF), BF), pltpu.SemaphoreType.DMA(())],
        compiler_params=params(),
        name="second_project",
    )(me, normed, *arrays)


def three_parts(values):
    first = values.astype(BF)
    rest = values - first.astype(F32)
    second = rest.astype(BF)
    return first, second, (rest - second.astype(F32)).astype(BF)


def mask_operands(segments):
    kind = jnp.arange(64, dtype=jnp.int32)
    mine = segments[None, :] + 1 == kind[:, None]
    query_side = jnp.where(mine, -1e30, 0.0).astype(BF)
    key_side = jnp.where((kind[None, :] < 4) & ~mine.T, 1.0, 0.0).astype(BF)
    return (
        jnp.concatenate((query_side, query_side), axis=0),
        jnp.concatenate((key_side, key_side), axis=1),
    )


def attend_forward_kernel(q_ref, k_ref, v_ref, mask_q_ref, mask_k_ref, out_ref, extra_ref):
    queries_t = (q_ref[...].astype(F32) * score_scale).astype(BF).T
    keys = k_ref[...]
    values_t = v_ref[...].T
    mask_q = mask_q_ref[...]
    mask_k = mask_k_ref[...]
    lane = lax.broadcasted_iota(jnp.int32, (1, 128), 1)
    row = lax.broadcasted_iota(jnp.int32, (64, 1), 0)
    ones = jnp.ones((16, LONG), BF)
    key_sides = (jnp.where(lane < 64, keys, mask_k), jnp.where(lane >= 64, keys, mask_k))
    query_sides = (
        jnp.concatenate((queries_t[0:64], mask_q[64:128]), axis=0),
        jnp.concatenate((mask_q[0:64], queries_t[64:128]), axis=0),
    )
    value_sides = [jnp.concatenate((values_t[64 * head : 64 * head + 64], ones), axis=0) for head in range(2)]
    out_blocks = ([], [])
    log_blocks = ([], [])

    def score(head, start):
        return dot(key_sides[head], query_sides[head][:, start : start + QUERY_BLOCK])

    def finish(head, top, expo):
        both = dot(value_sides[head], expo)
        sums = both[64:65]
        out_blocks[head].append((both[0:64] * (1.0 / sums)).astype(BF))
        log_blocks[head].append(-(top + jnp.log(sums)))

    jobs = [(head, start) for head in range(2) for start in range(0, LONG, QUERY_BLOCK)]
    scores = score(*jobs[0])
    waiting = None
    for index, job in enumerate(jobs):
        later = score(*jobs[index + 1]) if index + 1 < len(jobs) else None
        top = jnp.max(scores, axis=0, keepdims=True)
        expo = jnp.exp(scores - top).astype(BF)
        if waiting is not None:
            finish(*waiting)
        waiting = (job[0], top, expo)
        scores = later
    finish(*waiting)
    outs = [jnp.concatenate(blocks, axis=1) for blocks in out_blocks]
    extras = []
    for head in range(2):
        extra = mask_q[0:64].astype(F32)
        for index, part in enumerate(three_parts(jnp.concatenate(log_blocks[head], axis=1))):
            extra = jnp.where(row == 4 + index, part.astype(F32), extra)
        extras.append(extra.astype(BF))
    out_ref[...] = jnp.concatenate(outs, axis=0).T
    extra_ref[...] = jnp.concatenate((extras[1], extras[0]), axis=0).T


def tile_specs(rows, narrow, first):
    return [pl.BlockSpec((rows, 128), lambda i, c=c: (0, narrow * 6 + (first + i) * 3 + c)) for c in range(3)]


def attend_forward(projected, narrow, mask_q, mask_k):
    rows = projected.shape[0]
    tile = pl.BlockSpec((rows, 128), lambda i: (0, i))
    return pl.pallas_call(
        attend_forward_kernel,
        grid=(2,),
        in_specs=tile_specs(rows, narrow, 0)
        + [pl.BlockSpec((128, rows), lambda i: (0, 0)), pl.BlockSpec((rows, 128), lambda i: (0, 0))],
        out_specs=[tile, tile],
        out_shape=[shape((rows, 256), BF), shape((rows, 256), BF)],
        compiler_params=params(),
        name="attend_forward",
    )(projected, projected, projected, mask_q, mask_k)


def attend_backward_kernel(
    q_ref, k_ref, v_ref, out_ref, grad_ref, extra_ref, mask_k_ref, result_ref
):
    queries = (q_ref[...].astype(F32) * score_scale).astype(BF)
    queries_t = queries.T
    keys = k_ref[...]
    keys_t = keys.T
    values_t = v_ref[...].T
    grad = grad_ref[...]
    grad_t = grad.T
    extra = extra_ref[...]
    mask_k_t = mask_k_ref[...].T
    lane = lax.broadcasted_iota(jnp.int32, (1, 128), 1)
    row = lax.broadcasted_iota(jnp.int32, (64, 1), 0)
    product_t = (grad.astype(F32) * out_ref[...].astype(F32)).T
    inner = []
    for head in (1, 0):
        total = -jnp.sum(product_t[64 * head : 64 * head + 64], axis=0, keepdims=True)
        rows = jnp.zeros((64, LONG), F32)
        for index, part in enumerate(three_parts(total)):
            rows = jnp.where(row == index, part.astype(F32), rows)
        inner.append(rows.astype(BF))
    inner_cols = jnp.concatenate(inner, axis=0).T
    key_extra = jnp.where((row >= 4) & (row < 7), 1.0, mask_k_t[0:64].astype(F32)).astype(BF)
    value_extra = jnp.broadcast_to(jnp.where(row < 3, 1.0, 0.0).astype(BF), (64, LONG))
    grad_q = []
    grad_k = []
    grad_v = []
    for head in range(2):
        half = slice(64 * head, 64 * head + 64)
        own = (lane < 64) if head == 0 else (lane >= 64)
        query_side = jnp.where(own, queries, extra)
        grad_side = jnp.where(own, grad, inner_cols)
        if head == 0:
            key_side = jnp.concatenate((keys_t[half], key_extra), axis=0)
            value_side = jnp.concatenate((values_t[half], value_extra), axis=0)
        else:
            key_side = jnp.concatenate((key_extra, keys_t[half]), axis=0)
            value_side = jnp.concatenate((value_extra, values_t[half]), axis=0)
        q_blocks = []
        k_total = None
        v_total = None
        for start in range(0, LONG, QUERY_BLOCK):
            block = slice(start, start + QUERY_BLOCK)
            probs = jnp.exp(dot(query_side[block], key_side))
            grad_scores = (probs * dot(grad_side[block], value_side)).astype(BF)
            v_part = dot(grad_t[half, block], probs.astype(BF))
            k_part = dot(queries_t[half, block], grad_scores)
            v_total = v_part if v_total is None else v_total + v_part
            k_total = k_part if k_total is None else k_total + k_part
            q_blocks.append(dot(grad_scores, keys) * score_scale)
        grad_q.append(jnp.concatenate(q_blocks, axis=0))
        grad_k.append(k_total)
        grad_v.append(v_total)
    result_ref[:, 0:128] = jnp.where(lane < 64, grad_q[0], grad_q[1]).astype(BF)
    result_ref[:, 128:256] = jnp.concatenate(grad_k, axis=0).astype(BF).T
    result_ref[:, 256:384] = jnp.concatenate(grad_v, axis=0).astype(BF).T


def attend_backward(projected, attended, grad_attended, extra, mask_k, half, narrow, first, count):
    rows = projected.shape[0]
    own = pl.BlockSpec((rows, 128), lambda i: (0, first + i))
    return pl.pallas_call(
        attend_backward_kernel,
        grid=(count,),
        in_specs=tile_specs(rows, narrow, first)
        + [
            own,
            pl.BlockSpec((rows, 128), lambda i: (0, half * 4 + narrow * 2 + first + i)),
            own,
            pl.BlockSpec((rows, 128), lambda i: (0, 0)),
        ],
        out_specs=pl.BlockSpec((rows, 384), lambda i: (0, i)),
        out_shape=shape((rows, 384 * count), BF),
        compiler_params=params(),
        name="attend_backward",
    )(projected, projected, projected, attended, grad_attended, extra, mask_k)


class fetch:
    def __init__(self, sources, targets, sems):
        self.targets = targets
        self.copies = [pltpu.make_async_copy(*triple) for triple in zip(sources, targets, sems)]
        for copy in self.copies:
            copy.start()

    def wait(self, index):
        self.copies[index].wait()

    def __call__(self, index):
        self.wait(index)
        return self.targets[index][...]


def fetched(arrays):
    return [pltpu.VMEM(array.shape, array.dtype) for array in arrays] + [pltpu.SemaphoreType.DMA((len(arrays),))]


def one_buffer(dims):
    return pl.BlockSpec(dims, lambda step: (0,) * len(dims), pipeline_mode=pl.Buffered(buffer_count=1))


def load_out(me_ref, arrays, order, rows_piece, w_out, sem):
    cols, at = (GAIN_COLS, PART) if order else (HD, HALF)

    def start(source, dp, narrow):
        pltpu.make_async_copy(
            source.at[pl.ds(0, rows_piece), pl.ds(at, cols)],
            w_out.at[span(head_rows(dp, order is not None), rows_piece, 16), span(narrow, cols, 128)],
            sem,
        ).start()

    each_place(me_ref, arrays, order, start)


def load_wide(me_ref, arrays, orders, targets, sems):
    count = len(arrays) // 2
    for index, target in enumerate(targets):
        order = orders and orders[index]
        cols = target.shape[1] // (2 if order else 1)

        def start(source, dp, narrow, index=index, target=target, cols=cols):
            rows = source.shape[0]
            pltpu.make_async_copy(
                source, target.at[span(dp, rows, 16), span(narrow, cols, 128)], sems[index]
            ).start()

        each_place(me_ref, arrays[index * count : (index + 1) * count], order, start)


def load_wide_by_half(me_ref, arrays, orders, targets, sems):
    whole = targets[0].shape[1]
    count = len(arrays) // 2
    for half in range(2):
        cols = pl.ds(half * (whole // 2), whole // 2)
        for index, target in enumerate(targets):
            if orders is None:
                pltpu.make_async_copy(arrays[index].at[0, :, cols], target.at[:, cols], sems.at[index, half]).start()
                continue

            def start(source, dp, narrow, half=half, index=index, target=target, cols=cols):
                copy = pltpu.make_async_copy(
                    source, target.at[span(dp, source.shape[0], 16), cols], sems.at[index, half]
                )
                pl.when(narrow == half)(copy.start)

            each_place(me_ref, arrays[index * count : (index + 1) * count], orders[index], start)


def wait_half(targets, sems, half):
    whole = targets[0].shape[1]
    for index, target in enumerate(targets):
        part = target.at[:, pl.ds(half * (whole // 2), whole // 2)]
        pltpu.make_async_copy(part, part, sems.at[index, half]).wait()


def load_down(me_ref, arrays, order, w_down, sem):
    rows, cols = arrays[0].shape[1:]

    def start(source, dp, narrow):
        pltpu.make_async_copy(source, w_down.at[span(dp, rows, 16), span(narrow, cols, 128)], sem).start()

    each_place(me_ref, arrays, order, start)


def load_down_by_group(me_ref, arrays, order, w_down, sems):
    rows, cols = arrays[0].shape[1:]
    if order is None:
        rows = rows // N_GROUPS
        for group in range(N_GROUPS):
            part = pl.ds(group * rows, rows)
            pltpu.make_async_copy(arrays[0].at[0, part], w_down.at[part], sems.at[group]).start()
        return

    def start(source, dp, narrow):
        pltpu.make_async_copy(
            source, w_down.at[span(dp, rows, 16), span(narrow, cols, 128)], sems.at[dp >> 2]
        ).start()

    each_place(me_ref, arrays, order, start)


def wait_group(w_down, sems, group):
    rows = w_down.shape[0] // N_GROUPS
    part = w_down.at[pl.ds(group * rows, rows)]
    pltpu.make_async_copy(part, part, sems.at[group]).wait()


def all_of(ref, sem):
    pltpu.make_async_copy(ref, ref, sem).wait()


def gelu_parts(gate):
    square = gate * gate
    curve = jnp.tanh(gate * (0.7978845608028654 + (0.7978845608028654 * 0.044715) * square))
    half = 0.5 + 0.5 * curve
    active = gate * half
    bend = (2.0 * 0.7978845608028654) + (6.0 * 0.7978845608028654 * 0.044715) * square
    return active, half + active * (1.0 - half) * bend


def feed_in_kernel(orders, rows_piece, me_ref, valid_ref, gains_ref, *refs):
    square_order, wide_orders, _, _, down_order = orders
    given, refs = refs[:6], refs[6:]
    n_arrays = GATHERED if down_order else 1
    square, wide = refs[:n_arrays], refs[n_arrays : 3 * n_arrays]
    refs = refs[3 * n_arrays :]
    active_out, sloped_out, inner_out, hidden_out, normed_t_out, grad_mixed_out = refs[:6]
    n_grads = SCATTERED if down_order else 1
    grad_down = refs[6 : 6 + n_grads]
    w_out, w_gate, w_up, w_down, hidden, normed, normed_t, inner = refs[6 + n_grads : 14 + n_grads]
    stages, sem, wide_sems, out_sems, stage_sems, down_sems, *own = refs[14 + n_grads :]
    att_a, att_b, att_c, att_d, x_ref, grad_mixed, in_sems = own
    ff = w_down.shape[0]
    load_out(me_ref, square, square_order, rows_piece, w_out, sem)
    get = fetch(given, own[:6], [in_sems.at[index] for index in range(6)])
    load_wide_by_half(me_ref, wide, wide_orders, (w_gate, w_up), wide_sems)
    gain = gains_ref[1:2]
    for index in range(6):
        get.wait(index)
    all_of(w_out, sem)

    def row_block(index):
        return pl.ds(pl.multiple_of(index * QUERY_BLOCK, QUERY_BLOCK), QUERY_BLOCK)

    def before(index, carry):
        part = row_block(index)
        left = jnp.concatenate([ref[part, :] for ref in (att_a, att_b, att_c, att_d)], axis=1)
        state = x_ref[part, :].astype(F32) + dot(left, w_out[...])
        hidden[part, :] = state
        low = (state * lax.rsqrt(jnp.mean(state * state, axis=-1, keepdims=True) + norm_eps) * gain).astype(BF)
        normed[part, :] = low
        normed_t[:, part] = low.T
        grad_mixed[part, :] = (grad_mixed[part, :].astype(F32) * valid_ref[part, :]).astype(BF)
        return carry

    blocks = x_ref.shape[0] // QUERY_BLOCK
    lax.fori_loop(0, blocks, before, 0)
    leaving = [
        pltpu.make_async_copy(hidden, hidden_out, out_sems.at[0]),
        pltpu.make_async_copy(normed_t, normed_t_out, out_sems.at[1]),
        pltpu.make_async_copy(grad_mixed, grad_mixed_out, out_sems.at[2]),
    ]
    for copy in leaving:
        copy.start()
    for half in range(2):
        wait_half((w_gate, w_up), wide_sems, half)
    width = ff // 2

    def stage_copy(index, half, which, target):
        return pltpu.make_async_copy(
            stages.at[half, which], target.at[row_block(index), pl.ds(half * width, width)], stage_sems.at[half, which]
        )

    def block(index, carry):
        part = row_block(index)
        left = normed[part, :]
        for half in range(2):
            cols = pl.ds(half * width, width)
            gate = dot(left, w_gate[:, cols])
            upward = dot(left, w_up[:, cols])
            active, slope = gelu_parts(gate)
            inner[part, cols] = (active * upward).astype(BF)

            @pl.when(index > 0)
            def _():
                stage_copy(index, half, 0, active_out).wait()
                stage_copy(index, half, 1, sloped_out).wait()

            stages[half, 0] = active.astype(BF)
            stages[half, 1] = (upward * slope).astype(BF)
            stage_copy(index, half, 0, active_out).start()
            stage_copy(index, half, 1, sloped_out).start()
        return carry

    lax.fori_loop(0, blocks, block, 0)
    leaving.append(pltpu.make_async_copy(inner, inner_out, out_sems.at[3]))
    leaving[-1].start()
    for group in range(N_GROUPS):
        begin, end = group * DOWN_BLOCK, min((group + 1) * DOWN_BLOCK, ff)
        w_down[begin:end, :] = dot(inner[:, begin:end].T, grad_mixed[...]).astype(BF)
        if down_order is None:
            part = pl.ds(group * (ff // N_GROUPS), ff // N_GROUPS)
            pltpu.make_async_copy(w_down.at[part], grad_down[0].at[0, part], down_sems.at[group]).start()
            continue

        def finish(target, dp, narrow, group=group):
            rows, cols = target.shape
            copy = pltpu.make_async_copy(
                w_down.at[span(dp, rows, 16), span(narrow, cols, 128)], target, down_sems.at[group]
            )
            pl.when(dp >> 2 == group)(copy.start)

        each_place(me_ref, grad_down, down_order, finish)
    for half in range(2):
        stage_copy(blocks - 1, half, 0, active_out).wait()
        stage_copy(blocks - 1, half, 1, sloped_out).wait()
    for copy in leaving:
        copy.wait()
    for group in range(N_GROUPS):
        wait_group(w_down, down_sems, group)


def feed_in(me, tokens, attended, cotangent, valid, gains, square, wide, orders, rows_piece, ff, down_shape):
    rows = tokens.shape[0]
    n_grads = SCATTERED if orders[4] else 1
    given = (*attended, tokens, cotangent)
    outs = pl.pallas_call(
        functools.partial(feed_in_kernel, orders, rows_piece),
        in_specs=[IN_SMEM, IN_VMEM, IN_VMEM] + [IN_HBM] * (len(given) + len(square) + len(wide)),
        out_specs=[IN_HBM] * (6 + n_grads),
        out_shape=[
            shape((rows, ff), BF),
            shape((rows, ff), BF),
            shape((rows, ff), BF),
            shape((rows, HD), F32),
            shape((HD, rows), BF),
            shape((rows, HD), BF),
        ]
        + [shape(down_shape, BF)] * n_grads,
        scratch_shapes=[
            pltpu.VMEM((HD, HD), BF),
            pltpu.VMEM((HD, ff), BF),
            pltpu.VMEM((HD, ff), BF),
            pltpu.VMEM((ff, HD), BF),
            pltpu.VMEM((rows, HD), F32),
            pltpu.VMEM((rows, HD), BF),
            pltpu.VMEM((HD, rows), BF),
            pltpu.VMEM((rows, ff), BF),
            pltpu.VMEM((2, 2, QUERY_BLOCK, ff // 2), BF),
            pltpu.SemaphoreType.DMA(()),
            pltpu.SemaphoreType.DMA((2, 2)),
            pltpu.SemaphoreType.DMA((4,)),
            pltpu.SemaphoreType.DMA((2, 2)),
            pltpu.SemaphoreType.DMA((N_GROUPS,)),
        ]
        + fetched(given),
        compiler_params=params(),
        name="feed_in",
    )(me, valid, gains, *given, *square, *wide)
    return (*outs[:6], outs[6:])


def feed_grad_kernel(orders, rows_piece, me_ref, active_ref, sloped_ref, *refs):
    _, _, down_order, wide_order, _ = orders
    given, refs = refs[:2], refs[2:]
    n_arrays = GATHERED if down_order else 1
    down = refs[:n_arrays]
    grad_gate_out, grad_up_out = refs[n_arrays : n_arrays + 2]
    n_grads = SCATTERED if wide_order else 1
    grad_wide = refs[n_arrays + 2 : n_arrays + 2 + n_grads]
    w_down, w_gate, w_up, up_side, gate_side, down_sems, side_sems, leave_sems, out_sems = refs[
        n_arrays + 2 + n_grads : -3
    ]
    grad_mixed, normed_t, in_sems = refs[-3:]
    rows, ff = active_ref.shape
    blocks = rows // QUERY_BLOCK
    parts = [pl.ds(index * QUERY_BLOCK, QUERY_BLOCK) for index in range(blocks)]
    first = pltpu.make_async_copy(given[0], grad_mixed, in_sems.at[0])
    first.start()
    load_down_by_group(me_ref, down, down_order, w_down, down_sems)
    sides = [
        [pltpu.make_async_copy(source.at[part], target.at[part], side_sems.at[which, index]) for index, part in enumerate(parts)]
        for which, (source, target) in enumerate(((active_ref, up_side), (sloped_ref, gate_side)))
    ]
    for index in range(blocks):
        for which in range(2):
            sides[which][index].start()
    last = pltpu.make_async_copy(given[1], normed_t, in_sems.at[1])
    last.start()
    first.wait()
    width = ff // 2
    leaving = []
    for index, part in enumerate(parts):
        left = grad_mixed[part, :]
        sides[0][index].wait()
        sides[1][index].wait()
        for half in range(2):
            if index == 0:
                for group in range(N_GROUPS // 2):
                    wait_group(w_down, down_sems, half * (N_GROUPS // 2) + group)
            cols = pl.ds(half * width, width)
            grad_inner = dot(left, w_down[cols, :], NT)
            gate_side[part, cols] = (grad_inner * gate_side[part, cols].astype(F32)).astype(BF)
            up_side[part, cols] = (grad_inner * up_side[part, cols].astype(F32)).astype(BF)
        for which, (source, target) in enumerate(((gate_side, grad_gate_out), (up_side, grad_up_out))):
            leaving.append(pltpu.make_async_copy(source.at[part], target.at[part], leave_sems.at[which, index]))
            leaving[-1].start()
    last.wait()
    left = normed_t[...]
    ready = (6 * FF_BLOCK, 9 * FF_BLOCK, ff)
    ends = (ff // 2, ff // 2 + 3 * FF_BLOCK + FF_BLOCK // 2, ff)
    piece = ff // 2 if wide_order else ff
    for place, (done, upto, begin, end) in enumerate(zip((0, *ready), ready, (0, *ends), ends)):
        w_gate[:, done:upto] = dot(left, gate_side[:, done:upto]).astype(BF)
        w_up[:, done:upto] = dot(left, up_side[:, done:upto]).astype(BF)

        def finish(target, dp, narrow, place=place, begin=begin, count=end - begin):
            def copies():
                for index, source in enumerate((w_gate, w_up)):
                    pltpu.make_async_copy(
                        source.at[span(dp, rows_piece, 16), pl.ds(begin, count)],
                        target.at[pl.ds(index * rows_piece, rows_piece), pl.ds(begin % piece, count)],
                        out_sems.at[index, place],
                    ).start()

            if wide_order is None:
                copies()
            else:
                pl.when(narrow == begin // piece)(copies)

        each_place(me_ref, grad_wide, wide_order, finish)
    for copy in leaving:
        copy.wait()
    for index, source in enumerate((w_gate, w_up)):
        for place, (begin, end) in enumerate(zip((0, *ends), ends)):
            part = source.at[:, pl.ds(begin, end - begin)]
            pltpu.make_async_copy(part, part, out_sems.at[index, place]).wait()


def feed_grad(me, active, sloped, grad_mixed, normed_t, down, orders, rows_piece, wide_shape):
    rows, ff = active.shape
    n_grads = SCATTERED if orders[3] else 1
    blocks = rows // QUERY_BLOCK
    outs = pl.pallas_call(
        functools.partial(feed_grad_kernel, orders, rows_piece),
        in_specs=[IN_SMEM] + [IN_HBM] * (4 + len(down)),
        out_specs=[IN_HBM] * (2 + n_grads),
        out_shape=[shape((rows, ff), BF)] * 2 + [shape(wide_shape, BF)] * n_grads,
        scratch_shapes=[
            pltpu.VMEM((ff, HD), BF),
            pltpu.VMEM((HD, ff), BF),
            pltpu.VMEM((HD, ff), BF),
            pltpu.VMEM((rows, ff), BF),
            pltpu.VMEM((rows, ff), BF),
            pltpu.SemaphoreType.DMA((N_GROUPS,)),
            pltpu.SemaphoreType.DMA((2, blocks)),
            pltpu.SemaphoreType.DMA((2, blocks)),
            pltpu.SemaphoreType.DMA((2, 3)),
        ]
        + fetched((grad_mixed, normed_t)),
        compiler_params=params(),
        name="feed_grad",
    )(me, active, sloped, grad_mixed, normed_t, *down)
    return outs[0], outs[1], outs[2:]


def feed_out_kernel(orders, rows_piece, me_ref, inner_ref, grad_gate_ref, grad_up_ref, hidden_ref, grad_mixed_ref, gains_ref, *refs):
    square_order, wide_orders, down_order, _, _ = orders
    n_arrays = GATHERED if down_order else 1
    square, wide, down = refs[:n_arrays], refs[n_arrays : 3 * n_arrays], refs[3 * n_arrays : 4 * n_arrays]
    mixed_ref, grad_hidden_ref, grad_attended_ref, gain_grad_ref = refs[4 * n_arrays : 4 * n_arrays + 4]
    w_out, w_gate, w_up, w_down, sems = refs[4 * n_arrays + 4 :]
    step = pl.program_id(0)

    @pl.when(step == 0)
    def _():
        load_down(me_ref, down, down_order, w_down, sems.at[3])
        load_wide(me_ref, wide, wide_orders, (w_gate, w_up), (sems.at[1], sems.at[2]))
        load_out(me_ref, square, square_order, rows_piece, w_out, sems.at[0])
        gain_grad_ref[...] = jnp.zeros_like(gain_grad_ref)
        all_of(w_down, sems.at[3])

    @pl.when(step < pl.num_programs(0) // 2)
    def _():
        mixed_ref[...] = (hidden_ref[...] + dot(inner_ref[...], w_down[...])).astype(BF)

    @pl.when(step == pl.num_programs(0) // 2)
    def _():
        all_of(w_gate, sems.at[1])
        all_of(w_up, sems.at[2])
        all_of(w_out, sems.at[0])

    @pl.when(step >= pl.num_programs(0) // 2)
    def _():
        state = hidden_ref[...]
        through = dot(grad_gate_ref[...], w_gate[...], NT) + dot(grad_up_ref[...], w_up[...], NT)
        scale = lax.rsqrt(jnp.mean(state * state, axis=-1, keepdims=True) + norm_eps)
        unit = state * scale
        gain_grad_ref[...] += jnp.sum(through * unit, axis=0, keepdims=True)
        through = through * gains_ref[1:2]
        result = grad_mixed_ref[...].astype(F32) + scale * (
            through - unit * jnp.mean(through * unit, axis=-1, keepdims=True)
        )
        grad_hidden_ref[...] = result
        grad_attended_ref[...] = dot(result.astype(BF), w_out[...], NT).astype(BF)


def feed_out(me, inner, grad_gate, grad_up, hidden, grad_mixed, gains, square, wide, down, orders, rows_piece):
    rows, ff = inner.shape
    n_arrays = len(down)
    count = rows // QUERY_BLOCK
    early = lambda cols: pl.BlockSpec((QUERY_BLOCK, cols), lambda step: (jnp.minimum(step, count - 1), 0))
    late = lambda cols: pl.BlockSpec((QUERY_BLOCK, cols), lambda step: (jnp.maximum(step - count, 0), 0))
    both = pl.BlockSpec((QUERY_BLOCK, HD), lambda step: (step % count, 0))
    return pl.pallas_call(
        functools.partial(feed_out_kernel, orders, rows_piece),
        grid=(2 * count,),
        in_specs=[IN_SMEM, early(ff), late(ff), late(ff), both, late(HD), one_buffer((2, HD))]
        + [IN_HBM] * (4 * n_arrays),
        out_specs=[early(HD), late(HD), late(HD), pl.BlockSpec((1, HD), lambda step: (0, 0))],
        out_shape=[shape((rows, HD), BF), shape((rows, HD), F32), shape((rows, HD), BF), shape((1, HD), F32)],
        scratch_shapes=[
            pltpu.VMEM((HD, HD), BF),
            pltpu.VMEM((HD, ff), BF),
            pltpu.VMEM((HD, ff), BF),
            pltpu.VMEM((ff, HD), BF),
            pltpu.SemaphoreType.DMA((4,)),
        ],
        compiler_params=params(),
        name="feed_out",
    )(me, inner, grad_gate, grad_up, hidden, grad_mixed, gains, *square, *wide, *down)


def half_of_grads(refs):
    wide = []
    held = []
    for ref in refs:
        held.append(ref)
        if sum(part.shape[1] for part in held) == PART:
            wide.append(held)
            held = []
    return wide


def weight_grad_kernel(order, rows_piece, n_grads, with_out, me_ref, *refs):
    n_arrays = 4 if order else 1
    fast = order is not None
    n_in = 1 + n_grads + (5 if with_out else 0)
    sources, targets, own = refs[:n_in], refs[n_in : n_in + n_arrays], refs[n_in + n_arrays :]
    held, in_sems = own[:n_in], own[n_in]
    weight, sems = own[n_in + 1 : n_in + 3]
    get = fetch(sources, held, [in_sems.at[index] for index in range(n_in)])
    cols = PART if fast else HALF
    left = get(0)
    begin = 1
    for index, group in enumerate(half_of_grads(sources[1 : 1 + n_grads])):
        right = [get(begin + place) for place in range(len(group))]
        begin += len(group)
        right = right[0] if len(right) == 1 else jnp.concatenate(right, axis=1)
        part = pl.ds(index * PART, PART)
        weight[:, part] = dot(left, right).astype(BF)

        def finish(target, dp, narrow, index=index, part=part):
            copy = pltpu.make_async_copy(
                weight.at[span(dp, rows_piece, 16), part],
                target.at[pl.ds(0, rows_piece), pl.ds(0 if fast else index * PART, PART)],
                sems.at[index],
            )
            if fast:
                pl.when(narrow == index)(copy.start)
            else:
                copy.start()

        each_place(me_ref, targets, order, finish)
    if with_out:
        w_out, out_sem = own[n_in + 3 :]
        col_d = GAIN_COLS if fast else HD
        attended = [get(1 + n_grads + index) for index in range(4)]
        branch = get(n_in - 1).astype(BF)
        for index in range(4):
            w_out[index * 256 : (index + 1) * 256, :] = dot(attended[index].T, branch).astype(BF)

        def finish_out(target, dp, narrow):
            pltpu.make_async_copy(
                w_out.at[span(head_rows(dp, fast), rows_piece, 16), span(narrow, col_d, 128)],
                target.at[pl.ds(0, rows_piece), pl.ds(cols, col_d)],
                out_sem,
            ).start()

        each_place(me_ref, targets, order, finish_out)
        all_of(w_out, out_sem)
    for index in range(2):
        part = weight.at[:, pl.ds(index * PART, PART)]
        pltpu.make_async_copy(part, part, sems.at[index]).wait()


def weight_grad(me, normed_t, grads, order, rows_piece, attended=(), grad_hidden=None):
    with_out = grad_hidden is not None
    cols = (PART if order else HALF) + ((GAIN_COLS if order else HD) if with_out else 0)
    outs = [shape((8 if order else 1, rows_piece, cols), BF)] * (4 if order else 1)
    more = [*attended, grad_hidden] if with_out else []
    given = [normed_t, *grads, *more]
    scratch = fetched(given) + [pltpu.VMEM((HD, HALF), BF), pltpu.SemaphoreType.DMA((2,))]
    if with_out:
        scratch += [pltpu.VMEM((HD, HD), BF), pltpu.SemaphoreType.DMA(())]
    return pl.pallas_call(
        functools.partial(weight_grad_kernel, order, rows_piece, len(grads), with_out),
        in_specs=[IN_SMEM] + [IN_HBM] * len(given),
        out_specs=[IN_HBM] * len(outs),
        out_shape=outs,
        scratch_shapes=scratch,
        compiler_params=params(),
        name="weight_grad",
    )(me, *given)


def input_grad_kernel(order, rows_piece, n_grads, last, me_ref, *refs):
    n_arrays = GATHERED if order else 1
    n_in = n_grads + (3 if last else 0)
    arrays, sources = refs[:n_arrays], refs[n_arrays : n_arrays + n_in]
    refs = refs[n_arrays + n_in :]
    if last:
        gains_ref, out_ref, gain_grad_ref = refs[:3]
        refs = refs[3:]
    else:
        out_ref = refs[0]
        refs = refs[1:]
    held, in_sems, weight, sem = refs[:n_in], refs[n_in], refs[n_in + 1], refs[n_in + 2]
    load_half(me_ref, arrays, order, rows_piece, weight, sem)
    get = fetch(sources, held, [in_sems.at[index] for index in range(n_in)])
    left = jnp.concatenate([get(index) for index in range(n_grads)], axis=1)
    all_of(weight, sem)
    if not last:
        out_ref[...] = dot(left, weight[...], NT).astype(BF)
        return
    found, out_sem = refs[n_in + 3 :]
    found[...] = dot(left, weight[...], NT)
    for index in range(3):
        get.wait(n_grads + index)
    through_ref, x_ref, grad_hidden_ref = held[n_grads:]
    gain_grad_ref[...] = jnp.zeros_like(gain_grad_ref)

    def rows(index, carry):
        part = pl.ds(pl.multiple_of(index * QUERY_BLOCK, QUERY_BLOCK), QUERY_BLOCK)
        through = through_ref[part, :].astype(F32) + found[part, :]
        x = x_ref[part, :].astype(F32)
        scale = lax.rsqrt(jnp.mean(x * x, axis=-1, keepdims=True) + norm_eps)
        unit = x * scale
        gain_grad_ref[...] += jnp.sum(through * unit, axis=0, keepdims=True)
        through = through * gains_ref[0:1]
        found[part, :] = grad_hidden_ref[part, :] + scale * (
            through - unit * jnp.mean(through * unit, axis=-1, keepdims=True)
        )
        pltpu.make_async_copy(found.at[part], out_ref.at[part], out_sem).start()
        return carry

    lax.fori_loop(0, found.shape[0] // QUERY_BLOCK, rows, 0)
    pltpu.make_async_copy(found, out_ref, out_sem).wait()


def input_gradient(me, grads, arrays, order, rows_piece, more=(), gains=None):
    rows = grads[0].shape[0]
    last = gains is not None
    given = [*grads, *more]
    outs = [shape((rows, HD), F32), shape((1, HD), F32)] if last else [shape((rows, HD), BF)]
    scratch = fetched(given) + [pltpu.VMEM((HD, HALF), BF), pltpu.SemaphoreType.DMA(())]
    if last:
        scratch += [pltpu.VMEM((rows, HD), F32), pltpu.SemaphoreType.DMA(())]
    return pl.pallas_call(
        functools.partial(input_grad_kernel, order, rows_piece, len(grads), last),
        in_specs=[IN_SMEM] + [IN_HBM] * (len(arrays) + len(given)) + ([IN_VMEM] if last else []),
        out_specs=[IN_HBM, IN_VMEM] if last else [IN_VMEM],
        out_shape=outs,
        scratch_shapes=scratch,
        compiler_params=params(),
        name="input_gradient",
    )(me, *arrays, *given, *([gains] if last else []))


def segment_ids(bucket_one, text_one):
    position = jnp.arange(LONG, dtype=jnp.int32)
    slot_index = position // SLOT
    inside = position - slot_index * SLOT
    slot_length = SHORT_PATCH + jnp.where(
        slot_index == 0, text_one[0], jnp.where(slot_index == 1, text_one[1], text_one[2])
    )
    long_valid = position < LONG_PATCH + text_one[0]
    short_valid = inside < slot_length
    return jnp.where(
        bucket_one == 1, jnp.where(long_valid, 0, -1), jnp.where(short_valid, slot_index, -1)
    ).astype(jnp.int32)


def adamw(weight, grad_total, first, second, rate):
    first_new = beta_one * first + (1.0 - beta_one) * grad_total
    second_new = beta_two * second + (1.0 - beta_two) * grad_total * grad_total
    first_hat = first_new / (1.0 - beta_one**STEP)
    second_hat = second_new / (1.0 - beta_two**STEP)
    weight_new = weight - rate * (first_hat / (jnp.sqrt(second_hat) + adam_eps) + decay_rate * weight)
    return (grad_total, first_new, second_new, weight_new)


def heads_first(array):
    rows = array.shape[1]
    return array.reshape(3, rows, 2, 2, 2, 128).transpose(3, 1, 2, 4, 0, 5).reshape(2, rows, HALF)


def heads_back(first, second):
    rows = first.shape[0]
    stacked = jnp.stack((first, second)).reshape(2, rows, 2, 2, 3, 128)
    return stacked.transpose(4, 1, 2, 0, 3, 5).reshape(3, rows, HD)


def gain_block(low_gains, cols):
    return jnp.pad(low_gains.reshape(4, GAIN_COLS), ((0, ROWS_GAIN - 4), (0, cols - GAIN_COLS)))


def local(n_dp, n_narrow, tokens, cotangent, bucket, text_lengths, *weights):
    attn_qkv, attn_out, ffn_in, ffn_out, norm_gains = weights[:5]
    masters, firsts, seconds = weights[:5], weights[5:10], weights[10:]
    run = local_fast if (n_dp, n_narrow) == (16, 2) else local_any
    linear = lax.axis_index("dp") * n_narrow + lax.axis_index("narrow")
    me = linear.astype(jnp.int32)[None]
    own = norm_gains.shape[1]
    low_gains = lax.dynamic_update_slice(jnp.zeros((2, HD), BF), norm_gains.astype(BF), (0, linear * own))
    segments = segment_ids(bucket[0], text_lengths[0])
    valid = (segments >= 0).astype(F32)[:, None]
    masks = mask_operands(segments)
    mixed, input_grad, shares, gain_sums = run(
        me, tokens, cotangent, valid, masks, attn_qkv, attn_out, ffn_in, ffn_out, low_gains
    )
    shares = (*shares, lax.dynamic_slice(gain_sums, (0, linear * own), (2, own)))
    results = [mixed, input_grad]
    for index in range(5):
        results.extend(adamw(masters[index], shares[index], firsts[index], seconds[index], rates[index]))
    return tuple(results)


def local_fast(me, tokens, cotangent, valid, masks, attn_qkv, attn_out, ffn_in, ffn_out, low_gains):
    mask_q, mask_k = masks
    row_d, width = attn_out.shape
    row_f, col_f = ffn_out.shape[0], ffn_in.shape[2]
    low_qkv = attn_qkv.astype(BF).reshape(3, row_d, 2, 2, 128).transpose(2, 1, 3, 0, 4).reshape(2, row_d, PART)
    one = joined(low_qkv[0], gain_block(low_gains, PART))[None]
    two = jnp.concatenate((low_qkv[1], attn_out.astype(BF)), axis=1)[None]
    gate = ffn_in[0].astype(BF)[None]
    up = ffn_in[1].astype(BF)[None]
    down = ffn_out.astype(BF)[None]
    z_a, z_b, z_c, z_d, core = BY_Z
    p_a, p_b, p_c, p_d, _ = BY_PLANE

    one_in, gate, two, up = tie(swap(one, z_a), gate, two, up)
    one = joined(one, one_in)
    one_in, two_in, gate, up = tie(swap(one, z_b), swap(two, z_a), gate, up)
    one, two = joined(one, one_in), joined(two, two_in)
    one_c, one_d, one_x, two_in, gate, up, valid = tie(
        swap(one, z_c), swap(one, z_d), swap(one, core), swap(two, z_b), gate, up, valid
    )
    two = joined(two, two_in)
    one_cd, one_cx, one_dx, up_in, gate_in, two, mask_q, mask_k = tie(
        swap(one_c, z_d), swap(one_c, core), swap(one_d, core), swap(up, z_a), swap(gate, p_a), two, mask_q, mask_k
    )
    one_cdx, two, up_in, gate_in, cotangent = tie(swap(one_cd, core), two, up_in, gate_in, cotangent)
    ones = (one, one_c, one_d, one_cd, one_x, one_cx, one_dx, one_cdx)
    up, gate = joined(up, up_in), joined(gate, gate_in)
    two_c = swap(two, z_c)
    up_in = swap(up, z_b)
    gate_in = swap(gate, p_b)
    two_x = swap(two, core)
    first, normed, normed_t, gains = first_project(me, tokens, ones, BY_Z, row_d)
    first, two, two_c, two_x, up_in, gate_in = tie(first, two, two_c, two_x, up_in, gate_in)
    up, gate = joined(up, up_in), joined(gate, gate_in)
    two_d = swap(two, z_d)
    two_cd = swap(two_c, z_d)
    gate_c = swap(gate, p_c)
    two_cx = swap(two_c, core)
    att_a, extra_a = attend_forward(first, 0, mask_q, mask_k)
    first, att_a, two_d, two_cx, up, down = tie(first, att_a, two_d, two_cx, up, down)
    gate_x = swap(gate, core)
    up_c = swap(up, z_c)
    two_dx = swap(two_d, core)
    down_in = swap(down, z_a)
    att_b, extra_b = attend_forward(first, 1, mask_q, mask_k)
    normed, att_b, two_cd, two_dx, up_c, gate_c, gate_x, down_in, up, gate = tie(
        normed, att_b, two_cd, two_dx, up_c, gate_c, gate_x, down_in, up, gate
    )
    down = joined(down, down_in)
    up_d = swap(up, z_d)
    gate_d = swap(gate, p_d)
    normed, two_cdx = tie(normed, swap(two_cd, core))
    twos = (two, two_c, two_d, two_cd, two_x, two_cx, two_dx, two_cdx)
    up_x = swap(up, core)
    gate_cx = swap(gate_c, core)
    down_in = swap(down, z_b)
    second = second_project(me, normed, twos, BY_Z, row_d)
    second, up_d, up_x, gate_cx, down_in, up_c, gate_c = tie(second, up_d, up_x, gate_cx, down_in, up_c, gate_c)
    down = joined(down, down_in)
    up_cd = swap(up_c, z_d)
    gate_cd = swap(gate_c, p_d)
    up_cx = swap(up_c, core)
    up_dx = swap(up_d, core)
    att_c, extra_c = attend_forward(second, 0, mask_q, mask_k)
    second, att_c, up_cd, up_cx, up_dx, gate_d, down = tie(second, att_c, up_cd, up_cx, up_dx, gate_d, down)
    up_cdx = swap(up_cd, core)
    gate_dx = swap(gate_d, core)
    down_c = swap(down, z_c)
    down_x = swap(down, core)
    att_d, extra_d = attend_forward(second, 1, mask_q, mask_k)
    att_d, up_cdx, gate_dx, gate_cd, down_c, down_x, down = tie(
        att_d, up_cdx, gate_dx, gate_cd, down_c, down_x, down
    )
    down_d = swap(down, z_d)
    gate_cdx, att_d = tie(swap(gate_cd, core), att_d)
    down_cd = swap(down_c, z_d)
    down_cx = swap(down_c, core)
    gates = (gate, gate_c, gate_d, gate_cd, gate_x, gate_cx, gate_dx, gate_cdx)
    ups = (up, up_c, up_d, up_cd, up_x, up_cx, up_dx, up_cdx)
    wides = (*gates, *ups)
    attended = (att_a, att_b, att_c, att_d)
    extras = (extra_a, extra_b, extra_c, extra_d)
    orders = (BY_Z, (BY_PLANE, BY_Z), BY_Z, BY_Z, BY_PLANE)
    active, sloped, inner, hidden, normed_two_t, grad_mixed, g_down = feed_in(
        me, tokens, attended, cotangent, valid, gains, twos, wides, orders, row_d, 2 * col_f, (8, row_f, width)
    )
    grad_mixed, g_down, down_d, down_cd, down_cx = tie(grad_mixed, g_down, down_d, down_cd, down_cx)
    down_dx = swap(down_d, core)
    down_cdx = swap(down_cd, core)
    d_on = swap(g_down[3], core)
    d_other = swap(g_down[2], core)
    grad_mixed, down_dx, down_cdx = tie(grad_mixed, down_dx, down_cdx)
    downs = (down, down_c, down_d, down_cd, down_x, down_cx, down_dx, down_cdx)

    def back(half, narrow, grad_now):
        place = half * 2 + narrow
        return attend_backward(
            (first, second)[half], attended[place], grad_now, extras[place], mask_k, half, narrow, 0, 2
        )

    grad_gate, grad_up, g_wide = feed_grad(
        me, active, sloped, grad_mixed, normed_two_t, downs, orders, row_d, (8, 2 * row_d, col_f)
    )
    grad_gate, g_wide, d_on, d_other = tie(grad_gate, g_wide, d_on, d_other)
    d_in = swap(add_low((g_down[1], d_on), 0, 8), p_d)
    w_on = swap(g_wide[3], core)
    w_other = swap(g_wide[2], core)
    mixed, grad_hidden, grad_att, gain_two = feed_out(
        me, inner, grad_gate, grad_up, hidden, grad_mixed, gains, twos, wides, downs, orders, row_d
    )
    grad_att, d_in, w_on, w_other = tie(grad_att, d_in, w_on, w_other)
    w_in = swap(add_low((g_wide[1], w_on), 0, 8), z_d)
    d_parts = [g_down[0], d_other, d_in]
    d_next = swap(add_low(d_parts, 4, 8), p_c)
    back_a = back(0, 0, grad_att)
    grad_att, back_a, d_next = tie(grad_att, back_a, d_next)
    d_parts.append(d_next)
    d_next = swap(add_low(d_parts, 2, 4), p_b)
    back_b = back(0, 1, grad_att)
    normed_t, back_b, w_in, d_next = tie(normed_t, back_b, w_in, d_next)
    d_parts.append(d_next)
    d_next = swap(add_low(d_parts, 1, 2), p_a)
    w_parts = [g_wide[0], w_other, w_in]
    w_next = swap(add_low(w_parts, 4, 8), z_c)
    g_one = weight_grad(me, normed_t, (back_a, back_b), BY_Z, row_d, attended, grad_hidden)
    back_a, g_one, d_next = tie(back_a, g_one, d_next)
    d_parts.append(d_next)
    o_on = swap(g_one[3], core)
    o_other = swap(g_one[2], core)
    (through,) = input_gradient(me, (back_a, back_b), ones, BY_Z, row_d)
    grad_att, through, o_on, o_other, w_next = tie(grad_att, through, o_on, o_other, w_next)
    w_parts.append(w_next)
    o_in = swap(add_low((g_one[1], o_on), 0, 8), z_d)
    w_next = swap(add_low(w_parts, 2, 4), z_b)
    back_c = back(1, 0, grad_att)
    grad_att, back_c, w_next, o_in = tie(grad_att, back_c, w_next, o_in)
    w_parts.append(w_next)
    o_parts = [g_one[0], o_other, o_in]
    o_next = swap(add_low(o_parts, 4, 8), z_c)
    w_next = swap(add_low(w_parts, 1, 2), z_a)
    back_d = back(1, 1, grad_att)
    back_d, normed_t, w_next, o_next = tie(back_d, normed_t, w_next, o_next)
    w_parts.append(w_next)
    o_parts.append(o_next)
    o_next = swap(add_low(o_parts, 2, 4), z_b)
    g_two = weight_grad(me, normed_t, (back_c, back_d), BY_Z, row_d)
    g_two, o_next = tie(g_two, o_next)
    o_parts.append(o_next)
    t_on = swap(g_two[3], core)
    t_other = swap(g_two[2], core)
    tokens, t_on, t_other = tie(tokens, t_on, t_other)
    t_in = swap(add_low((g_two[1], t_on), 0, 8), z_d)
    o_next = swap(add_low(o_parts, 1, 2), z_a)
    input_grad, gain_one = input_gradient(
        me, (back_c, back_d), twos, BY_Z, row_d, (through, tokens, grad_hidden), gains
    )
    gain_one, t_in, o_next = tie(gain_one, t_in, o_next)
    o_parts.append(o_next)
    t_parts = [g_two[0], t_other, t_in]
    t_next = swap(add_low(t_parts, 4, 8), z_c)
    gain_sums = jnp.concatenate((gain_one, gain_two), axis=0)
    gain_sums = gain_sums + swap(gain_sums, core)
    gain_in = [swap(gain_sums, (kind, kind)) for kind in ("x", "y", "xy")]
    t_next, gain_in, w_parts, d_parts, o_parts = tie(t_next, gain_in, w_parts, d_parts, o_parts)
    share_ffin = total(*(part[0] for part in w_parts)).reshape(2, row_d, col_f)
    share_down = total(*(part[0] for part in d_parts))
    t_parts.append(t_next)
    t_next = swap(add_low(t_parts, 2, 4), z_b)
    gain_sums = gain_sums + (gain_in[0] + gain_in[1] + gain_in[2])
    gain_in = swap(gain_sums, z_b)
    t_next, gain_in = tie(t_next, gain_in)
    t_parts.append(t_next)
    t_next = swap(add_low(t_parts, 1, 2), z_a)
    gain_sums = gain_sums + gain_in
    gain_sums = gain_sums + swap(gain_sums, z_a)
    t_parts.append(t_next)
    share_one = total(*(part[0] for part in o_parts))
    share_two = total(*(part[0] for part in t_parts))
    share_qkv = jnp.stack((share_one[:, :PART], share_two)).reshape(2, row_d, 2, 3, 128)
    share_qkv = share_qkv.transpose(3, 1, 0, 2, 4).reshape(3, row_d, width)
    return mixed, input_grad, (share_qkv, share_one[:, PART:], share_ffin, share_down), gain_sums


def local_any(me, tokens, cotangent, valid, masks, attn_qkv, attn_out, ffn_in, ffn_out, low_gains):
    mask_q, mask_k = masks

    def whole(array, axis):
        wide = lax.all_gather(array.astype(BF), "narrow", axis=axis + 1, tiled=True)
        return lax.all_gather(wide, "dp", axis=axis, tiled=True)

    def own(grad, axis):
        rows = lax.psum_scatter(grad, "dp", scatter_dimension=axis, tiled=True)
        return lax.psum_scatter(rows, "narrow", scatter_dimension=axis + 1, tiled=True).astype(F32)

    halves = heads_first(whole(attn_qkv, 1))
    full_gains = lax.psum(low_gains, AXES)
    full_out = whole(attn_out, 0).reshape(2, 2, 256, HD).transpose(1, 0, 2, 3).reshape(HD, HD)
    full_ffin = whole(ffn_in, 1)
    ff = full_ffin.shape[2]
    ones = (joined(halves[0], gain_block(full_gains, HALF))[None],)
    twos = (jnp.concatenate((halves[1], full_out), axis=1)[None],)
    wides = (full_ffin[0][None], full_ffin[1][None])
    orders = (None,) * 5
    downs = (whole(ffn_out, 0)[None],)
    first, normed, normed_t, gains = first_project(me, tokens, ones, None, HD)
    second = second_project(me, normed, twos, None, HD)
    projected = (first, first, second, second)
    found = [attend_forward(projected[i], i % 2, mask_q, mask_k) for i in range(4)]
    attended = tuple(pair[0] for pair in found)
    active, sloped, inner, hidden, normed_two_t, grad_mixed, g_down = feed_in(
        me, tokens, attended, cotangent, valid, gains, twos, wides, orders, HD, ff, (1, ff, HD)
    )
    grad_gate, grad_up, g_wide = feed_grad(
        me, active, sloped, grad_mixed, normed_two_t, downs, orders, HD, (1, 2 * HD, ff)
    )
    mixed, grad_hidden, grad_att, gain_two = feed_out(
        me, inner, grad_gate, grad_up, hidden, grad_mixed, gains, twos, wides, downs, orders, HD
    )
    grads = [
        attend_backward(projected[i], attended[i], grad_att, found[i][1], mask_k, i // 2, i % 2, 0, 2)
        for i in range(4)
    ]
    g_one = weight_grad(me, normed_t, grads[:2], None, HD, attended, grad_hidden)[0][0]
    g_two = weight_grad(me, normed_t, grads[2:], None, HD)[0][0]
    (through,) = input_gradient(me, grads[:2], ones, None, HD)
    input_grad, gain_one = input_gradient(me, grads[2:], twos, None, HD, (through, tokens, grad_hidden), gains)
    gain_sums = lax.psum(jnp.concatenate((gain_one, gain_two), axis=0), AXES)
    grad_out = g_one[:, HALF:].reshape(2, 2, 256, HD).transpose(1, 0, 2, 3).reshape(HD, HD)
    shares = (
        own(heads_back(g_one[:, :HALF], g_two), 1),
        own(grad_out, 0),
        own(g_wide[0].reshape(2, HD, ff), 1),
        own(g_down[0][0], 0),
    )
    return mixed, input_grad, shares, gain_sums


def solution(mesh):
    rows = P(("dp", "narrow"), None)
    cube = P(None, "dp", "narrow")
    flat = P("dp", "narrow")
    gain = P(None, ("dp", "narrow"))
    weights = (cube, flat, cube, flat, gain)
    in_specs = (rows, rows, P(("dp", "narrow")), rows, *weights, *weights, *weights)
    out_specs = (rows, rows, *(spec for spec in weights for _ in range(4)))
    step = functools.partial(local, mesh.shape["dp"], mesh.shape["narrow"])
    return jax.shard_map(step, mesh=mesh, in_specs=in_specs, out_specs=out_specs, check_vma=False)
```

```python
import functools

import jax
import jax.numpy as jnp
from jax import lax
from jax.experimental import pallas as pl
from jax.experimental.pallas import tpu as pltpu
from jax.sharding import PartitionSpec as P

HEADS = 16
DK = 64
SHORT_PATCH = 256
STEP = 10
HD = 1024
SLOT = 384
LONG = 1152
LONG_PATCH = 1024

norm_eps = 1e-06
score_scale = 0.125
beta_one = 0.9
beta_two = 0.999
adam_eps = 1e-08
decay_rate = 0.01
rates = (0.08, 0.8, 0.08, 0.05, 0.6)

BF = jnp.bfloat16
F32 = jnp.float32
NN = (((1,), (0,)), ((), ()))
NT = (((1,), (1,)), ((), ()))
TN = (((0,), (0,)), ((), ()))
AXES = ("dp", "narrow")
VMEM_BYTES = 60 * 2**20
ROWS_GAIN = 16
GAIN_COLS = 512
PART = 6 * 128
HALF = 2 * PART
FF_BLOCK = 256
QUERY_BLOCK = 384
N_GROUPS = 4
DOWN_BLOCK = 768
GATHERED = 8
SCATTERED = 4


def dot(left, right, dims=NN):
    return lax.dot_general(left, right, dims, preferred_element_type=F32)


def params():
    return pltpu.CompilerParams(vmem_limit_bytes=VMEM_BYTES)


def shape(dims, dtype):
    return jax.ShapeDtypeStruct(dims, dtype)


IN_VMEM = pl.BlockSpec(memory_space=pltpu.VMEM)
IN_HBM = pl.BlockSpec(memory_space=pl.ANY)
IN_SMEM = pl.BlockSpec(memory_space=pltpu.SMEM)


BY_Z = (("z2", "z1"), ("z1", "z2"), ("x", "y"), ("y", "x"), ("core", "core"))
BY_PLANE = (("x", "y"), ("y", "x"), ("z2", "z1"), ("z1", "z2"), ("core", "core"))
BIT = {"y": 1, "core": 2, "x": 4, "xy": 5, "z1": 8, "z2": 16}


def partners(kinds):
    return [(me, me ^ BIT[kinds[(me >> 1) & 1]]) for me in range(32)]


def swap(array, kinds):
    return lax.ppermute(array, AXES, partners(kinds))


def owner_of(me, index, order):
    flips = [0, 0]
    for step in range(4):
        if (index >> step) & 1:
            for core in range(2):
                flips[core] ^= BIT[order[step][core]]
    own = me ^ 2 if index >> 4 else me
    device = own ^ jnp.where((own >> 1) & 1 == 1, flips[1], flips[0])
    return device >> 1, device & 1


def tie(*values):
    return lax.optimization_barrier(values)


def total(*parts):
    return sum(part.astype(F32) for part in parts)


def joined(held, arrived):
    return jnp.concatenate((held, arrived), axis=0)


def add_low(parts, low, high):
    return total(*(part[low:high] for part in parts)).astype(BF)


def each_place(me_ref, arrays, order, body):
    if order is None:
        body(arrays[0].at[0], 0, 0)
        return
    me = me_ref[0]
    slots = 32 // len(arrays)
    for index in range(32):
        dp, narrow = owner_of(me, index, order)
        body(arrays[index // slots].at[index % slots], dp, narrow)


def span(start, size, unit):
    if isinstance(start, int):
        return pl.ds(start * size, size)
    return pl.ds(pl.multiple_of(start * size, unit), size)


def head_rows(dp, fast):
    return (dp & 4) * 2 + (dp >> 3) * 4 + (dp & 3) if fast else 0


def load_half(me_ref, arrays, order, rows_piece, weight, sem):
    cols = PART if order else HALF

    def start(source, dp, narrow):
        pltpu.make_async_copy(
            source.at[pl.ds(0, rows_piece), pl.ds(0, cols)],
            weight.at[span(dp, rows_piece, 16), span(narrow, cols, 128)],
            sem,
        ).start()

    each_place(me_ref, arrays, order, start)


def first_project_kernel(order, rows_piece, me_ref, x_ref, *refs):
    n_arrays = GATHERED if order else 1
    arrays = refs[:n_arrays]
    out_ref, normed_ref, normed_t_ref, gains_ref, weight, gain_parts, sem, gain_sem = refs[n_arrays:]
    step = pl.program_id(0)

    @pl.when(step == 0)
    def _():
        slots = 32 // GATHERED if order else 1
        for index in range(n_arrays):
            pltpu.make_async_copy(
                arrays[index].at[:, pl.ds(rows_piece, ROWS_GAIN), pl.ds(0, GAIN_COLS)],
                gain_parts.at[pl.ds(index * slots, slots)],
                gain_sem,
            ).start()
        load_half(me_ref, arrays, order, rows_piece, weight, sem)
        x = x_ref[...].astype(F32)
        scaled = x * lax.rsqrt(jnp.mean(x * x, axis=-1, keepdims=True) + norm_eps)
        pltpu.make_async_copy(gain_parts, gain_parts, gain_sem).wait()
        parts = jnp.sum(gain_parts[...].astype(F32), axis=0)
        one = jnp.concatenate((parts[0:1], parts[1:2]), axis=1)
        gains_ref[...] = jnp.concatenate((one, jnp.concatenate((parts[2:3], parts[3:4]), axis=1)), axis=0)
        low = (scaled * one).astype(BF)
        normed_ref[...] = low
        normed_t_ref[...] = low.T
        pltpu.make_async_copy(weight, weight, sem).wait()

    column = pl.multiple_of(step * PART, PART)
    out_ref[...] = dot(normed_ref[...], weight[:, pl.ds(column, PART)]).astype(BF)


def first_project(me, tokens, arrays, order, rows_piece):
    rows = tokens.shape[0]
    full = lambda dims: pl.BlockSpec(dims, lambda step: (0,) * len(dims))
    return pl.pallas_call(
        functools.partial(first_project_kernel, order, rows_piece),
        grid=(2,),
        in_specs=[IN_SMEM, full((rows, HD))] + [IN_HBM] * len(arrays),
        out_specs=[
            pl.BlockSpec((rows, PART), lambda step: (0, step)),
            full((rows, HD)),
            full((HD, rows)),
            full((2, HD)),
        ],
        out_shape=[shape((rows, HALF), BF), shape((rows, HD), BF), shape((HD, rows), BF), shape((2, HD), F32)],
        scratch_shapes=[
            pltpu.VMEM((HD, HALF), BF),
            pltpu.VMEM((32 if order else 1, ROWS_GAIN, GAIN_COLS), BF),
            pltpu.SemaphoreType.DMA(()),
            pltpu.SemaphoreType.DMA(()),
        ],
        compiler_params=params(),
        name="first_project",
    )(me, tokens, *arrays)


def second_project_kernel(order, rows_piece, me_ref, normed_ref, *refs):
    n_arrays = GATHERED if order else 1
    arrays = refs[:n_arrays]
    out_ref, weight, sem = refs[n_arrays:]
    step = pl.program_id(0)

    @pl.when(step == 0)
    def _():
        load_half(me_ref, arrays, order, rows_piece, weight, sem)
        pltpu.make_async_copy(weight, weight, sem).wait()

    column = pl.multiple_of(step * PART, PART)
    out_ref[...] = dot(normed_ref[...], weight[:, pl.ds(column, PART)]).astype(BF)


def second_project(me, normed, arrays, order, rows_piece):
    rows = normed.shape[0]
    return pl.pallas_call(
        functools.partial(second_project_kernel, order, rows_piece),
        grid=(2,),
        in_specs=[IN_SMEM, pl.BlockSpec((rows, HD), lambda step: (0, 0))] + [IN_HBM] * len(arrays),
        out_specs=pl.BlockSpec((rows, PART), lambda step: (0, step)),
        out_shape=shape((rows, HALF), BF),
        scratch_shapes=[pltpu.VMEM((HD, HALF), BF), pltpu.SemaphoreType.DMA(())],
        compiler_params=params(),
        name="second_project",
    )(me, normed, *arrays)


def three_parts(values):
    first = values.astype(BF)
    rest = values - first.astype(F32)
    second = rest.astype(BF)
    return first, second, (rest - second.astype(F32)).astype(BF)


def mask_operands(segments):
    kind = jnp.arange(64, dtype=jnp.int32)
    mine = segments[None, :] + 1 == kind[:, None]
    query_side = jnp.where(mine, -1e30, 0.0).astype(BF)
    key_side = jnp.where((kind[None, :] < 4) & ~mine.T, 1.0, 0.0).astype(BF)
    return (
        jnp.concatenate((query_side, query_side), axis=0),
        jnp.concatenate((key_side, key_side), axis=1),
    )


def attend_forward_kernel(q_ref, k_ref, v_ref, mask_q_ref, mask_k_ref, out_ref, extra_ref):
    queries_t = (q_ref[...].astype(F32) * score_scale).astype(BF).T
    keys = k_ref[...]
    values_t = v_ref[...].T
    mask_q = mask_q_ref[...]
    mask_k = mask_k_ref[...]
    lane = lax.broadcasted_iota(jnp.int32, (1, 128), 1)
    row = lax.broadcasted_iota(jnp.int32, (64, 1), 0)
    ones = jnp.ones((16, LONG), BF)
    key_sides = (jnp.where(lane < 64, keys, mask_k), jnp.where(lane >= 64, keys, mask_k))
    query_sides = (
        jnp.concatenate((queries_t[0:64], mask_q[64:128]), axis=0),
        jnp.concatenate((mask_q[0:64], queries_t[64:128]), axis=0),
    )
    value_sides = [jnp.concatenate((values_t[64 * head : 64 * head + 64], ones), axis=0) for head in range(2)]
    out_blocks = ([], [])
    log_blocks = ([], [])

    def score(head, start):
        return dot(key_sides[head], query_sides[head][:, start : start + QUERY_BLOCK])

    def finish(head, top, expo):
        both = dot(value_sides[head], expo)
        sums = both[64:65]
        out_blocks[head].append((both[0:64] * (1.0 / sums)).astype(BF))
        log_blocks[head].append(-(top + jnp.log(sums)))

    jobs = [(head, start) for head in range(2) for start in range(0, LONG, QUERY_BLOCK)]
    scores = score(*jobs[0])
    waiting = None
    for index, job in enumerate(jobs):
        later = score(*jobs[index + 1]) if index + 1 < len(jobs) else None
        top = jnp.max(scores, axis=0, keepdims=True)
        expo = jnp.exp(scores - top).astype(BF)
        if waiting is not None:
            finish(*waiting)
        waiting = (job[0], top, expo)
        scores = later
    finish(*waiting)
    outs = [jnp.concatenate(blocks, axis=1) for blocks in out_blocks]
    extras = []
    for head in range(2):
        extra = mask_q[0:64].astype(F32)
        for index, part in enumerate(three_parts(jnp.concatenate(log_blocks[head], axis=1))):
            extra = jnp.where(row == 4 + index, part.astype(F32), extra)
        extras.append(extra.astype(BF))
    out_ref[...] = jnp.concatenate(outs, axis=0).T
    extra_ref[...] = jnp.concatenate((extras[1], extras[0]), axis=0).T


def tile_specs(rows, narrow, first):
    return [pl.BlockSpec((rows, 128), lambda i, c=c: (0, narrow * 6 + (first + i) * 3 + c)) for c in range(3)]


def attend_forward(projected, narrow, mask_q, mask_k):
    rows = projected.shape[0]
    tile = pl.BlockSpec((rows, 128), lambda i: (0, i))
    return pl.pallas_call(
        attend_forward_kernel,
        grid=(2,),
        in_specs=tile_specs(rows, narrow, 0)
        + [pl.BlockSpec((128, rows), lambda i: (0, 0)), pl.BlockSpec((rows, 128), lambda i: (0, 0))],
        out_specs=[tile, tile],
        out_shape=[shape((rows, 256), BF), shape((rows, 256), BF)],
        compiler_params=params(),
        name="attend_forward",
    )(projected, projected, projected, mask_q, mask_k)


def attend_backward_kernel(
    q_ref, k_ref, v_ref, out_ref, grad_ref, extra_ref, mask_k_ref, result_ref
):
    queries = (q_ref[...].astype(F32) * score_scale).astype(BF)
    queries_t = queries.T
    keys = k_ref[...]
    keys_t = keys.T
    values_t = v_ref[...].T
    grad = grad_ref[...]
    grad_t = grad.T
    extra = extra_ref[...]
    mask_k_t = mask_k_ref[...].T
    lane = lax.broadcasted_iota(jnp.int32, (1, 128), 1)
    row = lax.broadcasted_iota(jnp.int32, (64, 1), 0)
    product_t = (grad.astype(F32) * out_ref[...].astype(F32)).T
    inner = []
    for head in (1, 0):
        total = -jnp.sum(product_t[64 * head : 64 * head + 64], axis=0, keepdims=True)
        rows = jnp.zeros((64, LONG), F32)
        for index, part in enumerate(three_parts(total)):
            rows = jnp.where(row == index, part.astype(F32), rows)
        inner.append(rows.astype(BF))
    inner_cols = jnp.concatenate(inner, axis=0).T
    key_extra = jnp.where((row >= 4) & (row < 7), 1.0, mask_k_t[0:64].astype(F32)).astype(BF)
    value_extra = jnp.broadcast_to(jnp.where(row < 3, 1.0, 0.0).astype(BF), (64, LONG))
    grad_q = []
    grad_k = []
    grad_v = []
    for head in range(2):
        half = slice(64 * head, 64 * head + 64)
        own = (lane < 64) if head == 0 else (lane >= 64)
        query_side = jnp.where(own, queries, extra)
        grad_side = jnp.where(own, grad, inner_cols)
        if head == 0:
            key_side = jnp.concatenate((keys_t[half], key_extra), axis=0)
            value_side = jnp.concatenate((values_t[half], value_extra), axis=0)
        else:
            key_side = jnp.concatenate((key_extra, keys_t[half]), axis=0)
            value_side = jnp.concatenate((value_extra, values_t[half]), axis=0)
        q_blocks = []
        k_total = None
        v_total = None
        for start in range(0, LONG, QUERY_BLOCK):
            block = slice(start, start + QUERY_BLOCK)
            probs = jnp.exp(dot(query_side[block], key_side))
            grad_scores = (probs * dot(grad_side[block], value_side)).astype(BF)
            v_part = dot(grad_t[half, block], probs.astype(BF))
            k_part = dot(queries_t[half, block], grad_scores)
            v_total = v_part if v_total is None else v_total + v_part
            k_total = k_part if k_total is None else k_total + k_part
            q_blocks.append(dot(grad_scores, keys) * score_scale)
        grad_q.append(jnp.concatenate(q_blocks, axis=0))
        grad_k.append(k_total)
        grad_v.append(v_total)
    result_ref[:, 0:128] = jnp.where(lane < 64, grad_q[0], grad_q[1]).astype(BF)
    result_ref[:, 128:256] = jnp.concatenate(grad_k, axis=0).astype(BF).T
    result_ref[:, 256:384] = jnp.concatenate(grad_v, axis=0).astype(BF).T


def attend_backward(projected, attended, grad_attended, extra, mask_k, half, narrow, first, count):
    rows = projected.shape[0]
    own = pl.BlockSpec((rows, 128), lambda i: (0, first + i))
    return pl.pallas_call(
        attend_backward_kernel,
        grid=(count,),
        in_specs=tile_specs(rows, narrow, first)
        + [
            own,
            pl.BlockSpec((rows, 128), lambda i: (0, half * 4 + narrow * 2 + first + i)),
            own,
            pl.BlockSpec((rows, 128), lambda i: (0, 0)),
        ],
        out_specs=pl.BlockSpec((rows, 384), lambda i: (0, i)),
        out_shape=shape((rows, 384 * count), BF),
        compiler_params=params(),
        name="attend_backward",
    )(projected, projected, projected, attended, grad_attended, extra, mask_k)


class fetch:
    def __init__(self, sources, targets, sems):
        self.targets = targets
        self.copies = [pltpu.make_async_copy(*triple) for triple in zip(sources, targets, sems)]
        for copy in self.copies:
            copy.start()

    def wait(self, index):
        self.copies[index].wait()

    def __call__(self, index):
        self.wait(index)
        return self.targets[index][...]


def fetched(arrays):
    return [pltpu.VMEM(array.shape, array.dtype) for array in arrays] + [pltpu.SemaphoreType.DMA((len(arrays),))]


def one_buffer(dims):
    return pl.BlockSpec(dims, lambda step: (0,) * len(dims), pipeline_mode=pl.Buffered(buffer_count=1))


def load_out(me_ref, arrays, order, rows_piece, w_out, sem):
    cols, at = (GAIN_COLS, PART) if order else (HD, HALF)

    def start(source, dp, narrow):
        pltpu.make_async_copy(
            source.at[pl.ds(0, rows_piece), pl.ds(at, cols)],
            w_out.at[span(head_rows(dp, order is not None), rows_piece, 16), span(narrow, cols, 128)],
            sem,
        ).start()

    each_place(me_ref, arrays, order, start)


def load_wide(me_ref, arrays, orders, targets, sems):
    count = len(arrays) // 2
    for index, target in enumerate(targets):
        order = orders and orders[index]
        cols = target.shape[1] // (2 if order else 1)

        def start(source, dp, narrow, index=index, target=target, cols=cols):
            rows = source.shape[0]
            pltpu.make_async_copy(
                source, target.at[span(dp, rows, 16), span(narrow, cols, 128)], sems[index]
            ).start()

        each_place(me_ref, arrays[index * count : (index + 1) * count], order, start)


def load_wide_by_half(me_ref, arrays, orders, targets, sems):
    whole = targets[0].shape[1]
    count = len(arrays) // 2
    for half in range(2):
        cols = pl.ds(half * (whole // 2), whole // 2)
        for index, target in enumerate(targets):
            if orders is None:
                pltpu.make_async_copy(arrays[index].at[0, :, cols], target.at[:, cols], sems.at[index, half]).start()
                continue

            def start(source, dp, narrow, half=half, index=index, target=target, cols=cols):
                copy = pltpu.make_async_copy(
                    source, target.at[span(dp, source.shape[0], 16), cols], sems.at[index, half]
                )
                pl.when(narrow == half)(copy.start)

            each_place(me_ref, arrays[index * count : (index + 1) * count], orders[index], start)


def wait_half(targets, sems, half):
    whole = targets[0].shape[1]
    for index, target in enumerate(targets):
        part = target.at[:, pl.ds(half * (whole // 2), whole // 2)]
        pltpu.make_async_copy(part, part, sems.at[index, half]).wait()


def load_down(me_ref, arrays, order, w_down, sem):
    rows, cols = arrays[0].shape[1:]

    def start(source, dp, narrow):
        pltpu.make_async_copy(source, w_down.at[span(dp, rows, 16), span(narrow, cols, 128)], sem).start()

    each_place(me_ref, arrays, order, start)


def load_down_by_group(me_ref, arrays, order, w_down, sems):
    rows, cols = arrays[0].shape[1:]
    if order is None:
        rows = rows // N_GROUPS
        for group in range(N_GROUPS):
            part = pl.ds(group * rows, rows)
            pltpu.make_async_copy(arrays[0].at[0, part], w_down.at[part], sems.at[group]).start()
        return

    def start(source, dp, narrow):
        pltpu.make_async_copy(
            source, w_down.at[span(dp, rows, 16), span(narrow, cols, 128)], sems.at[dp >> 2]
        ).start()

    each_place(me_ref, arrays, order, start)


def wait_group(w_down, sems, group):
    rows = w_down.shape[0] // N_GROUPS
    part = w_down.at[pl.ds(group * rows, rows)]
    pltpu.make_async_copy(part, part, sems.at[group]).wait()


def all_of(ref, sem):
    pltpu.make_async_copy(ref, ref, sem).wait()


def gelu_parts(gate):
    square = gate * gate
    curve = jnp.tanh(gate * (0.7978845608028654 + (0.7978845608028654 * 0.044715) * square))
    half = 0.5 + 0.5 * curve
    active = gate * half
    bend = (2.0 * 0.7978845608028654) + (6.0 * 0.7978845608028654 * 0.044715) * square
    return active, half + active * (1.0 - half) * bend


def feed_in_kernel(orders, rows_piece, me_ref, valid_ref, gains_ref, *refs):
    square_order, wide_orders, _, _, down_order = orders
    given, refs = refs[:6], refs[6:]
    n_arrays = GATHERED if down_order else 1
    square, wide = refs[:n_arrays], refs[n_arrays : 3 * n_arrays]
    refs = refs[3 * n_arrays :]
    active_out, sloped_out, inner_out, hidden_out, normed_t_out, grad_mixed_out = refs[:6]
    n_grads = SCATTERED if down_order else 1
    grad_down = refs[6 : 6 + n_grads]
    w_out, w_gate, w_up, w_down, hidden, normed, normed_t, inner = refs[6 + n_grads : 14 + n_grads]
    stages, sem, wide_sems, out_sems, stage_sems, down_sems, *own = refs[14 + n_grads :]
    att_a, att_b, att_c, att_d, x_ref, grad_mixed, in_sems = own
    ff = w_down.shape[0]
    load_out(me_ref, square, square_order, rows_piece, w_out, sem)
    get = fetch(given, own[:6], [in_sems.at[index] for index in range(6)])
    load_wide_by_half(me_ref, wide, wide_orders, (w_gate, w_up), wide_sems)
    gain = gains_ref[1:2]
    for index in range(6):
        get.wait(index)
    all_of(w_out, sem)

    def row_block(index):
        return pl.ds(pl.multiple_of(index * QUERY_BLOCK, QUERY_BLOCK), QUERY_BLOCK)

    def before(index, carry):
        part = row_block(index)
        left = jnp.concatenate([ref[part, :] for ref in (att_a, att_b, att_c, att_d)], axis=1)
        state = x_ref[part, :].astype(F32) + dot(left, w_out[...])
        hidden[part, :] = state
        low = (state * lax.rsqrt(jnp.mean(state * state, axis=-1, keepdims=True) + norm_eps) * gain).astype(BF)
        normed[part, :] = low
        normed_t[:, part] = low.T
        grad_mixed[part, :] = (grad_mixed[part, :].astype(F32) * valid_ref[part, :]).astype(BF)
        return carry

    blocks = x_ref.shape[0] // QUERY_BLOCK
    lax.fori_loop(0, blocks, before, 0)
    leaving = [
        pltpu.make_async_copy(hidden, hidden_out, out_sems.at[0]),
        pltpu.make_async_copy(normed_t, normed_t_out, out_sems.at[1]),
        pltpu.make_async_copy(grad_mixed, grad_mixed_out, out_sems.at[2]),
    ]
    for copy in leaving:
        copy.start()
    for half in range(2):
        wait_half((w_gate, w_up), wide_sems, half)
    width = ff // 2

    def stage_copy(index, half, which, target):
        return pltpu.make_async_copy(
            stages.at[half, which], target.at[row_block(index), pl.ds(half * width, width)], stage_sems.at[half, which]
        )

    def block(index, carry):
        part = row_block(index)
        left = normed[part, :]
        for half in range(2):
            cols = pl.ds(half * width, width)
            gate = dot(left, w_gate[:, cols])
            upward = dot(left, w_up[:, cols])
            active, slope = gelu_parts(gate)
            inner[part, cols] = (active * upward).astype(BF)

            @pl.when(index > 0)
            def _():
                stage_copy(index, half, 0, active_out).wait()
                stage_copy(index, half, 1, sloped_out).wait()

            stages[half, 0] = active.astype(BF)
            stages[half, 1] = (upward * slope).astype(BF)
            stage_copy(index, half, 0, active_out).start()
            stage_copy(index, half, 1, sloped_out).start()
        return carry

    lax.fori_loop(0, blocks, block, 0)
    leaving.append(pltpu.make_async_copy(inner, inner_out, out_sems.at[3]))
    leaving[-1].start()
    for group in range(N_GROUPS):
        begin, end = group * DOWN_BLOCK, min((group + 1) * DOWN_BLOCK, ff)
        w_down[begin:end, :] = dot(inner[:, begin:end].T, grad_mixed[...]).astype(BF)
        if down_order is None:
            part = pl.ds(group * (ff // N_GROUPS), ff // N_GROUPS)
            pltpu.make_async_copy(w_down.at[part], grad_down[0].at[0, part], down_sems.at[group]).start()
            continue

        def finish(target, dp, narrow, group=group):
            rows, cols = target.shape
            copy = pltpu.make_async_copy(
                w_down.at[span(dp, rows, 16), span(narrow, cols, 128)], target, down_sems.at[group]
            )
            pl.when(dp >> 2 == group)(copy.start)

        each_place(me_ref, grad_down, down_order, finish)
    for half in range(2):
        stage_copy(blocks - 1, half, 0, active_out).wait()
        stage_copy(blocks - 1, half, 1, sloped_out).wait()
    for copy in leaving:
        copy.wait()
    for group in range(N_GROUPS):
        wait_group(w_down, down_sems, group)


def feed_in(me, tokens, attended, cotangent, valid, gains, square, wide, orders, rows_piece, ff, down_shape):
    rows = tokens.shape[0]
    n_grads = SCATTERED if orders[4] else 1
    given = (*attended, tokens, cotangent)
    outs = pl.pallas_call(
        functools.partial(feed_in_kernel, orders, rows_piece),
        in_specs=[IN_SMEM, IN_VMEM, IN_VMEM] + [IN_HBM] * (len(given) + len(square) + len(wide)),
        out_specs=[IN_HBM] * (6 + n_grads),
        out_shape=[
            shape((rows, ff), BF),
            shape((rows, ff), BF),
            shape((rows, ff), BF),
            shape((rows, HD), F32),
            shape((HD, rows), BF),
            shape((rows, HD), BF),
        ]
        + [shape(down_shape, BF)] * n_grads,
        scratch_shapes=[
            pltpu.VMEM((HD, HD), BF),
            pltpu.VMEM((HD, ff), BF),
            pltpu.VMEM((HD, ff), BF),
            pltpu.VMEM((ff, HD), BF),
            pltpu.VMEM((rows, HD), F32),
            pltpu.VMEM((rows, HD), BF),
            pltpu.VMEM((HD, rows), BF),
            pltpu.VMEM((rows, ff), BF),
            pltpu.VMEM((2, 2, QUERY_BLOCK, ff // 2), BF),
            pltpu.SemaphoreType.DMA(()),
            pltpu.SemaphoreType.DMA((2, 2)),
            pltpu.SemaphoreType.DMA((4,)),
            pltpu.SemaphoreType.DMA((2, 2)),
            pltpu.SemaphoreType.DMA((N_GROUPS,)),
        ]
        + fetched(given),
        compiler_params=params(),
        name="feed_in",
    )(me, valid, gains, *given, *square, *wide)
    return (*outs[:6], outs[6:])


def feed_grad_kernel(orders, rows_piece, me_ref, active_ref, sloped_ref, *refs):
    _, _, down_order, wide_order, _ = orders
    given, refs = refs[:2], refs[2:]
    n_arrays = GATHERED if down_order else 1
    down = refs[:n_arrays]
    grad_gate_out, grad_up_out = refs[n_arrays : n_arrays + 2]
    n_grads = SCATTERED if wide_order else 1
    grad_wide = refs[n_arrays + 2 : n_arrays + 2 + n_grads]
    w_down, w_gate, w_up, up_side, gate_side, down_sems, side_sems, leave_sems, out_sems = refs[
        n_arrays + 2 + n_grads : -3
    ]
    grad_mixed, normed_t, in_sems = refs[-3:]
    rows, ff = active_ref.shape
    blocks = rows // QUERY_BLOCK
    parts = [pl.ds(index * QUERY_BLOCK, QUERY_BLOCK) for index in range(blocks)]
    first = pltpu.make_async_copy(given[0], grad_mixed, in_sems.at[0])
    first.start()
    load_down_by_group(me_ref, down, down_order, w_down, down_sems)
    sides = [
        [pltpu.make_async_copy(source.at[part], target.at[part], side_sems.at[which, index]) for index, part in enumerate(parts)]
        for which, (source, target) in enumerate(((active_ref, up_side), (sloped_ref, gate_side)))
    ]
    for index in range(blocks):
        for which in range(2):
            sides[which][index].start()
    last = pltpu.make_async_copy(given[1], normed_t, in_sems.at[1])
    last.start()
    first.wait()
    width = ff // 2
    leaving = []
    for index, part in enumerate(parts):
        left = grad_mixed[part, :]
        sides[0][index].wait()
        sides[1][index].wait()
        for half in range(2):
            if index == 0:
                for group in range(N_GROUPS // 2):
                    wait_group(w_down, down_sems, half * (N_GROUPS // 2) + group)
            cols = pl.ds(half * width, width)
            grad_inner = dot(left, w_down[cols, :], NT)
            gate_side[part, cols] = (grad_inner * gate_side[part, cols].astype(F32)).astype(BF)
            up_side[part, cols] = (grad_inner * up_side[part, cols].astype(F32)).astype(BF)
        for which, (source, target) in enumerate(((gate_side, grad_gate_out), (up_side, grad_up_out))):
            leaving.append(pltpu.make_async_copy(source.at[part], target.at[part], leave_sems.at[which, index]))
            leaving[-1].start()
    last.wait()
    left = normed_t[...]
    ready = (6 * FF_BLOCK, 9 * FF_BLOCK, ff)
    ends = (ff // 2, ff // 2 + 3 * FF_BLOCK + FF_BLOCK // 2, ff)
    piece = ff // 2 if wide_order else ff
    for place, (done, upto, begin, end) in enumerate(zip((0, *ready), ready, (0, *ends), ends)):
        w_gate[:, done:upto] = dot(left, gate_side[:, done:upto]).astype(BF)
        w_up[:, done:upto] = dot(left, up_side[:, done:upto]).astype(BF)

        def finish(target, dp, narrow, place=place, begin=begin, count=end - begin):
            def copies():
                for index, source in enumerate((w_gate, w_up)):
                    pltpu.make_async_copy(
                        source.at[span(dp, rows_piece, 16), pl.ds(begin, count)],
                        target.at[pl.ds(index * rows_piece, rows_piece), pl.ds(begin % piece, count)],
                        out_sems.at[index, place],
                    ).start()

            if wide_order is None:
                copies()
            else:
                pl.when(narrow == begin // piece)(copies)

        each_place(me_ref, grad_wide, wide_order, finish)
    for copy in leaving:
        copy.wait()
    for index, source in enumerate((w_gate, w_up)):
        for place, (begin, end) in enumerate(zip((0, *ends), ends)):
            part = source.at[:, pl.ds(begin, end - begin)]
            pltpu.make_async_copy(part, part, out_sems.at[index, place]).wait()


def feed_grad(me, active, sloped, grad_mixed, normed_t, down, orders, rows_piece, wide_shape):
    rows, ff = active.shape
    n_grads = SCATTERED if orders[3] else 1
    blocks = rows // QUERY_BLOCK
    outs = pl.pallas_call(
        functools.partial(feed_grad_kernel, orders, rows_piece),
        in_specs=[IN_SMEM] + [IN_HBM] * (4 + len(down)),
        out_specs=[IN_HBM] * (2 + n_grads),
        out_shape=[shape((rows, ff), BF)] * 2 + [shape(wide_shape, BF)] * n_grads,
        scratch_shapes=[
            pltpu.VMEM((ff, HD), BF),
            pltpu.VMEM((HD, ff), BF),
            pltpu.VMEM((HD, ff), BF),
            pltpu.VMEM((rows, ff), BF),
            pltpu.VMEM((rows, ff), BF),
            pltpu.SemaphoreType.DMA((N_GROUPS,)),
            pltpu.SemaphoreType.DMA((2, blocks)),
            pltpu.SemaphoreType.DMA((2, blocks)),
            pltpu.SemaphoreType.DMA((2, 3)),
        ]
        + fetched((grad_mixed, normed_t)),
        compiler_params=params(),
        name="feed_grad",
    )(me, active, sloped, grad_mixed, normed_t, *down)
    return outs[0], outs[1], outs[2:]


def feed_out_kernel(orders, rows_piece, me_ref, inner_ref, grad_gate_ref, grad_up_ref, hidden_ref, grad_mixed_ref, gains_ref, *refs):
    square_order, wide_orders, down_order, _, _ = orders
    n_arrays = GATHERED if down_order else 1
    square, wide, down = refs[:n_arrays], refs[n_arrays : 3 * n_arrays], refs[3 * n_arrays : 4 * n_arrays]
    mixed_ref, grad_hidden_ref, grad_attended_ref, gain_grad_ref = refs[4 * n_arrays : 4 * n_arrays + 4]
    w_out, w_gate, w_up, w_down, sems = refs[4 * n_arrays + 4 :]
    step = pl.program_id(0)

    @pl.when(step == 0)
    def _():
        load_down(me_ref, down, down_order, w_down, sems.at[3])
        load_wide(me_ref, wide, wide_orders, (w_gate, w_up), (sems.at[1], sems.at[2]))
        load_out(me_ref, square, square_order, rows_piece, w_out, sems.at[0])
        gain_grad_ref[...] = jnp.zeros_like(gain_grad_ref)
        all_of(w_down, sems.at[3])

    @pl.when(step < pl.num_programs(0) // 2)
    def _():
        mixed_ref[...] = (hidden_ref[...] + dot(inner_ref[...], w_down[...])).astype(BF)

    @pl.when(step == pl.num_programs(0) // 2)
    def _():
        all_of(w_gate, sems.at[1])
        all_of(w_up, sems.at[2])
        all_of(w_out, sems.at[0])

    @pl.when(step >= pl.num_programs(0) // 2)
    def _():
        state = hidden_ref[...]
        through = dot(grad_gate_ref[...], w_gate[...], NT) + dot(grad_up_ref[...], w_up[...], NT)
        scale = lax.rsqrt(jnp.mean(state * state, axis=-1, keepdims=True) + norm_eps)
        unit = state * scale
        gain_grad_ref[...] += jnp.sum(through * unit, axis=0, keepdims=True)
        through = through * gains_ref[1:2]
        result = grad_mixed_ref[...].astype(F32) + scale * (
            through - unit * jnp.mean(through * unit, axis=-1, keepdims=True)
        )
        grad_hidden_ref[...] = result
        grad_attended_ref[...] = dot(result.astype(BF), w_out[...], NT).astype(BF)


def feed_out(me, inner, grad_gate, grad_up, hidden, grad_mixed, gains, square, wide, down, orders, rows_piece):
    rows, ff = inner.shape
    n_arrays = len(down)
    count = rows // QUERY_BLOCK
    early = lambda cols: pl.BlockSpec((QUERY_BLOCK, cols), lambda step: (jnp.minimum(step, count - 1), 0))
    late = lambda cols: pl.BlockSpec((QUERY_BLOCK, cols), lambda step: (jnp.maximum(step - count, 0), 0))
    both = pl.BlockSpec((QUERY_BLOCK, HD), lambda step: (step % count, 0))
    return pl.pallas_call(
        functools.partial(feed_out_kernel, orders, rows_piece),
        grid=(2 * count,),
        in_specs=[IN_SMEM, early(ff), late(ff), late(ff), both, late(HD), one_buffer((2, HD))]
        + [IN_HBM] * (4 * n_arrays),
        out_specs=[early(HD), late(HD), late(HD), pl.BlockSpec((1, HD), lambda step: (0, 0))],
        out_shape=[shape((rows, HD), BF), shape((rows, HD), F32), shape((rows, HD), BF), shape((1, HD), F32)],
        scratch_shapes=[
            pltpu.VMEM((HD, HD), BF),
            pltpu.VMEM((HD, ff), BF),
            pltpu.VMEM((HD, ff), BF),
            pltpu.VMEM((ff, HD), BF),
            pltpu.SemaphoreType.DMA((4,)),
        ],
        compiler_params=params(),
        name="feed_out",
    )(me, inner, grad_gate, grad_up, hidden, grad_mixed, gains, *square, *wide, *down)


def half_of_grads(refs):
    wide = []
    held = []
    for ref in refs:
        held.append(ref)
        if sum(part.shape[1] for part in held) == PART:
            wide.append(held)
            held = []
    return wide


def weight_grad_kernel(order, rows_piece, n_grads, with_out, me_ref, *refs):
    n_arrays = 4 if order else 1
    fast = order is not None
    n_in = 1 + n_grads + (5 if with_out else 0)
    sources, targets, own = refs[:n_in], refs[n_in : n_in + n_arrays], refs[n_in + n_arrays :]
    held, in_sems = own[:n_in], own[n_in]
    weight, sems = own[n_in + 1 : n_in + 3]
    get = fetch(sources, held, [in_sems.at[index] for index in range(n_in)])
    cols = PART if fast else HALF
    left = get(0)
    begin = 1
    for index, group in enumerate(half_of_grads(sources[1 : 1 + n_grads])):
        right = [get(begin + place) for place in range(len(group))]
        begin += len(group)
        right = right[0] if len(right) == 1 else jnp.concatenate(right, axis=1)
        part = pl.ds(index * PART, PART)
        weight[:, part] = dot(left, right).astype(BF)

        def finish(target, dp, narrow, index=index, part=part):
            copy = pltpu.make_async_copy(
                weight.at[span(dp, rows_piece, 16), part],
                target.at[pl.ds(0, rows_piece), pl.ds(0 if fast else index * PART, PART)],
                sems.at[index],
            )
            if fast:
                pl.when(narrow == index)(copy.start)
            else:
                copy.start()

        each_place(me_ref, targets, order, finish)
    if with_out:
        w_out, out_sem = own[n_in + 3 :]
        col_d = GAIN_COLS if fast else HD
        attended = [get(1 + n_grads + index) for index in range(4)]
        branch = get(n_in - 1).astype(BF)
        for index in range(4):
            w_out[index * 256 : (index + 1) * 256, :] = dot(attended[index].T, branch).astype(BF)

        def finish_out(target, dp, narrow):
            pltpu.make_async_copy(
                w_out.at[span(head_rows(dp, fast), rows_piece, 16), span(narrow, col_d, 128)],
                target.at[pl.ds(0, rows_piece), pl.ds(cols, col_d)],
                out_sem,
            ).start()

        each_place(me_ref, targets, order, finish_out)
        all_of(w_out, out_sem)
    for index in range(2):
        part = weight.at[:, pl.ds(index * PART, PART)]
        pltpu.make_async_copy(part, part, sems.at[index]).wait()


def weight_grad(me, normed_t, grads, order, rows_piece, attended=(), grad_hidden=None):
    with_out = grad_hidden is not None
    cols = (PART if order else HALF) + ((GAIN_COLS if order else HD) if with_out else 0)
    outs = [shape((8 if order else 1, rows_piece, cols), BF)] * (4 if order else 1)
    more = [*attended, grad_hidden] if with_out else []
    given = [normed_t, *grads, *more]
    scratch = fetched(given) + [pltpu.VMEM((HD, HALF), BF), pltpu.SemaphoreType.DMA((2,))]
    if with_out:
        scratch += [pltpu.VMEM((HD, HD), BF), pltpu.SemaphoreType.DMA(())]
    return pl.pallas_call(
        functools.partial(weight_grad_kernel, order, rows_piece, len(grads), with_out),
        in_specs=[IN_SMEM] + [IN_HBM] * len(given),
        out_specs=[IN_HBM] * len(outs),
        out_shape=outs,
        scratch_shapes=scratch,
        compiler_params=params(),
        name="weight_grad",
    )(me, *given)


def pair_grad_kernel(order, rows_piece, narrow_now, n_into, me_ref, *refs):
    sources, refs = refs[:4], refs[4 + n_into :]
    targets, held, in_sems, weight, sem = refs[:2], refs[2:6], *refs[6:]
    get = fetch(sources, held, [in_sems.at[index] for index in range(4)])
    own = dot(get(0), get(1))
    weight[...] = (own + dot(get(2), get(3))).astype(BF)
    me = me_ref[0]
    for index in range(16):
        dp, narrow = owner_of(me, index, order)
        copy = pltpu.make_async_copy(
            weight.at[span(dp >> 1, rows_piece, 16)], targets[index // 8].at[index % 8], sem
        )
        pl.when(narrow == narrow_now)(copy.start)
    all_of(weight, sem)


def pair_grad(me, own_t, own_grad, other_t, other_grad, order, rows_piece, narrow_now, into=()):
    given = [own_t, own_grad, other_t, other_grad]
    outs = [shape((8, rows_piece, PART), BF)] * 2
    return pl.pallas_call(
        functools.partial(pair_grad_kernel, order, rows_piece, narrow_now, len(into)),
        in_specs=[IN_SMEM] + [IN_HBM] * (4 + len(into)),
        input_output_aliases={5 + index: index for index in range(len(into))},
        out_specs=[IN_HBM] * 2,
        out_shape=outs,
        scratch_shapes=fetched(given) + [pltpu.VMEM((HD // 2, PART), BF), pltpu.SemaphoreType.DMA(())],
        compiler_params=params(),
        name="pair_grad",
    )(me, *given, *into)


def input_grad_kernel(order, rows_piece, n_grads, last, me_ref, *refs):
    n_arrays = GATHERED if order else 1
    n_in = n_grads + (3 if last else 0)
    arrays, sources = refs[:n_arrays], refs[n_arrays : n_arrays + n_in]
    refs = refs[n_arrays + n_in :]
    if last:
        gains_ref, out_ref, gain_grad_ref = refs[:3]
        refs = refs[3:]
    else:
        out_ref = refs[0]
        refs = refs[1:]
    held, in_sems, weight, sem = refs[:n_in], refs[n_in], refs[n_in + 1], refs[n_in + 2]
    load_half(me_ref, arrays, order, rows_piece, weight, sem)
    get = fetch(sources, held, [in_sems.at[index] for index in range(n_in)])
    left = jnp.concatenate([get(index) for index in range(n_grads)], axis=1)
    all_of(weight, sem)
    if not last:
        out_ref[...] = dot(left, weight[...], NT).astype(BF)
        return
    found, out_sem = refs[n_in + 3 :]
    found[...] = dot(left, weight[...], NT)
    for index in range(3):
        get.wait(n_grads + index)
    through_ref, x_ref, grad_hidden_ref = held[n_grads:]
    gain_grad_ref[...] = jnp.zeros_like(gain_grad_ref)

    def rows(index, carry):
        part = pl.ds(pl.multiple_of(index * QUERY_BLOCK, QUERY_BLOCK), QUERY_BLOCK)
        through = through_ref[part, :].astype(F32) + found[part, :]
        x = x_ref[part, :].astype(F32)
        scale = lax.rsqrt(jnp.mean(x * x, axis=-1, keepdims=True) + norm_eps)
        unit = x * scale
        gain_grad_ref[...] += jnp.sum(through * unit, axis=0, keepdims=True)
        through = through * gains_ref[0:1]
        found[part, :] = grad_hidden_ref[part, :] + scale * (
            through - unit * jnp.mean(through * unit, axis=-1, keepdims=True)
        )
        pltpu.make_async_copy(found.at[part], out_ref.at[part], out_sem).start()
        return carry

    lax.fori_loop(0, found.shape[0] // QUERY_BLOCK, rows, 0)
    pltpu.make_async_copy(found, out_ref, out_sem).wait()


def input_gradient(me, grads, arrays, order, rows_piece, more=(), gains=None):
    rows = grads[0].shape[0]
    last = gains is not None
    given = [*grads, *more]
    outs = [shape((rows, HD), F32), shape((1, HD), F32)] if last else [shape((rows, HD), BF)]
    scratch = fetched(given) + [pltpu.VMEM((HD, HALF), BF), pltpu.SemaphoreType.DMA(())]
    if last:
        scratch += [pltpu.VMEM((rows, HD), F32), pltpu.SemaphoreType.DMA(())]
    return pl.pallas_call(
        functools.partial(input_grad_kernel, order, rows_piece, len(grads), last),
        in_specs=[IN_SMEM] + [IN_HBM] * (len(arrays) + len(given)) + ([IN_VMEM] if last else []),
        out_specs=[IN_HBM, IN_VMEM] if last else [IN_VMEM],
        out_shape=outs,
        scratch_shapes=scratch,
        compiler_params=params(),
        name="input_gradient",
    )(me, *arrays, *given, *([gains] if last else []))


def segment_ids(bucket_one, text_one):
    position = jnp.arange(LONG, dtype=jnp.int32)
    slot_index = position // SLOT
    inside = position - slot_index * SLOT
    slot_length = SHORT_PATCH + jnp.where(
        slot_index == 0, text_one[0], jnp.where(slot_index == 1, text_one[1], text_one[2])
    )
    long_valid = position < LONG_PATCH + text_one[0]
    short_valid = inside < slot_length
    return jnp.where(
        bucket_one == 1, jnp.where(long_valid, 0, -1), jnp.where(short_valid, slot_index, -1)
    ).astype(jnp.int32)


def adamw(weight, grad_total, first, second, rate):
    first_new = beta_one * first + (1.0 - beta_one) * grad_total
    second_new = beta_two * second + (1.0 - beta_two) * grad_total * grad_total
    first_hat = first_new / (1.0 - beta_one**STEP)
    second_hat = second_new / (1.0 - beta_two**STEP)
    weight_new = weight - rate * (first_hat / (jnp.sqrt(second_hat) + adam_eps) + decay_rate * weight)
    return (grad_total, first_new, second_new, weight_new)


def heads_first(array):
    rows = array.shape[1]
    return array.reshape(3, rows, 2, 2, 2, 128).transpose(3, 1, 2, 4, 0, 5).reshape(2, rows, HALF)


def heads_back(first, second):
    rows = first.shape[0]
    stacked = jnp.stack((first, second)).reshape(2, rows, 2, 2, 3, 128)
    return stacked.transpose(4, 1, 2, 0, 3, 5).reshape(3, rows, HD)


def gain_block(low_gains, cols):
    return jnp.pad(low_gains.reshape(4, GAIN_COLS), ((0, ROWS_GAIN - 4), (0, cols - GAIN_COLS)))


def local(n_dp, n_narrow, tokens, cotangent, bucket, text_lengths, *weights):
    attn_qkv, attn_out, ffn_in, ffn_out, norm_gains = weights[:5]
    masters, firsts, seconds = weights[:5], weights[5:10], weights[10:]
    run = local_fast if (n_dp, n_narrow) == (16, 2) else local_any
    linear = lax.axis_index("dp") * n_narrow + lax.axis_index("narrow")
    me = linear.astype(jnp.int32)[None]
    own = norm_gains.shape[1]
    low_gains = lax.dynamic_update_slice(jnp.zeros((2, HD), BF), norm_gains.astype(BF), (0, linear * own))
    segments = segment_ids(bucket[0], text_lengths[0])
    valid = (segments >= 0).astype(F32)[:, None]
    masks = mask_operands(segments)
    mixed, input_grad, shares, gain_sums = run(
        me, tokens, cotangent, valid, masks, attn_qkv, attn_out, ffn_in, ffn_out, low_gains
    )
    shares = (*shares, lax.dynamic_slice(gain_sums, (0, linear * own), (2, own)))
    results = [mixed, input_grad]
    for index in range(5):
        results.extend(adamw(masters[index], shares[index], firsts[index], seconds[index], rates[index]))
    return tuple(results)


def local_fast(me, tokens, cotangent, valid, masks, attn_qkv, attn_out, ffn_in, ffn_out, low_gains):
    mask_q, mask_k = masks
    row_d, width = attn_out.shape
    row_f, col_f = ffn_out.shape[0], ffn_in.shape[2]
    low_one = attn_qkv.reshape(3, row_d, 2, 2, 128)[:, :, 0].transpose(1, 2, 0, 3).reshape(row_d, PART)
    one = joined(low_one.astype(BF), gain_block(low_gains, PART))[None]
    z_a, z_b, z_c, z_d, core = BY_Z
    p_a, p_b, p_c, p_d, _ = BY_PLANE

    one_in, attn_qkv, attn_out, ffn_in, ffn_out = tie(swap(one, z_a), attn_qkv, attn_out, ffn_in, ffn_out)
    one = joined(one, one_in)
    low_two = attn_qkv.reshape(3, row_d, 2, 2, 128)[:, :, 1].transpose(1, 2, 0, 3).reshape(row_d, PART)
    two = jnp.concatenate((low_two, attn_out), axis=1).astype(BF)[None]
    gate = ffn_in[0].astype(BF)[None]
    up = ffn_in[1].astype(BF)[None]
    down = ffn_out.astype(BF)[None]
    one_in, two_in, gate, up = tie(swap(one, z_b), swap(two, z_a), gate, up)
    one, two = joined(one, one_in), joined(two, two_in)
    one_c, one_d, one_x, two_in, gate, up, valid = tie(
        swap(one, z_c), swap(one, z_d), swap(one, core), swap(two, z_b), gate, up, valid
    )
    two = joined(two, two_in)
    one_cd, one_cx, one_dx, up_in, gate_in, two, mask_q, mask_k = tie(
        swap(one_c, z_d), swap(one_c, core), swap(one_d, core), swap(up, z_a), swap(gate, p_a), two, mask_q, mask_k
    )
    one_cdx, two, up_in, gate_in, cotangent = tie(swap(one_cd, core), two, up_in, gate_in, cotangent)
    ones = (one, one_c, one_d, one_cd, one_x, one_cx, one_dx, one_cdx)
    up, gate = joined(up, up_in), joined(gate, gate_in)
    two_c = swap(two, z_c)
    up_in = swap(up, z_b)
    gate_in = swap(gate, p_b)
    two_x = swap(two, core)
    first, normed, normed_t, gains = first_project(me, tokens, ones, BY_Z, row_d)
    first, two, two_c, two_x, up_in, gate_in = tie(first, two, two_c, two_x, up_in, gate_in)
    up, gate = joined(up, up_in), joined(gate, gate_in)
    two_d = swap(two, z_d)
    two_cd = swap(two_c, z_d)
    gate_c = swap(gate, p_c)
    two_cx = swap(two_c, core)
    att_a, extra_a = attend_forward(first, 0, mask_q, mask_k)
    first, att_a, two_d, two_cx, up, down = tie(first, att_a, two_d, two_cx, up, down)
    gate_x = swap(gate, core)
    up_c = swap(up, z_c)
    two_dx = swap(two_d, core)
    down_in = swap(down, z_a)
    att_b, extra_b = attend_forward(first, 1, mask_q, mask_k)
    normed, att_b, two_cd, two_dx, up_c, gate_c, gate_x, down_in, up, gate = tie(
        normed, att_b, two_cd, two_dx, up_c, gate_c, gate_x, down_in, up, gate
    )
    down = joined(down, down_in)
    up_d = swap(up, z_d)
    gate_d = swap(gate, p_d)
    normed, two_cdx = tie(normed, swap(two_cd, core))
    twos = (two, two_c, two_d, two_cd, two_x, two_cx, two_dx, two_cdx)
    up_x = swap(up, core)
    gate_cx = swap(gate_c, core)
    down_in = swap(down, z_b)
    second = second_project(me, normed, twos, BY_Z, row_d)
    second, up_d, up_x, gate_cx, down_in, up_c, gate_c = tie(second, up_d, up_x, gate_cx, down_in, up_c, gate_c)
    down = joined(down, down_in)
    up_cd = swap(up_c, z_d)
    gate_cd = swap(gate_c, p_d)
    up_cx = swap(up_c, core)
    up_dx = swap(up_d, core)
    att_c, extra_c = attend_forward(second, 0, mask_q, mask_k)
    second, att_c, up_cd, up_cx, up_dx, gate_d, down = tie(second, att_c, up_cd, up_cx, up_dx, gate_d, down)
    up_cdx = swap(up_cd, core)
    gate_dx = swap(gate_d, core)
    down_c = swap(down, z_c)
    down_x = swap(down, core)
    att_d, extra_d = attend_forward(second, 1, mask_q, mask_k)
    att_d, up_cdx, gate_dx, gate_cd, down_c, down_x, down = tie(
        att_d, up_cdx, gate_dx, gate_cd, down_c, down_x, down
    )
    down_d = swap(down, z_d)
    gate_cdx, att_d = tie(swap(gate_cd, core), att_d)
    down_cd = swap(down_c, z_d)
    down_cx = swap(down_c, core)
    gates = (gate, gate_c, gate_d, gate_cd, gate_x, gate_cx, gate_dx, gate_cdx)
    ups = (up, up_c, up_d, up_cd, up_x, up_cx, up_dx, up_cdx)
    wides = (*gates, *ups)
    attended = (att_a, att_b, att_c, att_d)
    extras = (extra_a, extra_b, extra_c, extra_d)
    orders = (BY_Z, (BY_PLANE, BY_Z), BY_Z, BY_Z, BY_PLANE)
    active, sloped, inner, hidden, normed_two_t, grad_mixed, g_down = feed_in(
        me, tokens, attended, cotangent, valid, gains, twos, wides, orders, row_d, 2 * col_f, (8, row_f, width)
    )
    grad_mixed, g_down, down_d, down_cd, down_cx = tie(grad_mixed, g_down, down_d, down_cd, down_cx)
    down_dx = swap(down_d, core)
    down_cdx = swap(down_cd, core)
    d_on = swap(g_down[3], core)
    d_other = swap(g_down[2], core)
    grad_mixed, down_dx, down_cdx = tie(grad_mixed, down_dx, down_cdx)
    downs = (down, down_c, down_d, down_cd, down_x, down_cx, down_dx, down_cdx)

    def back(half, narrow, grad_now):
        place = half * 2 + narrow
        return attend_backward(
            (first, second)[half], attended[place], grad_now, extras[place], mask_k, half, narrow, 0, 2
        )

    grad_gate, grad_up, g_wide = feed_grad(
        me, active, sloped, grad_mixed, normed_two_t, downs, orders, row_d, (8, 2 * row_d, col_f)
    )
    grad_gate, g_wide, d_on, d_other = tie(grad_gate, g_wide, d_on, d_other)
    d_in = swap(add_low((g_down[1], d_on), 0, 8), p_d)
    w_on = swap(g_wide[3], core)
    w_other = swap(g_wide[2], core)
    mixed, grad_hidden, grad_att, gain_two = feed_out(
        me, inner, grad_gate, grad_up, hidden, grad_mixed, gains, twos, wides, downs, orders, row_d
    )
    grad_att, d_in, w_on, w_other = tie(grad_att, d_in, w_on, w_other)
    w_in = swap(add_low((g_wide[1], w_on), 0, 8), z_d)
    d_parts = [g_down[0], d_other, d_in]
    d_next = swap(add_low(d_parts, 4, 8), p_c)
    back_a = back(0, 0, grad_att)
    grad_att, back_a, d_next = tie(grad_att, back_a, d_next)
    d_parts.append(d_next)
    d_next = swap(add_low(d_parts, 2, 4), p_b)
    back_b = back(0, 1, grad_att)
    normed_t, back_b, w_in, d_next = tie(normed_t, back_b, w_in, d_next)
    d_parts.append(d_next)
    d_next = swap(add_low(d_parts, 1, 2), p_a)
    w_parts = [g_wide[0], w_other, w_in]
    w_next = swap(add_low(w_parts, 4, 8), z_c)
    g_one = weight_grad(me, normed_t, (back_a, back_b), BY_Z, row_d, attended, grad_hidden)
    back_a, g_one, d_next = tie(back_a, g_one, d_next)
    d_parts.append(d_next)
    o_on = swap(g_one[3], core)
    o_other = swap(g_one[2], core)
    (through,) = input_gradient(me, (back_a, back_b), ones, BY_Z, row_d)
    grad_att, through, o_on, o_other, w_next = tie(grad_att, through, o_on, o_other, w_next)
    w_parts.append(w_next)
    o_in = swap(add_low((g_one[1], o_on), 0, 8), z_d)
    w_next = swap(add_low(w_parts, 2, 4), z_b)
    back_c = back(1, 0, grad_att)
    grad_att, back_c, o_in, normed_t = tie(grad_att, back_c, o_in, normed_t)
    by_core = normed_t.reshape(-1, 2, row_d, normed_t.shape[1])
    core_now = (me[0] >> 1) & 1
    rows_for = lambda which: lax.dynamic_index_in_dim(by_core, which, 1, keepdims=False).reshape(HD // 2, -1)
    other_t = swap(rows_for(1 - core_now), core)
    o_parts = [g_one[0], o_other, o_in]
    o_next = swap(add_low(o_parts, 4, 8), z_c)
    other_c = swap(back_c, core)
    back_d = back(1, 1, grad_att)
    back_d, w_next, o_next, other_c, other_t = tie(back_d, w_next, o_next, other_c, other_t)
    w_parts.append(w_next)
    o_parts.append(o_next)
    other_d = swap(back_d, core)
    o_next = swap(add_low(o_parts, 2, 4), z_b)
    w_next = swap(add_low(w_parts, 1, 2), z_a)
    own_t = rows_for(core_now)
    g_two = pair_grad(me, own_t, back_c, other_t, other_c, BY_Z, row_d, 0)
    g_two, other_d = tie(g_two, other_d)
    g_two = pair_grad(me, own_t, back_d, other_t, other_d, BY_Z, row_d, 1, g_two)
    g_two, o_next, tokens = tie(g_two, o_next, tokens)
    o_parts.append(o_next)
    t_in = swap(g_two[1], z_d)
    o_next = swap(add_low(o_parts, 1, 2), z_a)
    input_grad, gain_one = input_gradient(
        me, (back_c, back_d), twos, BY_Z, row_d, (through, tokens, grad_hidden), gains
    )
    gain_one, t_in, o_next, w_next = tie(gain_one, t_in, o_next, w_next)
    w_parts.append(w_next)
    o_parts.append(o_next)
    t_parts = [g_two[0], t_in]
    t_next = swap(add_low(t_parts, 4, 8), z_c)
    gain_sums = jnp.concatenate((gain_one, gain_two), axis=0)
    gain_sums = gain_sums + swap(gain_sums, core)
    gain_in = [swap(gain_sums, (kind, kind)) for kind in ("x", "y", "xy")]
    t_next, gain_in, d_parts, o_parts = tie(t_next, gain_in, d_parts, o_parts)
    share_down = total(*(part[0] for part in d_parts))
    t_parts.append(t_next)
    t_next = swap(add_low(t_parts, 2, 4), z_b)
    gain_sums = gain_sums + (gain_in[0] + gain_in[1] + gain_in[2])
    gain_in = swap(gain_sums, z_b)
    t_next, gain_in, w_parts = tie(t_next, gain_in, w_parts)
    share_ffin = total(*(part[0] for part in w_parts)).reshape(2, row_d, col_f)
    t_parts.append(t_next)
    t_next = swap(add_low(t_parts, 1, 2), z_a)
    gain_sums = gain_sums + gain_in
    gain_sums = gain_sums + swap(gain_sums, z_a)
    t_parts.append(t_next)
    share_one = total(*(part[0] for part in o_parts))
    share_two = total(*(part[0] for part in t_parts))
    share_qkv = jnp.stack((share_one[:, :PART], share_two)).reshape(2, row_d, 2, 3, 128)
    share_qkv = share_qkv.transpose(3, 1, 0, 2, 4).reshape(3, row_d, width)
    return mixed, input_grad, (share_qkv, share_one[:, PART:], share_ffin, share_down), gain_sums


def local_any(me, tokens, cotangent, valid, masks, attn_qkv, attn_out, ffn_in, ffn_out, low_gains):
    mask_q, mask_k = masks

    def whole(array, axis):
        wide = lax.all_gather(array.astype(BF), "narrow", axis=axis + 1, tiled=True)
        return lax.all_gather(wide, "dp", axis=axis, tiled=True)

    def own(grad, axis):
        rows = lax.psum_scatter(grad, "dp", scatter_dimension=axis, tiled=True)
        return lax.psum_scatter(rows, "narrow", scatter_dimension=axis + 1, tiled=True).astype(F32)

    halves = heads_first(whole(attn_qkv, 1))
    full_gains = lax.psum(low_gains, AXES)
    full_out = whole(attn_out, 0).reshape(2, 2, 256, HD).transpose(1, 0, 2, 3).reshape(HD, HD)
    full_ffin = whole(ffn_in, 1)
    ff = full_ffin.shape[2]
    ones = (joined(halves[0], gain_block(full_gains, HALF))[None],)
    twos = (jnp.concatenate((halves[1], full_out), axis=1)[None],)
    wides = (full_ffin[0][None], full_ffin[1][None])
    orders = (None,) * 5
    downs = (whole(ffn_out, 0)[None],)
    first, normed, normed_t, gains = first_project(me, tokens, ones, None, HD)
    second = second_project(me, normed, twos, None, HD)
    projected = (first, first, second, second)
    found = [attend_forward(projected[i], i % 2, mask_q, mask_k) for i in range(4)]
    attended = tuple(pair[0] for pair in found)
    active, sloped, inner, hidden, normed_two_t, grad_mixed, g_down = feed_in(
        me, tokens, attended, cotangent, valid, gains, twos, wides, orders, HD, ff, (1, ff, HD)
    )
    grad_gate, grad_up, g_wide = feed_grad(
        me, active, sloped, grad_mixed, normed_two_t, downs, orders, HD, (1, 2 * HD, ff)
    )
    mixed, grad_hidden, grad_att, gain_two = feed_out(
        me, inner, grad_gate, grad_up, hidden, grad_mixed, gains, twos, wides, downs, orders, HD
    )
    grads = [
        attend_backward(projected[i], attended[i], grad_att, found[i][1], mask_k, i // 2, i % 2, 0, 2)
        for i in range(4)
    ]
    g_one = weight_grad(me, normed_t, grads[:2], None, HD, attended, grad_hidden)[0][0]
    g_two = weight_grad(me, normed_t, grads[2:], None, HD)[0][0]
    (through,) = input_gradient(me, grads[:2], ones, None, HD)
    input_grad, gain_one = input_gradient(me, grads[2:], twos, None, HD, (through, tokens, grad_hidden), gains)
    gain_sums = lax.psum(jnp.concatenate((gain_one, gain_two), axis=0), AXES)
    grad_out = g_one[:, HALF:].reshape(2, 2, 256, HD).transpose(1, 0, 2, 3).reshape(HD, HD)
    shares = (
        own(heads_back(g_one[:, :HALF], g_two), 1),
        own(grad_out, 0),
        own(g_wide[0].reshape(2, HD, ff), 1),
        own(g_down[0][0], 0),
    )
    return mixed, input_grad, shares, gain_sums


def solution(mesh):
    rows = P(("dp", "narrow"), None)
    cube = P(None, "dp", "narrow")
    flat = P("dp", "narrow")
    gain = P(None, ("dp", "narrow"))
    weights = (cube, flat, cube, flat, gain)
    in_specs = (rows, rows, P(("dp", "narrow")), rows, *weights, *weights, *weights)
    out_specs = (rows, rows, *(spec for spec in weights for _ in range(4)))
    step = functools.partial(local, mesh.shape["dp"], mesh.shape["narrow"])
    return jax.shard_map(step, mesh=mesh, in_specs=in_specs, out_specs=out_specs, check_vma=False)
```

```python
import functools

import jax
import jax.numpy as jnp
from jax import lax
from jax.experimental import pallas as pl
from jax.experimental.pallas import tpu as pltpu
from jax.sharding import PartitionSpec as P

HEADS = 16
DK = 64
SHORT_PATCH = 256
STEP = 10
HD = 1024
SLOT = 384
LONG = 1152
LONG_PATCH = 1024

norm_eps = 1e-06
score_scale = 0.125
beta_one = 0.9
beta_two = 0.999
adam_eps = 1e-08
decay_rate = 0.01
rates = (0.08, 0.8, 0.08, 0.05, 0.6)

BF = jnp.bfloat16
F32 = jnp.float32
NN = (((1,), (0,)), ((), ()))
NT = (((1,), (1,)), ((), ()))
TN = (((0,), (0,)), ((), ()))
AXES = ("dp", "narrow")
VMEM_BYTES = 60 * 2**20
ROWS_GAIN = 16
GAIN_COLS = 512
PART = 6 * 128
HALF = 2 * PART
FF_BLOCK = 256
QUERY_BLOCK = 384
BACK_BLOCKS = (slice(0, 512), slice(512, 1024), slice(1024, LONG))
N_GROUPS = 4
DOWN_BLOCK = 768
GATHERED = 8
SCATTERED = 4


def dot(left, right, dims=NN):
    return lax.dot_general(left, right, dims, preferred_element_type=F32)


def params():
    return pltpu.CompilerParams(vmem_limit_bytes=VMEM_BYTES)


def shape(dims, dtype):
    return jax.ShapeDtypeStruct(dims, dtype)


IN_VMEM = pl.BlockSpec(memory_space=pltpu.VMEM)
IN_HBM = pl.BlockSpec(memory_space=pl.ANY)
IN_SMEM = pl.BlockSpec(memory_space=pltpu.SMEM)


BY_Z = (("z2", "z1"), ("z1", "z2"), ("x", "y"), ("y", "x"), ("core", "core"))
BY_PLANE = (("x", "y"), ("y", "x"), ("z2", "z1"), ("z1", "z2"), ("core", "core"))
BIT = {"y": 1, "core": 2, "x": 4, "xy": 5, "z1": 8, "z2": 16}


def partners(kinds):
    return [(me, me ^ BIT[kinds[(me >> 1) & 1]]) for me in range(32)]


def swap(array, kinds):
    return lax.ppermute(array, AXES, partners(kinds))


def owner_of(me, index, order):
    flips = [0, 0]
    for step in range(4):
        if (index >> step) & 1:
            for core in range(2):
                flips[core] ^= BIT[order[step][core]]
    own = me ^ 2 if index >> 4 else me
    device = own ^ jnp.where((own >> 1) & 1 == 1, flips[1], flips[0])
    return device >> 1, device & 1


def tie(*values):
    return lax.optimization_barrier(values)


def total(*parts):
    return sum(part.astype(F32) for part in parts)


def joined(held, arrived):
    return jnp.concatenate((held, arrived), axis=0)


def add_low(parts, low, high):
    return total(*(part[low:high] for part in parts)).astype(BF)


def each_place(me_ref, arrays, order, body):
    if order is None:
        body(arrays[0].at[0], 0, 0)
        return
    me = me_ref[0]
    slots = 32 // len(arrays)
    for index in range(32):
        dp, narrow = owner_of(me, index, order)
        body(arrays[index // slots].at[index % slots], dp, narrow)


def span(start, size, unit):
    if isinstance(start, int):
        return pl.ds(start * size, size)
    return pl.ds(pl.multiple_of(start * size, unit), size)


def head_rows(dp, fast):
    return (dp & 4) * 2 + (dp >> 3) * 4 + (dp & 3) if fast else 0


def load_half(me_ref, arrays, order, rows_piece, weight, sem):
    cols = PART if order else HALF

    def start(source, dp, narrow):
        pltpu.make_async_copy(
            source.at[pl.ds(0, rows_piece), pl.ds(0, cols)],
            weight.at[span(dp, rows_piece, 16), span(narrow, cols, 128)],
            sem,
        ).start()

    each_place(me_ref, arrays, order, start)


def first_project_kernel(order, rows_piece, me_ref, x_ref, *refs):
    n_arrays = GATHERED if order else 1
    arrays = refs[:n_arrays]
    out_ref, normed_ref, normed_t_ref, gains_ref, weight, gain_parts, sem, gain_sem = refs[n_arrays:]
    step = pl.program_id(0)

    @pl.when(step == 0)
    def _():
        slots = 32 // GATHERED if order else 1
        for index in range(n_arrays):
            pltpu.make_async_copy(
                arrays[index].at[:, pl.ds(rows_piece, ROWS_GAIN), pl.ds(0, GAIN_COLS)],
                gain_parts.at[pl.ds(index * slots, slots)],
                gain_sem,
            ).start()
        load_half(me_ref, arrays, order, rows_piece, weight, sem)
        x = x_ref[...].astype(F32)
        scaled = x * lax.rsqrt(jnp.mean(x * x, axis=-1, keepdims=True) + norm_eps)
        pltpu.make_async_copy(gain_parts, gain_parts, gain_sem).wait()
        parts = jnp.sum(gain_parts[...].astype(F32), axis=0)
        one = jnp.concatenate((parts[0:1], parts[1:2]), axis=1)
        gains_ref[...] = jnp.concatenate((one, jnp.concatenate((parts[2:3], parts[3:4]), axis=1)), axis=0)
        low = (scaled * one).astype(BF)
        normed_ref[...] = low
        normed_t_ref[...] = low.T
        pltpu.make_async_copy(weight, weight, sem).wait()

    column = pl.multiple_of(step * PART, PART)
    out_ref[...] = dot(normed_ref[...], weight[:, pl.ds(column, PART)]).astype(BF)


def first_project(me, tokens, arrays, order, rows_piece):
    rows = tokens.shape[0]
    full = lambda dims: pl.BlockSpec(dims, lambda step: (0,) * len(dims))
    return pl.pallas_call(
        functools.partial(first_project_kernel, order, rows_piece),
        grid=(2,),
        in_specs=[IN_SMEM, full((rows, HD))] + [IN_HBM] * len(arrays),
        out_specs=[
            pl.BlockSpec((rows, PART), lambda step: (0, step)),
            full((rows, HD)),
            full((HD, rows)),
            full((2, HD)),
        ],
        out_shape=[shape((rows, HALF), BF), shape((rows, HD), BF), shape((HD, rows), BF), shape((2, HD), F32)],
        scratch_shapes=[
            pltpu.VMEM((HD, HALF), BF),
            pltpu.VMEM((32 if order else 1, ROWS_GAIN, GAIN_COLS), BF),
            pltpu.SemaphoreType.DMA(()),
            pltpu.SemaphoreType.DMA(()),
        ],
        compiler_params=params(),
        name="first_project",
    )(me, tokens, *arrays)


def second_project_kernel(order, rows_piece, me_ref, normed_ref, *refs):
    n_arrays = GATHERED if order else 1
    arrays = refs[:n_arrays]
    out_ref, weight, sem = refs[n_arrays:]
    step = pl.program_id(0)

    @pl.when(step == 0)
    def _():
        load_half(me_ref, arrays, order, rows_piece, weight, sem)
        pltpu.make_async_copy(weight, weight, sem).wait()

    column = pl.multiple_of(step * PART, PART)
    out_ref[...] = dot(normed_ref[...], weight[:, pl.ds(column, PART)]).astype(BF)


def second_project(me, normed, arrays, order, rows_piece):
    rows = normed.shape[0]
    return pl.pallas_call(
        functools.partial(second_project_kernel, order, rows_piece),
        grid=(2,),
        in_specs=[IN_SMEM, pl.BlockSpec((rows, HD), lambda step: (0, 0))] + [IN_HBM] * len(arrays),
        out_specs=pl.BlockSpec((rows, PART), lambda step: (0, step)),
        out_shape=shape((rows, HALF), BF),
        scratch_shapes=[pltpu.VMEM((HD, HALF), BF), pltpu.SemaphoreType.DMA(())],
        compiler_params=params(),
        name="second_project",
    )(me, normed, *arrays)


def three_parts(values):
    first = values.astype(BF)
    rest = values - first.astype(F32)
    second = rest.astype(BF)
    return first, second, (rest - second.astype(F32)).astype(BF)


def mask_operands(segments):
    kind = jnp.arange(64, dtype=jnp.int32)
    mine = segments[None, :] + 1 == kind[:, None]
    query_side = jnp.where(mine, -1e30, 0.0).astype(BF)
    key_side = jnp.where((kind[None, :] < 4) & ~mine.T, 1.0, 0.0).astype(BF)
    return (
        jnp.concatenate((query_side, query_side), axis=0),
        jnp.concatenate((key_side, key_side), axis=1),
    )


def attend_forward_kernel(q_ref, k_ref, v_ref, mask_q_ref, mask_k_ref, out_ref, extra_ref):
    queries_t = (q_ref[...].astype(F32) * score_scale).astype(BF).T
    keys = k_ref[...]
    values_t = v_ref[...].T
    mask_q = mask_q_ref[...]
    mask_k = mask_k_ref[...]
    lane = lax.broadcasted_iota(jnp.int32, (1, 128), 1)
    row = lax.broadcasted_iota(jnp.int32, (64, 1), 0)
    ones = jnp.ones((16, LONG), BF)
    key_sides = (jnp.where(lane < 64, keys, mask_k), jnp.where(lane >= 64, keys, mask_k))
    query_sides = (
        jnp.concatenate((queries_t[0:64], mask_q[64:128]), axis=0),
        jnp.concatenate((mask_q[0:64], queries_t[64:128]), axis=0),
    )
    value_sides = [jnp.concatenate((values_t[64 * head : 64 * head + 64], ones), axis=0) for head in range(2)]
    out_blocks = ([], [])
    log_blocks = ([], [])

    def score(head, start):
        return dot(key_sides[head], query_sides[head][:, start : start + QUERY_BLOCK])

    def finish(head, top, expo):
        both = dot(value_sides[head], expo)
        sums = both[64:65]
        out_blocks[head].append((both[0:64] * (1.0 / sums)).astype(BF))
        log_blocks[head].append(-(top + jnp.log(sums)))

    jobs = [(head, start) for head in range(2) for start in range(0, LONG, QUERY_BLOCK)]
    scores = score(*jobs[0])
    waiting = None
    for index, job in enumerate(jobs):
        later = score(*jobs[index + 1]) if index + 1 < len(jobs) else None
        top = jnp.max(scores, axis=0, keepdims=True)
        expo = jnp.exp(scores - top).astype(BF)
        if waiting is not None:
            finish(*waiting)
        waiting = (job[0], top, expo)
        scores = later
    finish(*waiting)
    outs = [jnp.concatenate(blocks, axis=1) for blocks in out_blocks]
    extras = []
    for head in range(2):
        extra = mask_q[0:64].astype(F32)
        for index, part in enumerate(three_parts(jnp.concatenate(log_blocks[head], axis=1))):
            extra = jnp.where(row == 4 + index, part.astype(F32), extra)
        extras.append(extra.astype(BF))
    out_ref[...] = jnp.concatenate(outs, axis=0).T
    extra_ref[...] = jnp.concatenate((extras[1], extras[0]), axis=0).T


def tile_specs(rows, narrow, first):
    return [pl.BlockSpec((rows, 128), lambda i, c=c: (0, narrow * 6 + (first + i) * 3 + c)) for c in range(3)]


def attend_forward(projected, narrow, mask_q, mask_k):
    rows = projected.shape[0]
    tile = pl.BlockSpec((rows, 128), lambda i: (0, i))
    return pl.pallas_call(
        attend_forward_kernel,
        grid=(2,),
        in_specs=tile_specs(rows, narrow, 0)
        + [pl.BlockSpec((128, rows), lambda i: (0, 0)), pl.BlockSpec((rows, 128), lambda i: (0, 0))],
        out_specs=[tile, tile],
        out_shape=[shape((rows, 256), BF), shape((rows, 256), BF)],
        compiler_params=params(),
        name="attend_forward",
    )(projected, projected, projected, mask_q, mask_k)


def attend_backward_kernel(
    q_ref, k_ref, v_ref, out_ref, grad_ref, extra_ref, mask_k_ref, result_ref
):
    queries = (q_ref[...].astype(F32) * score_scale).astype(BF)
    queries_t = queries.T
    keys = k_ref[...]
    keys_t = keys.T
    values_t = v_ref[...].T
    grad = grad_ref[...]
    grad_t = grad.T
    extra = extra_ref[...]
    mask_k_t = mask_k_ref[...].T
    lane = lax.broadcasted_iota(jnp.int32, (1, 128), 1)
    row = lax.broadcasted_iota(jnp.int32, (64, 1), 0)
    product_t = (grad.astype(F32) * out_ref[...].astype(F32)).T
    inner = []
    for head in (1, 0):
        total = -jnp.sum(product_t[64 * head : 64 * head + 64], axis=0, keepdims=True)
        rows = jnp.zeros((64, LONG), F32)
        for index, part in enumerate(three_parts(total)):
            rows = jnp.where(row == index, part.astype(F32), rows)
        inner.append(rows.astype(BF))
    inner_cols = jnp.concatenate(inner, axis=0).T
    key_extra = jnp.where((row >= 4) & (row < 7), 1.0, mask_k_t[0:64].astype(F32)).astype(BF)
    value_extra = jnp.broadcast_to(jnp.where(row < 3, 1.0, 0.0).astype(BF), (64, LONG))
    query_sides = [jnp.where(lane < 64, queries, extra), jnp.where(lane >= 64, queries, extra)]
    grad_sides = [jnp.where(lane < 64, grad, inner_cols), jnp.where(lane >= 64, grad, inner_cols)]
    key_sides = [
        jnp.concatenate((keys_t[0:64], key_extra), axis=0),
        jnp.concatenate((key_extra, keys_t[64:128]), axis=0),
    ]
    value_sides = [
        jnp.concatenate((values_t[0:64], value_extra), axis=0),
        jnp.concatenate((value_extra, values_t[64:128]), axis=0),
    ]
    q_blocks = ([], [])
    grad_k = [None, None]
    grad_v = [None, None]

    def products(head, block):
        return dot(query_sides[head][block], key_sides[head]), dot(grad_sides[head][block], value_sides[head])

    def finish(head, block, probs, grad_scores):
        half = slice(64 * head, 64 * head + 64)
        v_part = dot(grad_t[half, block], probs)
        k_part = dot(queries_t[half, block], grad_scores)
        grad_v[head] = v_part if grad_v[head] is None else grad_v[head] + v_part
        grad_k[head] = k_part if grad_k[head] is None else grad_k[head] + k_part
        q_blocks[head].append(dot(grad_scores, keys) * score_scale)

    jobs = [(head, block) for head in range(2) for block in BACK_BLOCKS]
    scores, grad_probs = products(*jobs[0])
    waiting = None
    for index, job in enumerate(jobs):
        later = products(*jobs[index + 1]) if index + 1 < len(jobs) else (None, None)
        probs = jnp.exp(scores)
        low = (probs.astype(BF), (probs * grad_probs).astype(BF))
        if waiting is not None:
            finish(*waiting)
        waiting = (*job, *low)
        scores, grad_probs = later
    finish(*waiting)
    grad_q = [jnp.concatenate(blocks, axis=0) for blocks in q_blocks]
    result_ref[:, 0:128] = jnp.where(lane < 64, grad_q[0], grad_q[1]).astype(BF)
    result_ref[:, 128:256] = jnp.concatenate(grad_k, axis=0).astype(BF).T
    result_ref[:, 256:384] = jnp.concatenate(grad_v, axis=0).astype(BF).T


def attend_backward(projected, attended, grad_attended, extra, mask_k, half, narrow, first, count):
    rows = projected.shape[0]
    own = pl.BlockSpec((rows, 128), lambda i: (0, first + i))
    return pl.pallas_call(
        attend_backward_kernel,
        grid=(count,),
        in_specs=tile_specs(rows, narrow, first)
        + [
            own,
            pl.BlockSpec((rows, 128), lambda i: (0, half * 4 + narrow * 2 + first + i)),
            own,
            pl.BlockSpec((rows, 128), lambda i: (0, 0)),
        ],
        out_specs=pl.BlockSpec((rows, 384), lambda i: (0, i)),
        out_shape=shape((rows, 384 * count), BF),
        compiler_params=params(),
        name="attend_backward",
    )(projected, projected, projected, attended, grad_attended, extra, mask_k)


class fetch:
    def __init__(self, sources, targets, sems):
        self.targets = targets
        self.copies = [pltpu.make_async_copy(*triple) for triple in zip(sources, targets, sems)]
        for copy in self.copies:
            copy.start()

    def wait(self, index):
        self.copies[index].wait()

    def __call__(self, index):
        self.wait(index)
        return self.targets[index][...]


def fetched(arrays):
    return [pltpu.VMEM(array.shape, array.dtype) for array in arrays] + [pltpu.SemaphoreType.DMA((len(arrays),))]


def one_buffer(dims):
    return pl.BlockSpec(dims, lambda step: (0,) * len(dims), pipeline_mode=pl.Buffered(buffer_count=1))


def load_out(me_ref, arrays, order, rows_piece, w_out, sem):
    cols, at = (GAIN_COLS, PART) if order else (HD, HALF)

    def start(source, dp, narrow):
        pltpu.make_async_copy(
            source.at[pl.ds(0, rows_piece), pl.ds(at, cols)],
            w_out.at[span(head_rows(dp, order is not None), rows_piece, 16), span(narrow, cols, 128)],
            sem,
        ).start()

    each_place(me_ref, arrays, order, start)


def load_wide(me_ref, arrays, orders, targets, sems):
    count = len(arrays) // 2
    for index, target in enumerate(targets):
        order = orders and orders[index]
        cols = target.shape[1] // (2 if order else 1)

        def start(source, dp, narrow, index=index, target=target, cols=cols):
            rows = source.shape[0]
            pltpu.make_async_copy(
                source, target.at[span(dp, rows, 16), span(narrow, cols, 128)], sems[index]
            ).start()

        each_place(me_ref, arrays[index * count : (index + 1) * count], order, start)


def load_wide_by_half(me_ref, arrays, orders, targets, sems):
    whole = targets[0].shape[1]
    count = len(arrays) // 2
    for half in range(2):
        cols = pl.ds(half * (whole // 2), whole // 2)
        for index, target in enumerate(targets):
            if orders is None:
                pltpu.make_async_copy(arrays[index].at[0, :, cols], target.at[:, cols], sems.at[index, half]).start()
                continue

            def start(source, dp, narrow, half=half, index=index, target=target, cols=cols):
                copy = pltpu.make_async_copy(
                    source, target.at[span(dp, source.shape[0], 16), cols], sems.at[index, half]
                )
                pl.when(narrow == half)(copy.start)

            each_place(me_ref, arrays[index * count : (index + 1) * count], orders[index], start)


def wait_half(targets, sems, half):
    whole = targets[0].shape[1]
    for index, target in enumerate(targets):
        part = target.at[:, pl.ds(half * (whole // 2), whole // 2)]
        pltpu.make_async_copy(part, part, sems.at[index, half]).wait()


def load_down(me_ref, arrays, order, w_down, sem):
    rows, cols = arrays[0].shape[1:]

    def start(source, dp, narrow):
        pltpu.make_async_copy(source, w_down.at[span(dp, rows, 16), span(narrow, cols, 128)], sem).start()

    each_place(me_ref, arrays, order, start)


def load_down_by_group(me_ref, arrays, order, w_down, sems):
    rows, cols = arrays[0].shape[1:]
    if order is None:
        rows = rows // N_GROUPS
        for group in range(N_GROUPS):
            part = pl.ds(group * rows, rows)
            pltpu.make_async_copy(arrays[0].at[0, part], w_down.at[part], sems.at[group]).start()
        return

    def start(source, dp, narrow):
        pltpu.make_async_copy(
            source, w_down.at[span(dp, rows, 16), span(narrow, cols, 128)], sems.at[dp >> 2]
        ).start()

    each_place(me_ref, arrays, order, start)


def wait_group(w_down, sems, group):
    rows = w_down.shape[0] // N_GROUPS
    part = w_down.at[pl.ds(group * rows, rows)]
    pltpu.make_async_copy(part, part, sems.at[group]).wait()


def all_of(ref, sem):
    pltpu.make_async_copy(ref, ref, sem).wait()


def gelu_parts(gate):
    square = gate * gate
    curve = jnp.tanh(gate * (0.7978845608028654 + (0.7978845608028654 * 0.044715) * square))
    half = 0.5 + 0.5 * curve
    active = gate * half
    bend = (2.0 * 0.7978845608028654) + (6.0 * 0.7978845608028654 * 0.044715) * square
    return active, half + active * (1.0 - half) * bend


def feed_in_kernel(orders, rows_piece, me_ref, valid_ref, gains_ref, *refs):
    square_order, wide_orders, _, _, down_order = orders
    given, refs = refs[:6], refs[6:]
    n_arrays = GATHERED if down_order else 1
    square, wide = refs[:n_arrays], refs[n_arrays : 3 * n_arrays]
    refs = refs[3 * n_arrays :]
    active_out, sloped_out, inner_out, hidden_out, normed_t_out, grad_mixed_out = refs[:6]
    n_grads = SCATTERED if down_order else 1
    grad_down = refs[6 : 6 + n_grads]
    w_out, w_gate, w_up, w_down, hidden, normed, normed_t, inner = refs[6 + n_grads : 14 + n_grads]
    stages, sem, wide_sems, out_sems, stage_sems, down_sems, *own = refs[14 + n_grads :]
    att_a, att_b, att_c, att_d, x_ref, grad_mixed, in_sems = own
    ff = w_down.shape[0]
    load_out(me_ref, square, square_order, rows_piece, w_out, sem)
    get = fetch(given, own[:6], [in_sems.at[index] for index in range(6)])
    load_wide_by_half(me_ref, wide, wide_orders, (w_gate, w_up), wide_sems)
    gain = gains_ref[1:2]
    for index in range(6):
        get.wait(index)
    all_of(w_out, sem)

    def row_block(index):
        return pl.ds(pl.multiple_of(index * QUERY_BLOCK, QUERY_BLOCK), QUERY_BLOCK)

    def before(index, carry):
        part = row_block(index)
        left = jnp.concatenate([ref[part, :] for ref in (att_a, att_b, att_c, att_d)], axis=1)
        state = x_ref[part, :].astype(F32) + dot(left, w_out[...])
        hidden[part, :] = state
        low = (state * lax.rsqrt(jnp.mean(state * state, axis=-1, keepdims=True) + norm_eps) * gain).astype(BF)
        normed[part, :] = low
        normed_t[:, part] = low.T
        grad_mixed[part, :] = (grad_mixed[part, :].astype(F32) * valid_ref[part, :]).astype(BF)
        return carry

    blocks = x_ref.shape[0] // QUERY_BLOCK
    lax.fori_loop(0, blocks, before, 0)
    leaving = [
        pltpu.make_async_copy(hidden, hidden_out, out_sems.at[0]),
        pltpu.make_async_copy(normed_t, normed_t_out, out_sems.at[1]),
        pltpu.make_async_copy(grad_mixed, grad_mixed_out, out_sems.at[2]),
    ]
    for copy in leaving:
        copy.start()
    for half in range(2):
        wait_half((w_gate, w_up), wide_sems, half)
    width = ff // 2

    def stage_copy(index, half, which, target):
        return pltpu.make_async_copy(
            stages.at[half, which], target.at[row_block(index), pl.ds(half * width, width)], stage_sems.at[half, which]
        )

    def block(index, carry):
        part = row_block(index)
        left = normed[part, :]
        for half in range(2):
            cols = pl.ds(half * width, width)
            gate = dot(left, w_gate[:, cols])
            upward = dot(left, w_up[:, cols])
            active, slope = gelu_parts(gate)
            inner[part, cols] = (active * upward).astype(BF)

            @pl.when(index > 0)
            def _():
                stage_copy(index, half, 0, active_out).wait()
                stage_copy(index, half, 1, sloped_out).wait()

            stages[half, 0] = active.astype(BF)
            stages[half, 1] = (upward * slope).astype(BF)
            stage_copy(index, half, 0, active_out).start()
            stage_copy(index, half, 1, sloped_out).start()
        return carry

    lax.fori_loop(0, blocks, block, 0)
    leaving.append(pltpu.make_async_copy(inner, inner_out, out_sems.at[3]))
    leaving[-1].start()
    for group in range(N_GROUPS):
        begin, end = group * DOWN_BLOCK, min((group + 1) * DOWN_BLOCK, ff)
        w_down[begin:end, :] = dot(inner[:, begin:end].T, grad_mixed[...]).astype(BF)
        if down_order is None:
            part = pl.ds(group * (ff // N_GROUPS), ff // N_GROUPS)
            pltpu.make_async_copy(w_down.at[part], grad_down[0].at[0, part], down_sems.at[group]).start()
            continue

        def finish(target, dp, narrow, group=group):
            rows, cols = target.shape
            copy = pltpu.make_async_copy(
                w_down.at[span(dp, rows, 16), span(narrow, cols, 128)], target, down_sems.at[group]
            )
            pl.when(dp >> 2 == group)(copy.start)

        each_place(me_ref, grad_down, down_order, finish)
    for half in range(2):
        stage_copy(blocks - 1, half, 0, active_out).wait()
        stage_copy(blocks - 1, half, 1, sloped_out).wait()
    for copy in leaving:
        copy.wait()
    for group in range(N_GROUPS):
        wait_group(w_down, down_sems, group)


def feed_in(me, tokens, attended, cotangent, valid, gains, square, wide, orders, rows_piece, ff, down_shape):
    rows = tokens.shape[0]
    n_grads = SCATTERED if orders[4] else 1
    given = (*attended, tokens, cotangent)
    outs = pl.pallas_call(
        functools.partial(feed_in_kernel, orders, rows_piece),
        in_specs=[IN_SMEM, IN_VMEM, IN_VMEM] + [IN_HBM] * (len(given) + len(square) + len(wide)),
        out_specs=[IN_HBM] * (6 + n_grads),
        out_shape=[
            shape((rows, ff), BF),
            shape((rows, ff), BF),
            shape((rows, ff), BF),
            shape((rows, HD), F32),
            shape((HD, rows), BF),
            shape((rows, HD), BF),
        ]
        + [shape(down_shape, BF)] * n_grads,
        scratch_shapes=[
            pltpu.VMEM((HD, HD), BF),
            pltpu.VMEM((HD, ff), BF),
            pltpu.VMEM((HD, ff), BF),
            pltpu.VMEM((ff, HD), BF),
            pltpu.VMEM((rows, HD), F32),
            pltpu.VMEM((rows, HD), BF),
            pltpu.VMEM((HD, rows), BF),
            pltpu.VMEM((rows, ff), BF),
            pltpu.VMEM((2, 2, QUERY_BLOCK, ff // 2), BF),
            pltpu.SemaphoreType.DMA(()),
            pltpu.SemaphoreType.DMA((2, 2)),
            pltpu.SemaphoreType.DMA((4,)),
            pltpu.SemaphoreType.DMA((2, 2)),
            pltpu.SemaphoreType.DMA((N_GROUPS,)),
        ]
        + fetched(given),
        compiler_params=params(),
        name="feed_in",
    )(me, valid, gains, *given, *square, *wide)
    return (*outs[:6], outs[6:])


def feed_grad_kernel(orders, rows_piece, me_ref, active_ref, sloped_ref, *refs):
    _, _, down_order, wide_order, _ = orders
    given, refs = refs[:2], refs[2:]
    n_arrays = GATHERED if down_order else 1
    down = refs[:n_arrays]
    grad_gate_out, grad_up_out = refs[n_arrays : n_arrays + 2]
    n_grads = SCATTERED if wide_order else 1
    grad_wide = refs[n_arrays + 2 : n_arrays + 2 + n_grads]
    w_down, w_gate, w_up, up_side, gate_side, down_sems, side_sems, leave_sems, out_sems = refs[
        n_arrays + 2 + n_grads : -3
    ]
    grad_mixed, normed_t, in_sems = refs[-3:]
    rows, ff = active_ref.shape
    blocks = rows // QUERY_BLOCK
    parts = [pl.ds(index * QUERY_BLOCK, QUERY_BLOCK) for index in range(blocks)]
    first = pltpu.make_async_copy(given[0], grad_mixed, in_sems.at[0])
    first.start()
    load_down_by_group(me_ref, down, down_order, w_down, down_sems)
    sides = [
        [pltpu.make_async_copy(source.at[part], target.at[part], side_sems.at[which, index]) for index, part in enumerate(parts)]
        for which, (source, target) in enumerate(((active_ref, up_side), (sloped_ref, gate_side)))
    ]
    for index in range(blocks):
        for which in range(2):
            sides[which][index].start()
    last = pltpu.make_async_copy(given[1], normed_t, in_sems.at[1])
    last.start()
    first.wait()
    width = ff // 2
    leaving = []
    for index, part in enumerate(parts):
        left = grad_mixed[part, :]
        sides[0][index].wait()
        sides[1][index].wait()
        for half in range(2):
            if index == 0:
                for group in range(N_GROUPS // 2):
                    wait_group(w_down, down_sems, half * (N_GROUPS // 2) + group)
            cols = pl.ds(half * width, width)
            grad_inner = dot(left, w_down[cols, :], NT)
            gate_side[part, cols] = (grad_inner * gate_side[part, cols].astype(F32)).astype(BF)
            up_side[part, cols] = (grad_inner * up_side[part, cols].astype(F32)).astype(BF)
        for which, (source, target) in enumerate(((gate_side, grad_gate_out), (up_side, grad_up_out))):
            leaving.append(pltpu.make_async_copy(source.at[part], target.at[part], leave_sems.at[which, index]))
            leaving[-1].start()
    last.wait()
    left = normed_t[...]
    ready = (6 * FF_BLOCK, 9 * FF_BLOCK, ff)
    ends = (ff // 2, ff // 2 + 3 * FF_BLOCK + FF_BLOCK // 2, ff)
    piece = ff // 2 if wide_order else ff
    for place, (done, upto, begin, end) in enumerate(zip((0, *ready), ready, (0, *ends), ends)):
        w_gate[:, done:upto] = dot(left, gate_side[:, done:upto]).astype(BF)
        w_up[:, done:upto] = dot(left, up_side[:, done:upto]).astype(BF)

        def finish(target, dp, narrow, place=place, begin=begin, count=end - begin):
            def copies():
                for index, source in enumerate((w_gate, w_up)):
                    pltpu.make_async_copy(
                        source.at[span(dp, rows_piece, 16), pl.ds(begin, count)],
                        target.at[pl.ds(index * rows_piece, rows_piece), pl.ds(begin % piece, count)],
                        out_sems.at[index, place],
                    ).start()

            if wide_order is None:
                copies()
            else:
                pl.when(narrow == begin // piece)(copies)

        each_place(me_ref, grad_wide, wide_order, finish)
    for copy in leaving:
        copy.wait()
    for index, source in enumerate((w_gate, w_up)):
        for place, (begin, end) in enumerate(zip((0, *ends), ends)):
            part = source.at[:, pl.ds(begin, end - begin)]
            pltpu.make_async_copy(part, part, out_sems.at[index, place]).wait()


def feed_grad(me, active, sloped, grad_mixed, normed_t, down, orders, rows_piece, wide_shape):
    rows, ff = active.shape
    n_grads = SCATTERED if orders[3] else 1
    blocks = rows // QUERY_BLOCK
    outs = pl.pallas_call(
        functools.partial(feed_grad_kernel, orders, rows_piece),
        in_specs=[IN_SMEM] + [IN_HBM] * (4 + len(down)),
        out_specs=[IN_HBM] * (2 + n_grads),
        out_shape=[shape((rows, ff), BF)] * 2 + [shape(wide_shape, BF)] * n_grads,
        scratch_shapes=[
            pltpu.VMEM((ff, HD), BF),
            pltpu.VMEM((HD, ff), BF),
            pltpu.VMEM((HD, ff), BF),
            pltpu.VMEM((rows, ff), BF),
            pltpu.VMEM((rows, ff), BF),
            pltpu.SemaphoreType.DMA((N_GROUPS,)),
            pltpu.SemaphoreType.DMA((2, blocks)),
            pltpu.SemaphoreType.DMA((2, blocks)),
            pltpu.SemaphoreType.DMA((2, 3)),
        ]
        + fetched((grad_mixed, normed_t)),
        compiler_params=params(),
        name="feed_grad",
    )(me, active, sloped, grad_mixed, normed_t, *down)
    return outs[0], outs[1], outs[2:]


def feed_out_kernel(orders, rows_piece, me_ref, inner_ref, grad_gate_ref, grad_up_ref, hidden_ref, grad_mixed_ref, gains_ref, *refs):
    square_order, wide_orders, down_order, _, _ = orders
    n_arrays = GATHERED if down_order else 1
    square, wide, down = refs[:n_arrays], refs[n_arrays : 3 * n_arrays], refs[3 * n_arrays : 4 * n_arrays]
    mixed_ref, grad_hidden_ref, grad_attended_ref, gain_grad_ref = refs[4 * n_arrays : 4 * n_arrays + 4]
    w_out, w_gate, w_up, w_down, sems = refs[4 * n_arrays + 4 :]
    step = pl.program_id(0)

    @pl.when(step == 0)
    def _():
        load_down(me_ref, down, down_order, w_down, sems.at[3])
        load_wide(me_ref, wide, wide_orders, (w_gate, w_up), (sems.at[1], sems.at[2]))
        load_out(me_ref, square, square_order, rows_piece, w_out, sems.at[0])
        gain_grad_ref[...] = jnp.zeros_like(gain_grad_ref)
        all_of(w_down, sems.at[3])

    @pl.when(step < pl.num_programs(0) // 2)
    def _():
        mixed_ref[...] = (hidden_ref[...] + dot(inner_ref[...], w_down[...])).astype(BF)

    @pl.when(step == pl.num_programs(0) // 2)
    def _():
        all_of(w_gate, sems.at[1])
        all_of(w_up, sems.at[2])
        all_of(w_out, sems.at[0])

    @pl.when(step >= pl.num_programs(0) // 2)
    def _():
        state = hidden_ref[...]
        through = dot(grad_gate_ref[...], w_gate[...], NT) + dot(grad_up_ref[...], w_up[...], NT)
        scale = lax.rsqrt(jnp.mean(state * state, axis=-1, keepdims=True) + norm_eps)
        unit = state * scale
        gain_grad_ref[...] += jnp.sum(through * unit, axis=0, keepdims=True)
        through = through * gains_ref[1:2]
        result = grad_mixed_ref[...].astype(F32) + scale * (
            through - unit * jnp.mean(through * unit, axis=-1, keepdims=True)
        )
        grad_hidden_ref[...] = result
        grad_attended_ref[...] = dot(result.astype(BF), w_out[...], NT).astype(BF)


def feed_out(me, inner, grad_gate, grad_up, hidden, grad_mixed, gains, square, wide, down, orders, rows_piece):
    rows, ff = inner.shape
    n_arrays = len(down)
    count = rows // QUERY_BLOCK
    early = lambda cols: pl.BlockSpec((QUERY_BLOCK, cols), lambda step: (jnp.minimum(step, count - 1), 0))
    late = lambda cols: pl.BlockSpec((QUERY_BLOCK, cols), lambda step: (jnp.maximum(step - count, 0), 0))
    both = pl.BlockSpec((QUERY_BLOCK, HD), lambda step: (step % count, 0))
    return pl.pallas_call(
        functools.partial(feed_out_kernel, orders, rows_piece),
        grid=(2 * count,),
        in_specs=[IN_SMEM, early(ff), late(ff), late(ff), both, late(HD), one_buffer((2, HD))]
        + [IN_HBM] * (4 * n_arrays),
        out_specs=[early(HD), late(HD), late(HD), pl.BlockSpec((1, HD), lambda step: (0, 0))],
        out_shape=[shape((rows, HD), BF), shape((rows, HD), F32), shape((rows, HD), BF), shape((1, HD), F32)],
        scratch_shapes=[
            pltpu.VMEM((HD, HD), BF),
            pltpu.VMEM((HD, ff), BF),
            pltpu.VMEM((HD, ff), BF),
            pltpu.VMEM((ff, HD), BF),
            pltpu.SemaphoreType.DMA((4,)),
        ],
        compiler_params=params(),
        name="feed_out",
    )(me, inner, grad_gate, grad_up, hidden, grad_mixed, gains, *square, *wide, *down)


def half_of_grads(refs):
    wide = []
    held = []
    for ref in refs:
        held.append(ref)
        if sum(part.shape[1] for part in held) == PART:
            wide.append(held)
            held = []
    return wide


def weight_grad_kernel(order, rows_piece, n_grads, with_out, me_ref, *refs):
    n_arrays = 4 if order else 1
    fast = order is not None
    n_in = 1 + n_grads + (5 if with_out else 0)
    sources, targets, own = refs[:n_in], refs[n_in : n_in + n_arrays], refs[n_in + n_arrays :]
    held, in_sems = own[:n_in], own[n_in]
    weight, sems = own[n_in + 1 : n_in + 3]
    get = fetch(sources, held, [in_sems.at[index] for index in range(n_in)])
    cols = PART if fast else HALF
    left = get(0)
    begin = 1
    for index, group in enumerate(half_of_grads(sources[1 : 1 + n_grads])):
        right = [get(begin + place) for place in range(len(group))]
        begin += len(group)
        right = right[0] if len(right) == 1 else jnp.concatenate(right, axis=1)
        part = pl.ds(index * PART, PART)
        weight[:, part] = dot(left, right).astype(BF)

        def finish(target, dp, narrow, index=index, part=part):
            copy = pltpu.make_async_copy(
                weight.at[span(dp, rows_piece, 16), part],
                target.at[pl.ds(0, rows_piece), pl.ds(0 if fast else index * PART, PART)],
                sems.at[index],
            )
            if fast:
                pl.when(narrow == index)(copy.start)
            else:
                copy.start()

        each_place(me_ref, targets, order, finish)
    if with_out:
        w_out, out_sem = own[n_in + 3 :]
        col_d = GAIN_COLS if fast else HD
        attended = [get(1 + n_grads + index) for index in range(4)]
        branch = get(n_in - 1).astype(BF)
        for index in range(4):
            w_out[index * 256 : (index + 1) * 256, :] = dot(attended[index].T, branch).astype(BF)

        def finish_out(target, dp, narrow):
            pltpu.make_async_copy(
                w_out.at[span(head_rows(dp, fast), rows_piece, 16), span(narrow, col_d, 128)],
                target.at[pl.ds(0, rows_piece), pl.ds(cols, col_d)],
                out_sem,
            ).start()

        each_place(me_ref, targets, order, finish_out)
        all_of(w_out, out_sem)
    for index in range(2):
        part = weight.at[:, pl.ds(index * PART, PART)]
        pltpu.make_async_copy(part, part, sems.at[index]).wait()


def weight_grad(me, normed_t, grads, order, rows_piece, attended=(), grad_hidden=None):
    with_out = grad_hidden is not None
    cols = (PART if order else HALF) + ((GAIN_COLS if order else HD) if with_out else 0)
    outs = [shape((8 if order else 1, rows_piece, cols), BF)] * (4 if order else 1)
    more = [*attended, grad_hidden] if with_out else []
    given = [normed_t, *grads, *more]
    scratch = fetched(given) + [pltpu.VMEM((HD, HALF), BF), pltpu.SemaphoreType.DMA((2,))]
    if with_out:
        scratch += [pltpu.VMEM((HD, HD), BF), pltpu.SemaphoreType.DMA(())]
    return pl.pallas_call(
        functools.partial(weight_grad_kernel, order, rows_piece, len(grads), with_out),
        in_specs=[IN_SMEM] + [IN_HBM] * len(given),
        out_specs=[IN_HBM] * len(outs),
        out_shape=outs,
        scratch_shapes=scratch,
        compiler_params=params(),
        name="weight_grad",
    )(me, *given)


def pair_grad_kernel(order, rows_piece, narrow_now, n_into, me_ref, *refs):
    sources, refs = refs[:4], refs[4 + n_into :]
    targets, held, in_sems, weight, sem = refs[:2], refs[2:6], *refs[6:]
    get = fetch(sources, held, [in_sems.at[index] for index in range(4)])
    own = dot(get(0), get(1))
    weight[...] = (own + dot(get(2), get(3))).astype(BF)
    me = me_ref[0]
    for index in range(16):
        dp, narrow = owner_of(me, index, order)
        copy = pltpu.make_async_copy(
            weight.at[span(dp >> 1, rows_piece, 16)], targets[index // 8].at[index % 8], sem
        )
        pl.when(narrow == narrow_now)(copy.start)
    all_of(weight, sem)


def pair_grad(me, own_t, own_grad, other_t, other_grad, order, rows_piece, narrow_now, into=()):
    given = [own_t, own_grad, other_t, other_grad]
    outs = [shape((8, rows_piece, PART), BF)] * 2
    return pl.pallas_call(
        functools.partial(pair_grad_kernel, order, rows_piece, narrow_now, len(into)),
        in_specs=[IN_SMEM] + [IN_HBM] * (4 + len(into)),
        input_output_aliases={5 + index: index for index in range(len(into))},
        out_specs=[IN_HBM] * 2,
        out_shape=outs,
        scratch_shapes=fetched(given) + [pltpu.VMEM((HD // 2, PART), BF), pltpu.SemaphoreType.DMA(())],
        compiler_params=params(),
        name="pair_grad",
    )(me, *given, *into)


def input_grad_kernel(order, rows_piece, n_grads, last, me_ref, *refs):
    n_arrays = GATHERED if order else 1
    n_in = n_grads + (3 if last else 0)
    arrays, sources = refs[:n_arrays], refs[n_arrays : n_arrays + n_in]
    refs = refs[n_arrays + n_in :]
    if last:
        gains_ref, out_ref, gain_grad_ref = refs[:3]
        refs = refs[3:]
    else:
        out_ref = refs[0]
        refs = refs[1:]
    held, in_sems, weight, sem = refs[:n_in], refs[n_in], refs[n_in + 1], refs[n_in + 2]
    load_half(me_ref, arrays, order, rows_piece, weight, sem)
    get = fetch(sources, held, [in_sems.at[index] for index in range(n_in)])
    left = jnp.concatenate([get(index) for index in range(n_grads)], axis=1)
    all_of(weight, sem)
    if not last:
        out_ref[...] = dot(left, weight[...], NT).astype(BF)
        return
    found, out_sem = refs[n_in + 3 :]
    found[...] = dot(left, weight[...], NT)
    for index in range(3):
        get.wait(n_grads + index)
    through_ref, x_ref, grad_hidden_ref = held[n_grads:]
    gain_grad_ref[...] = jnp.zeros_like(gain_grad_ref)

    def rows(index, carry):
        part = pl.ds(pl.multiple_of(index * QUERY_BLOCK, QUERY_BLOCK), QUERY_BLOCK)
        through = through_ref[part, :].astype(F32) + found[part, :]
        x = x_ref[part, :].astype(F32)
        scale = lax.rsqrt(jnp.mean(x * x, axis=-1, keepdims=True) + norm_eps)
        unit = x * scale
        gain_grad_ref[...] += jnp.sum(through * unit, axis=0, keepdims=True)
        through = through * gains_ref[0:1]
        found[part, :] = grad_hidden_ref[part, :] + scale * (
            through - unit * jnp.mean(through * unit, axis=-1, keepdims=True)
        )
        pltpu.make_async_copy(found.at[part], out_ref.at[part], out_sem).start()
        return carry

    lax.fori_loop(0, found.shape[0] // QUERY_BLOCK, rows, 0)
    pltpu.make_async_copy(found, out_ref, out_sem).wait()


def input_gradient(me, grads, arrays, order, rows_piece, more=(), gains=None):
    rows = grads[0].shape[0]
    last = gains is not None
    given = [*grads, *more]
    outs = [shape((rows, HD), F32), shape((1, HD), F32)] if last else [shape((rows, HD), BF)]
    scratch = fetched(given) + [pltpu.VMEM((HD, HALF), BF), pltpu.SemaphoreType.DMA(())]
    if last:
        scratch += [pltpu.VMEM((rows, HD), F32), pltpu.SemaphoreType.DMA(())]
    return pl.pallas_call(
        functools.partial(input_grad_kernel, order, rows_piece, len(grads), last),
        in_specs=[IN_SMEM] + [IN_HBM] * (len(arrays) + len(given)) + ([IN_VMEM] if last else []),
        out_specs=[IN_HBM, IN_VMEM] if last else [IN_VMEM],
        out_shape=outs,
        scratch_shapes=scratch,
        compiler_params=params(),
        name="input_gradient",
    )(me, *arrays, *given, *([gains] if last else []))


def segment_ids(bucket_one, text_one):
    position = jnp.arange(LONG, dtype=jnp.int32)
    slot_index = position // SLOT
    inside = position - slot_index * SLOT
    slot_length = SHORT_PATCH + jnp.where(
        slot_index == 0, text_one[0], jnp.where(slot_index == 1, text_one[1], text_one[2])
    )
    long_valid = position < LONG_PATCH + text_one[0]
    short_valid = inside < slot_length
    return jnp.where(
        bucket_one == 1, jnp.where(long_valid, 0, -1), jnp.where(short_valid, slot_index, -1)
    ).astype(jnp.int32)


def adamw(weight, grad_total, first, second, rate):
    first_new = beta_one * first + (1.0 - beta_one) * grad_total
    second_new = beta_two * second + (1.0 - beta_two) * grad_total * grad_total
    first_hat = first_new / (1.0 - beta_one**STEP)
    second_hat = second_new / (1.0 - beta_two**STEP)
    weight_new = weight - rate * (first_hat / (jnp.sqrt(second_hat) + adam_eps) + decay_rate * weight)
    return (grad_total, first_new, second_new, weight_new)


def heads_first(array):
    rows = array.shape[1]
    return array.reshape(3, rows, 2, 2, 2, 128).transpose(3, 1, 2, 4, 0, 5).reshape(2, rows, HALF)


def heads_back(first, second):
    rows = first.shape[0]
    stacked = jnp.stack((first, second)).reshape(2, rows, 2, 2, 3, 128)
    return stacked.transpose(4, 1, 2, 0, 3, 5).reshape(3, rows, HD)


def gain_block(low_gains, cols):
    return jnp.pad(low_gains.reshape(4, GAIN_COLS), ((0, ROWS_GAIN - 4), (0, cols - GAIN_COLS)))


def local(n_dp, n_narrow, tokens, cotangent, bucket, text_lengths, *weights):
    attn_qkv, attn_out, ffn_in, ffn_out, norm_gains = weights[:5]
    masters, firsts, seconds = weights[:5], weights[5:10], weights[10:]
    run = local_fast if (n_dp, n_narrow) == (16, 2) else local_any
    linear = lax.axis_index("dp") * n_narrow + lax.axis_index("narrow")
    me = linear.astype(jnp.int32)[None]
    own = norm_gains.shape[1]
    low_gains = lax.dynamic_update_slice(jnp.zeros((2, HD), BF), norm_gains.astype(BF), (0, linear * own))
    segments = segment_ids(bucket[0], text_lengths[0])
    valid = (segments >= 0).astype(F32)[:, None]
    masks = mask_operands(segments)
    mixed, input_grad, shares, gain_sums = run(
        me, tokens, cotangent, valid, masks, attn_qkv, attn_out, ffn_in, ffn_out, low_gains
    )
    shares = (*shares, lax.dynamic_slice(gain_sums, (0, linear * own), (2, own)))
    results = [mixed, input_grad]
    for index in range(5):
        results.extend(adamw(masters[index], shares[index], firsts[index], seconds[index], rates[index]))
    return tuple(results)


def local_fast(me, tokens, cotangent, valid, masks, attn_qkv, attn_out, ffn_in, ffn_out, low_gains):
    mask_q, mask_k = masks
    row_d, width = attn_out.shape
    row_f, col_f = ffn_out.shape[0], ffn_in.shape[2]
    low_one = attn_qkv.reshape(3, row_d, 2, 2, 128)[:, :, 0].transpose(1, 2, 0, 3).reshape(row_d, PART)
    one = joined(low_one.astype(BF), gain_block(low_gains, PART))[None]
    z_a, z_b, z_c, z_d, core = BY_Z
    p_a, p_b, p_c, p_d, _ = BY_PLANE

    one_in, attn_qkv, attn_out, ffn_in, ffn_out = tie(swap(one, z_a), attn_qkv, attn_out, ffn_in, ffn_out)
    one = joined(one, one_in)
    low_two = attn_qkv.reshape(3, row_d, 2, 2, 128)[:, :, 1].transpose(1, 2, 0, 3).reshape(row_d, PART)
    two = jnp.concatenate((low_two, attn_out), axis=1).astype(BF)[None]
    gate = ffn_in[0].astype(BF)[None]
    up = ffn_in[1].astype(BF)[None]
    down = ffn_out.astype(BF)[None]
    one_in, two_in, gate, up = tie(swap(one, z_b), swap(two, z_a), gate, up)
    one, two = joined(one, one_in), joined(two, two_in)
    one_c, one_d, one_x, two_in, gate, up, valid = tie(
        swap(one, z_c), swap(one, z_d), swap(one, core), swap(two, z_b), gate, up, valid
    )
    two = joined(two, two_in)
    one_cd, one_cx, one_dx, up_in, gate_in, two, mask_q, mask_k = tie(
        swap(one_c, z_d), swap(one_c, core), swap(one_d, core), swap(up, z_a), swap(gate, p_a), two, mask_q, mask_k
    )
    one_cdx, two, up_in, gate_in, cotangent = tie(swap(one_cd, core), two, up_in, gate_in, cotangent)
    ones = (one, one_c, one_d, one_cd, one_x, one_cx, one_dx, one_cdx)
    up, gate = joined(up, up_in), joined(gate, gate_in)
    two_c = swap(two, z_c)
    up_in = swap(up, z_b)
    gate_in = swap(gate, p_b)
    two_x = swap(two, core)
    first, normed, normed_t, gains = first_project(me, tokens, ones, BY_Z, row_d)
    first, two, two_c, two_x, up_in, gate_in = tie(first, two, two_c, two_x, up_in, gate_in)
    up, gate = joined(up, up_in), joined(gate, gate_in)
    two_d = swap(two, z_d)
    two_cd = swap(two_c, z_d)
    gate_c = swap(gate, p_c)
    two_cx = swap(two_c, core)
    att_a, extra_a = attend_forward(first, 0, mask_q, mask_k)
    first, att_a, two_d, two_cx, up, down = tie(first, att_a, two_d, two_cx, up, down)
    gate_x = swap(gate, core)
    up_c = swap(up, z_c)
    two_dx = swap(two_d, core)
    down_in = swap(down, z_a)
    att_b, extra_b = attend_forward(first, 1, mask_q, mask_k)
    normed, att_b, two_cd, two_dx, up_c, gate_c, gate_x, down_in, up, gate = tie(
        normed, att_b, two_cd, two_dx, up_c, gate_c, gate_x, down_in, up, gate
    )
    down = joined(down, down_in)
    up_d = swap(up, z_d)
    gate_d = swap(gate, p_d)
    normed, two_cdx = tie(normed, swap(two_cd, core))
    twos = (two, two_c, two_d, two_cd, two_x, two_cx, two_dx, two_cdx)
    up_x = swap(up, core)
    gate_cx = swap(gate_c, core)
    down_in = swap(down, z_b)
    second = second_project(me, normed, twos, BY_Z, row_d)
    second, up_d, up_x, gate_cx, down_in, up_c, gate_c = tie(second, up_d, up_x, gate_cx, down_in, up_c, gate_c)
    down = joined(down, down_in)
    up_cd = swap(up_c, z_d)
    gate_cd = swap(gate_c, p_d)
    up_cx = swap(up_c, core)
    up_dx = swap(up_d, core)
    att_c, extra_c = attend_forward(second, 0, mask_q, mask_k)
    second, att_c, up_cd, up_cx, up_dx, gate_d, down = tie(second, att_c, up_cd, up_cx, up_dx, gate_d, down)
    up_cdx = swap(up_cd, core)
    gate_dx = swap(gate_d, core)
    down_c = swap(down, z_c)
    down_x = swap(down, core)
    att_d, extra_d = attend_forward(second, 1, mask_q, mask_k)
    att_d, up_cdx, gate_dx, gate_cd, down_c, down_x, down = tie(
        att_d, up_cdx, gate_dx, gate_cd, down_c, down_x, down
    )
    down_d = swap(down, z_d)
    gate_cdx, att_d = tie(swap(gate_cd, core), att_d)
    down_cd = swap(down_c, z_d)
    down_cx = swap(down_c, core)
    gates = (gate, gate_c, gate_d, gate_cd, gate_x, gate_cx, gate_dx, gate_cdx)
    ups = (up, up_c, up_d, up_cd, up_x, up_cx, up_dx, up_cdx)
    wides = (*gates, *ups)
    attended = (att_a, att_b, att_c, att_d)
    extras = (extra_a, extra_b, extra_c, extra_d)
    orders = (BY_Z, (BY_PLANE, BY_Z), BY_Z, BY_Z, BY_PLANE)
    active, sloped, inner, hidden, normed_two_t, grad_mixed, g_down = feed_in(
        me, tokens, attended, cotangent, valid, gains, twos, wides, orders, row_d, 2 * col_f, (8, row_f, width)
    )
    grad_mixed, g_down, down_d, down_cd, down_cx = tie(grad_mixed, g_down, down_d, down_cd, down_cx)
    down_dx = swap(down_d, core)
    down_cdx = swap(down_cd, core)
    d_on = swap(g_down[3], core)
    d_other = swap(g_down[2], core)
    grad_mixed, down_dx, down_cdx = tie(grad_mixed, down_dx, down_cdx)
    downs = (down, down_c, down_d, down_cd, down_x, down_cx, down_dx, down_cdx)

    def back(half, narrow, grad_now):
        place = half * 2 + narrow
        return attend_backward(
            (first, second)[half], attended[place], grad_now, extras[place], mask_k, half, narrow, 0, 2
        )

    grad_gate, grad_up, g_wide = feed_grad(
        me, active, sloped, grad_mixed, normed_two_t, downs, orders, row_d, (8, 2 * row_d, col_f)
    )
    grad_gate, g_wide, d_on, d_other = tie(grad_gate, g_wide, d_on, d_other)
    d_in = swap(add_low((g_down[1], d_on), 0, 8), p_d)
    w_on = swap(g_wide[3], core)
    w_other = swap(g_wide[2], core)
    mixed, grad_hidden, grad_att, gain_two = feed_out(
        me, inner, grad_gate, grad_up, hidden, grad_mixed, gains, twos, wides, downs, orders, row_d
    )
    grad_att, d_in, w_on, w_other = tie(grad_att, d_in, w_on, w_other)
    w_in = swap(add_low((g_wide[1], w_on), 0, 8), z_d)
    d_parts = [g_down[0], d_other, d_in]
    d_next = swap(add_low(d_parts, 4, 8), p_c)
    back_a = back(0, 0, grad_att)
    grad_att, back_a, d_next = tie(grad_att, back_a, d_next)
    d_parts.append(d_next)
    d_next = swap(add_low(d_parts, 2, 4), p_b)
    back_b = back(0, 1, grad_att)
    normed_t, back_b, w_in, d_next = tie(normed_t, back_b, w_in, d_next)
    d_parts.append(d_next)
    d_next = swap(add_low(d_parts, 1, 2), p_a)
    w_parts = [g_wide[0], w_other, w_in]
    w_next = swap(add_low(w_parts, 4, 8), z_c)
    g_one = weight_grad(me, normed_t, (back_a, back_b), BY_Z, row_d, attended, grad_hidden)
    back_a, g_one, d_next = tie(back_a, g_one, d_next)
    d_parts.append(d_next)
    o_on = swap(g_one[3], core)
    o_other = swap(g_one[2], core)
    (through,) = input_gradient(me, (back_a, back_b), ones, BY_Z, row_d)
    grad_att, through, o_on, o_other, w_next = tie(grad_att, through, o_on, o_other, w_next)
    w_parts.append(w_next)
    o_in = swap(add_low((g_one[1], o_on), 0, 8), z_d)
    w_next = swap(add_low(w_parts, 2, 4), z_b)
    back_c = back(1, 0, grad_att)
    grad_att, back_c, o_in, normed_t = tie(grad_att, back_c, o_in, normed_t)
    by_core = normed_t.reshape(-1, 2, row_d, normed_t.shape[1])
    core_now = (me[0] >> 1) & 1
    rows_for = lambda which: lax.dynamic_index_in_dim(by_core, which, 1, keepdims=False).reshape(HD // 2, -1)
    other_t = swap(rows_for(1 - core_now), core)
    o_parts = [g_one[0], o_other, o_in]
    o_next = swap(add_low(o_parts, 4, 8), z_c)
    other_c = swap(back_c, core)
    back_d = back(1, 1, grad_att)
    back_d, w_next, o_next, other_c, other_t = tie(back_d, w_next, o_next, other_c, other_t)
    w_parts.append(w_next)
    o_parts.append(o_next)
    other_d = swap(back_d, core)
    o_next = swap(add_low(o_parts, 2, 4), z_b)
    w_next = swap(add_low(w_parts, 1, 2), z_a)
    own_t = rows_for(core_now)
    g_two = pair_grad(me, own_t, back_c, other_t, other_c, BY_Z, row_d, 0)
    g_two, other_d = tie(g_two, other_d)
    g_two = pair_grad(me, own_t, back_d, other_t, other_d, BY_Z, row_d, 1, g_two)
    g_two, o_next, tokens = tie(g_two, o_next, tokens)
    o_parts.append(o_next)
    t_in = swap(g_two[1], z_d)
    o_next = swap(add_low(o_parts, 1, 2), z_a)
    input_grad, gain_one = input_gradient(
        me, (back_c, back_d), twos, BY_Z, row_d, (through, tokens, grad_hidden), gains
    )
    gain_one, t_in, o_next, w_next = tie(gain_one, t_in, o_next, w_next)
    w_parts.append(w_next)
    o_parts.append(o_next)
    t_parts = [g_two[0], t_in]
    t_next = swap(add_low(t_parts, 4, 8), z_c)
    gain_sums = jnp.concatenate((gain_one, gain_two), axis=0)
    gain_sums = gain_sums + swap(gain_sums, core)
    gain_in = [swap(gain_sums, (kind, kind)) for kind in ("x", "y", "xy")]
    t_next, gain_in, d_parts, o_parts = tie(t_next, gain_in, d_parts, o_parts)
    share_down = total(*(part[0] for part in d_parts))
    t_parts.append(t_next)
    t_next = swap(add_low(t_parts, 2, 4), z_b)
    gain_sums = gain_sums + (gain_in[0] + gain_in[1] + gain_in[2])
    gain_in = swap(gain_sums, z_b)
    t_next, gain_in, w_parts = tie(t_next, gain_in, w_parts)
    share_ffin = total(*(part[0] for part in w_parts)).reshape(2, row_d, col_f)
    t_parts.append(t_next)
    t_next = swap(add_low(t_parts, 1, 2), z_a)
    gain_sums = gain_sums + gain_in
    gain_sums = gain_sums + swap(gain_sums, z_a)
    t_parts.append(t_next)
    share_one = total(*(part[0] for part in o_parts))
    share_two = total(*(part[0] for part in t_parts))
    share_qkv = jnp.stack((share_one[:, :PART], share_two)).reshape(2, row_d, 2, 3, 128)
    share_qkv = share_qkv.transpose(3, 1, 0, 2, 4).reshape(3, row_d, width)
    return mixed, input_grad, (share_qkv, share_one[:, PART:], share_ffin, share_down), gain_sums


def local_any(me, tokens, cotangent, valid, masks, attn_qkv, attn_out, ffn_in, ffn_out, low_gains):
    mask_q, mask_k = masks

    def whole(array, axis):
        wide = lax.all_gather(array.astype(BF), "narrow", axis=axis + 1, tiled=True)
        return lax.all_gather(wide, "dp", axis=axis, tiled=True)

    def own(grad, axis):
        rows = lax.psum_scatter(grad, "dp", scatter_dimension=axis, tiled=True)
        return lax.psum_scatter(rows, "narrow", scatter_dimension=axis + 1, tiled=True).astype(F32)

    halves = heads_first(whole(attn_qkv, 1))
    full_gains = lax.psum(low_gains, AXES)
    full_out = whole(attn_out, 0).reshape(2, 2, 256, HD).transpose(1, 0, 2, 3).reshape(HD, HD)
    full_ffin = whole(ffn_in, 1)
    ff = full_ffin.shape[2]
    ones = (joined(halves[0], gain_block(full_gains, HALF))[None],)
    twos = (jnp.concatenate((halves[1], full_out), axis=1)[None],)
    wides = (full_ffin[0][None], full_ffin[1][None])
    orders = (None,) * 5
    downs = (whole(ffn_out, 0)[None],)
    first, normed, normed_t, gains = first_project(me, tokens, ones, None, HD)
    second = second_project(me, normed, twos, None, HD)
    projected = (first, first, second, second)
    found = [attend_forward(projected[i], i % 2, mask_q, mask_k) for i in range(4)]
    attended = tuple(pair[0] for pair in found)
    active, sloped, inner, hidden, normed_two_t, grad_mixed, g_down = feed_in(
        me, tokens, attended, cotangent, valid, gains, twos, wides, orders, HD, ff, (1, ff, HD)
    )
    grad_gate, grad_up, g_wide = feed_grad(
        me, active, sloped, grad_mixed, normed_two_t, downs, orders, HD, (1, 2 * HD, ff)
    )
    mixed, grad_hidden, grad_att, gain_two = feed_out(
        me, inner, grad_gate, grad_up, hidden, grad_mixed, gains, twos, wides, downs, orders, HD
    )
    grads = [
        attend_backward(projected[i], attended[i], grad_att, found[i][1], mask_k, i // 2, i % 2, 0, 2)
        for i in range(4)
    ]
    g_one = weight_grad(me, normed_t, grads[:2], None, HD, attended, grad_hidden)[0][0]
    g_two = weight_grad(me, normed_t, grads[2:], None, HD)[0][0]
    (through,) = input_gradient(me, grads[:2], ones, None, HD)
    input_grad, gain_one = input_gradient(me, grads[2:], twos, None, HD, (through, tokens, grad_hidden), gains)
    gain_sums = lax.psum(jnp.concatenate((gain_one, gain_two), axis=0), AXES)
    grad_out = g_one[:, HALF:].reshape(2, 2, 256, HD).transpose(1, 0, 2, 3).reshape(HD, HD)
    shares = (
        own(heads_back(g_one[:, :HALF], g_two), 1),
        own(grad_out, 0),
        own(g_wide[0].reshape(2, HD, ff), 1),
        own(g_down[0][0], 0),
    )
    return mixed, input_grad, shares, gain_sums


def solution(mesh):
    rows = P(("dp", "narrow"), None)
    cube = P(None, "dp", "narrow")
    flat = P("dp", "narrow")
    gain = P(None, ("dp", "narrow"))
    weights = (cube, flat, cube, flat, gain)
    in_specs = (rows, rows, P(("dp", "narrow")), rows, *weights, *weights, *weights)
    out_specs = (rows, rows, *(spec for spec in weights for _ in range(4)))
    step = functools.partial(local, mesh.shape["dp"], mesh.shape["narrow"])
    return jax.shard_map(step, mesh=mesh, in_specs=in_specs, out_specs=out_specs, check_vma=False)
```
